512 devices in a mesh: section: 8 (over y, core), dp: 64 (over z, x).
Axes of the slice: x: 4, y: 4, z: 16, core: 2. Of those that a mesh axis runs over, the one named last changes fastest.
Arguments:
- inputs: bfloat16 [16, 1024, 4096], P(None, 'dp'), may hold values from -6 to 6
- stashed: bfloat16 [8, 4096, 256], P('section', 'dp')
- master: float32 [8, 4096, 256], P('section', 'dp')
- first_moment: float32 [8, 4096, 256], P('section', 'dp'), may hold values from -0.0018 to 0.0018
- second_moment: float32 [8, 4096, 256], P('section', 'dp'), may hold values from 1e-08 to 1e-06
- counts: int32 [64, 16], P('dp'), may hold values from 1 to 16
- plan: int32 [16], replicated, may hold values from 0 to 15, each once
- layer_index: int32 [8], P('section'), may hold values from 0 to 47
Outputs:
- probe_out: bfloat16 [8, 1024, 4096], P('section', 'dp')
- new_master: float32 [8, 4096, 256], P('section', 'dp')
- new_first: float32 [8, 4096, 256], P('section', 'dp')
- new_second: float32 [8, 4096, 256], P('section', 'dp')
The draws below stay inside these ranges and needn't reach their ends.
All inputs are finite; a program needn't handle non-finite values.
Results may differ from the reference program's by a relative error of at most 0.0095.
Values may be sent and summed in bfloat16 or wider, within the bound.
A program may use at most 64 MiB of HBM per device.

```python
import math
import jax
import jax.numpy as jnp
from jax import lax

D = 4096
HID = 128
TOK_DEV = 16
MICRO = 16
DEPTH = 48
TOKENS = 1024
N_SECTION = 8
N_DP = 64


def fan_columns():
    column = jnp.arange(2 * HID)
    return jnp.where(column < HID, (3.0 / D) ** 0.5, (3.0 / HID) ** 0.5).astype(jnp.float32)


def draw_master(key, part):
    key = jax.random.fold_in(key, 11)
    array_shape = (N_SECTION, D, 2 * HID)
    values = jax.random.uniform(key, array_shape, jnp.float32, -1.0, 1.0)
    return values * fan_columns()


def draw_stashed(key, part):
    key = jax.random.fold_in(key, 12)
    array_shape = (N_SECTION, D, 2 * HID)
    values = jax.random.uniform(key, array_shape, jnp.float32, -1.0, 1.0)
    return (values * fan_columns()).astype(jnp.bfloat16)


def plant(array, key, smallest, largest):
    index_at = [jax.random.randint(jax.random.fold_in(key, axis), (), 0, length) for axis, length in enumerate(array.shape)]
    widest = array.shape.index(max(array.shape))
    neighbour = index_at[:widest] + [(index_at[widest] + 1) % array.shape[widest]] + index_at[widest + 1:]
    return array.at[tuple(index_at)].set(smallest).at[tuple(neighbour)].set(largest)


def levels(rng, extent, split, smallest, top_value):
    def one(position, shards_of):
        heights = jax.random.uniform(jax.random.fold_in(jax.random.fold_in(rng, 6), position), (shards_of,), jnp.float32, smallest / len(split), top_value / len(split))
        return jnp.repeat(jnp.exp(heights), extent[position] // shards_of).reshape((-1,) + (1,) * (len(extent) - position - 1))

    level = one(*split[0])
    for cut in split[1:]:
        level = level * one(*cut)
    return level


def noise(own_key, shape, scale, most, shards=(), held_as=jnp.bfloat16):
    factor_of = levels(own_key, shape, shards, -0.22, 0.18) if shards else 1.0
    values = jax.random.normal(own_key, shape, jnp.float32) * scale * factor_of
    return jnp.minimum(jnp.maximum(values, -most), most).astype(held_as)


def setup_inputs(seed: int = 0) -> dict:
    key_list = jax.random.split(jax.random.key(seed), 9)
    inputs = noise(key_list[0], (MICRO, TOKENS, D), 1.0, 6.0, ((1, 64),))
    stashed = draw_stashed(jax.random.fold_in(key_list[8], 71), 0)
    master = draw_master(jax.random.fold_in(key_list[8], 71), 0)
    first_moment = noise(key_list[3], (N_SECTION, D, 2 * HID), 0.0003, 0.0018, ((0, 8), (1, 64)), jnp.float32)
    second_moment = jnp.clip(jnp.exp(math.log(9.999999974752427e-07) - 4.6051702 * jax.random.uniform(key_list[4], (N_SECTION, D, 2 * HID), jnp.float32) ** levels(key_list[4], (N_SECTION, D, 2 * HID), ((0, 8), (1, 64)), -0.2, 0.2)), 9.99999993922529e-09, 9.999999974752427e-07)
    counts = plant(jax.random.randint(key_list[5], (N_DP, MICRO), 1, TOK_DEV + 1), jax.random.fold_in(key_list[5], 1), 1, TOK_DEV).astype(jnp.int32)
    plan = jax.random.permutation(key_list[6], MICRO).astype(jnp.int32)
    layer_index = plant(jax.random.randint(key_list[7], (N_SECTION,), 0, DEPTH), jax.random.fold_in(key_list[7], 1), 0, DEPTH - 1).astype(jnp.int32)
    return {"inputs": inputs, "stashed": stashed, "master": master, "first_moment": first_moment, "second_moment": second_moment, "counts": counts, "plan": plan, "layer_index": layer_index}


eps_norm = 1e-05
beta_one = 0.9
beta_two = 0.95
eps_adam = 1e-08
learn_rate = 0.002
decay_rate = 0.1

def branch_scale(layer_index):
    return lax.rsqrt(1.0 + layer_index.astype(jnp.float32) / 8.0)

def normalize(inputs):
    values = inputs.astype(jnp.float32)
    centred = values - lax.optimization_barrier(jnp.mean(values, axis=-1, keepdims=True))
    inv_spread = lax.rsqrt(lax.optimization_barrier(jnp.mean(centred * centred, axis=-1, keepdims=True)) + eps_norm)
    return (values, centred * inv_spread, inv_spread)

def contract_last(lhs_array, rhs_array):
    return lax.dot_general(lhs_array, rhs_array, (((1,), (1,)), ((), ())), preferred_element_type=jnp.float32)

def contract_first(lhs_array, rhs_array):
    return lax.dot_general(lhs_array, rhs_array, (((0,), (0,)), ((), ())), preferred_element_type=jnp.float32)

def layer_forward(inputs, weight, gain_value, hid_width):
    values, normed, _ = normalize(inputs)
    normed_b = normed.astype(jnp.bfloat16)
    pre_act = jnp.dot(normed_b, weight[:, :hid_width], preferred_element_type=jnp.float32)
    hidden_b = jax.nn.gelu(pre_act).astype(jnp.bfloat16)
    branch_out = contract_last(hidden_b, weight[:, hid_width:])
    return (values + gain_value * branch_out).astype(jnp.bfloat16)

def layer_backward(inputs, grad_out, weight, gain_value, hid_width):
    values, normed, inv_spread = normalize(inputs)
    normed_b = normed.astype(jnp.bfloat16)
    w_in = weight[:, :hid_width]
    w_out = weight[:, hid_width:]
    pre_act = jnp.dot(normed_b, w_in, preferred_element_type=jnp.float32)
    gelu_value, gelu_back = jax.vjp(jax.nn.gelu, pre_act)
    hidden_b = gelu_value.astype(jnp.bfloat16)
    grad_float = grad_out.astype(jnp.float32)
    out_b = (gain_value * grad_float).astype(jnp.bfloat16)
    hidden_grad = jnp.dot(out_b, w_out, preferred_element_type=jnp.float32)
    pre_b = gelu_back(hidden_grad)[0].astype(jnp.bfloat16)
    normed_grad = contract_last(pre_b, w_in)
    grad_mean = lax.optimization_barrier(jnp.mean(normed_grad, axis=-1, keepdims=True))
    cross_mean = lax.optimization_barrier(jnp.mean(normed_grad * normed, axis=-1, keepdims=True))
    grad_in = (grad_float + inv_spread * (normed_grad - grad_mean - normed * cross_mean)).astype(jnp.bfloat16)
    return (grad_in, normed_b, pre_b, out_b, hidden_b)

def reference(inputs, stashed, master, first_moment, second_moment, counts, plan, layer_index):
    section_gains = branch_scale(layer_index)
    repeated = jnp.repeat(jnp.transpose(counts), TOK_DEV, axis=1)
    row_pos = jnp.arange(TOKENS, dtype=jnp.int32) % TOK_DEV
    valid_all = row_pos[None, :] < repeated

    def forward_section(acts_now, section_data):
        weight, gain_value = section_data
        return (layer_forward(acts_now, weight, gain_value, HID), acts_now)

    def backward_section(grad_now, section_data):
        weight, gain_value, saved_in = section_data
        grad_in, normed_b, pre_b, out_b, hidden_b = layer_backward(saved_in, grad_now, weight, gain_value, HID)
        term_pair = jnp.concatenate([contract_first(normed_b, pre_b), contract_first(out_b, hidden_b)], axis=1)
        return (grad_in, term_pair)

    def one_micro(grad_total, micro_data):
        acts_in, valid_rows = micro_data
        top_out, section_inputs = lax.scan(forward_section, acts_in, (stashed, section_gains))
        start_grad = jnp.where(valid_rows[:, None], top_out, jnp.zeros_like(top_out))
        _, term_all = lax.scan(backward_section, start_grad, (stashed, section_gains, section_inputs), reverse=True)
        return (grad_total + term_all, None)
    grad_total, _ = lax.scan(one_micro, jnp.zeros(master.shape, jnp.float32), (inputs, valid_all))
    norm_sq = jnp.sum(grad_total * grad_total)
    clip_factor = 1.0 / jnp.maximum(jnp.sqrt(norm_sq), 1.0)
    clipped = grad_total * clip_factor
    new_first = beta_one * first_moment + (1.0 - beta_one) * clipped
    new_second = beta_two * second_moment + (1.0 - beta_two) * clipped * clipped
    new_master = master - learn_rate * (new_first / (jnp.sqrt(new_second) + eps_adam) + decay_rate * master)
    fresh_weight = new_master.astype(jnp.bfloat16)
    _, last_inputs = lax.scan(forward_section, inputs[plan[MICRO - 1]], (stashed, section_gains))

    def probe_section(section_data):
        weight, gain_value, saved_in = section_data
        return layer_forward(saved_in, weight, gain_value, HID)
    probe_out = lax.map(probe_section, (fresh_weight, section_gains, last_inputs))
    return (probe_out, new_master, new_first, new_second)
```

```python
import functools

import jax
import jax.numpy as jnp
from jax import lax
from jax.experimental import pallas as pl
from jax.experimental.pallas import tpu as pltpu
from jax.sharding import PartitionSpec as P

eps_norm = 1e-05
beta_one = 0.9
beta_two = 0.95
eps_adam = 1e-08
learn_rate = 0.002
decay_rate = 0.1

MESH = pl.DeviceIdType.MESH
WIDTH = 4096
HID = 128
ROWS = 256
TOK = 16
SECTIONS = 8
SHARD = 64
NZ = 16
NX = 4
NY = 4
f32 = jnp.float32
bf16 = jnp.bfloat16


class Place:

    def __init__(self):
        self.s = lax.axis_index("section")
        self.d = lax.axis_index("dp")
        self.c = lax.rem(self.s, 2)
        self.y = self.s // 2
        self.z = self.d // NX
        self.x = lax.rem(self.d, NX)

    def at_z(self, k):
        return (self.s, lax.rem(self.z + k + 2 * NZ, NZ) * NX + self.x)

    def at_x(self, k):
        return (self.s, self.z * NX + lax.rem(self.x + k + NX, NX))

    def at_y(self, k):
        return (lax.rem(self.y + k + NY, NY) * 2 + self.c, self.d)

    def sibling(self):
        return (self.y * 2 + 1 - self.c, self.d)


def greet(partners):
    barrier = pltpu.get_barrier_semaphore()
    for partner in partners:
        pl.semaphore_signal(barrier, inc=1, device_id=partner, device_id_type=MESH)
    pl.semaphore_wait(barrier, len(partners))


def remote(src, dst, send, recv, to):
    return pltpu.make_async_remote_copy(
        src_ref=src, dst_ref=dst, send_sem=send, recv_sem=recv, device_id=to, device_id_type=MESH
    )


def ring_gather(me, block, rz, zs, zr, xzs, xzr, xs, xr, fs, fr, done):
    rx = SHARD - rz

    def zblock(z):
        return block(z, None, 0, rz)

    def xblock(z, x):
        return block(z, x, rz, rx)

    def zcopy(flow, k, mode):
        z = lax.rem(me.z - (k - 1) + 2 * NZ, NZ) if flow == 0 else lax.rem(me.z + (k - 1), NZ)
        part = zblock(z) if mode == 0 else xblock(z, me.x)
        return remote(part, part, zs.at[flow, k, mode], zr.at[flow, k, mode], me.at_z(1 if flow == 0 else -1))

    def xcopy(flow, k, side):
        z = lax.rem(me.z - k + 2 * NZ, NZ) if flow == 0 else lax.rem(me.z + k, NZ)
        part = xblock(z, me.x)
        return remote(part, part, xs.at[flow, k, side], xr.at[flow, k, side], me.at_x(1 if side == 0 else -1))

    def fcopy(flow, k):
        z = lax.rem(me.z - k + 2 * NZ, NZ) if flow == 0 else lax.rem(me.z + k, NZ)
        came = -1 if flow == 0 else 1
        part = xblock(z, lax.rem(me.x + came + NX, NX))
        return remote(part, part, fs.at[flow, k], fr.at[flow, k], me.at_x(-came))

    def first(dx):
        part = block(me.z, me.x, 0, rz)
        return remote(part, part, xzs.at[dx], xzr.at[dx], me.at_x(dx))

    for flow in range(2):
        zcopy(flow, 1, 1).start()
    for dx in range(1, NX):
        first(dx).start()
    for side in range(2):
        xcopy(0, 0, side).start()
    for dx in range(1, NX):
        first(dx).wait_recv()
    for flow in range(2):
        zcopy(flow, 1, 0).start()

    def stage_a(flow, k):
        for mode in (1, 0):
            zcopy(flow, k, mode).wait_recv()

            @pl.when(k < (8 if flow == 0 else 7))
            def _():
                zcopy(flow, k + 1, mode).start()

            if mode == 1:
                for side in range(2):
                    xcopy(flow, k, side).start()

    def stage_b(flow, k):
        for side in range(2):
            xcopy(flow, k, side).wait_recv()
        fcopy(flow, k).start()

    def stage_c(flow, k):
        fcopy(flow, k).wait_recv()
        done(flow, k)

    def step(k, carry):
        stage_a(0, k)

        @pl.when(k < 8)
        def _():
            stage_a(1, k)

        stage_b(0, k - 1)

        @pl.when(k > 1)
        def _():
            stage_b(1, k - 1)
            stage_c(0, k - 2)

        @pl.when(k > 2)
        def _():
            stage_c(1, k - 2)

        return carry

    lax.fori_loop(1, 9, step, 0)
    stage_b(0, 8)
    stage_c(0, 7)
    stage_c(1, 7)
    stage_c(0, 8)

    def drain(k, carry):
        for flow in range(2):

            @pl.when((k >= 1) & (k <= (8 if flow == 0 else 7)))
            def _():
                for mode in range(2):
                    zcopy(flow, k, mode).wait_send()

            @pl.when((k <= (8 if flow == 0 else 7)) & (k >= flow))
            def _():
                for side in range(2):
                    xcopy(flow, k, side).wait_send()
                fcopy(flow, k).wait_send()

        return carry

    lax.fori_loop(0, 9, drain, 0)
    for dx in range(1, NX):
        first(dx).wait_send()


GATHER_SEMS = [
    pltpu.SemaphoreType.DMA((2, 9, 2)),
    pltpu.SemaphoreType.DMA((2, 9, 2)),
    pltpu.SemaphoreType.DMA((NX,)),
    pltpu.SemaphoreType.DMA((NX,)),
    pltpu.SemaphoreType.DMA((2, 9, 2)),
    pltpu.SemaphoreType.DMA((2, 9, 2)),
    pltpu.SemaphoreType.DMA((2, 9)),
    pltpu.SemaphoreType.DMA((2, 9)),
]


def gather_all_kernel(w_ref, gain_ref, all_ref, gains_ref, ys, yr, gs, gr, ss, sr, own, *ring_sems):
    me = Place()
    greet(
        [me.at_y(k) for k in range(1, NY)]
        + [me.at_x(k) for k in range(1, NX)]
        + [me.at_z(1), me.at_z(-1), me.sibling()]
    )

    def ycopy(k):
        return remote(w_ref, all_ref.at[me.c, me.y, me.z, me.x], ys.at[k], yr.at[k], me.at_y(k))

    def gcopy(k):
        part = gains_ref.at[me.c, me.y]
        return remote(gain_ref, part, gs.at[k], gr.at[k], me.at_y(k))

    for k in range(1, NY):
        ycopy(k).start()
        gcopy(k).start()
    keep = pltpu.make_async_copy(w_ref, all_ref.at[me.c, me.y, me.z, me.x], own.at[0])
    keep_gain = pltpu.make_async_copy(gain_ref, gains_ref.at[me.c, me.y], own.at[1])
    keep.start()
    keep_gain.start()
    for k in range(1, NY):
        ycopy(k).wait_recv()
        gcopy(k).wait_recv()
    keep.wait()
    keep_gain.wait()
    gains = remote(gains_ref.at[me.c], gains_ref.at[me.c], ss.at[2, 0], sr.at[2, 0], me.sibling())
    gains.start()

    def block(z, x, lo, n):
        if x is None:
            return all_ref.at[me.c, :, z, :, pl.ds(lo, n), :]
        return all_ref.at[me.c, :, z, x, pl.ds(lo, n), :]

    def side_copy(flow, k):
        z = lax.rem(me.z - k + 2 * NZ, NZ) if flow == 0 else lax.rem(me.z + k, NZ)
        part = all_ref.at[me.c, :, z]
        return remote(part, part, ss.at[flow, k], sr.at[flow, k], me.sibling())

    ring_gather(me, block, 32, *ring_sems, lambda flow, k: side_copy(flow, k).start())

    def finish(k, carry):
        for flow in range(2):

            @pl.when((k >= flow) & (k <= (8 if flow == 0 else 7)))
            def _():
                side_copy(flow, k).wait()

        return carry

    lax.fori_loop(0, 9, finish, 0)
    gains.wait()
    for k in range(1, NY):
        ycopy(k).wait_send()
        gcopy(k).wait_send()


def gather_all(shard, gain_tile):
    return pl.pallas_call(
        gather_all_kernel,
        out_shape=(
            jax.ShapeDtypeStruct((2, NY, NZ, NX, SHARD, 2 * HID), bf16),
            jax.ShapeDtypeStruct((2, NY, 8, 128), f32),
        ),
        in_specs=[pl.BlockSpec(memory_space=pltpu.VMEM)] * 2,
        out_specs=(pl.BlockSpec(memory_space=pl.ANY), pl.BlockSpec(memory_space=pltpu.VMEM)),
        scratch_shapes=[
            pltpu.SemaphoreType.DMA((NY,)),
            pltpu.SemaphoreType.DMA((NY,)),
            pltpu.SemaphoreType.DMA((NY,)),
            pltpu.SemaphoreType.DMA((NY,)),
            pltpu.SemaphoreType.DMA((3, 9)),
            pltpu.SemaphoreType.DMA((3, 9)),
            pltpu.SemaphoreType.DMA((2,)),
            *GATHER_SEMS,
        ],
        compiler_params=pltpu.CompilerParams(collective_id=0, has_side_effects=True),
        name="gather_all",
    )(shard, gain_tile)


def normalize(values):
    centred = values - jnp.mean(values, axis=-1, keepdims=True)
    inv_spread = lax.rsqrt(jnp.mean(centred * centred, axis=-1, keepdims=True) + eps_norm)
    return (centred * inv_spread, inv_spread)


def contract_last(lhs_array, rhs_array):
    return lax.dot_general(
        lhs_array, rhs_array, (((1,), (1,)), ((), ())), preferred_element_type=f32
    )


def contract_first(lhs_array, rhs_array):
    return lax.dot_general(
        lhs_array, rhs_array, (((0,), (0,)), ((), ())), preferred_element_type=f32
    )


root_two_over_pi = 0.7978845608028654
cubic = 0.044715


def gelu_parts(v):
    t = jnp.tanh(root_two_over_pi * (v + cubic * (v * v * v)))
    cdf = 0.5 * (1.0 + t)
    slope = cdf + 0.5 * v * (1.0 - t * t) * (root_two_over_pi * (1.0 + 3.0 * cubic * v * v))
    return v * cdf, slope


CHUNK = 256


def relay_kernel(
    which_ref, x_hbm, all_hbm, gains_ref, valid_ref, grad_ref, probe_ref,
    w, x, g, nb, inv, pre, hid, out_b, wsum, w_sem, x_sem,
):
    mine = lax.axis_index("section")

    def load(s):
        return pltpu.make_async_copy(all_hbm.at[lax.rem(s, 2), s // 2], w.at[s], w_sem.at[s])

    get_x = pltpu.make_async_copy(x_hbm, x, x_sem)
    get_x.start()
    for s in range(SECTIONS):
        load(s).start()
    get_x.wait()

    def gain_of(s):
        return gains_ref[lax.rem(s, 2), s // 2, 0:1, 0:1]

    def forward(s, carry):
        @pl.when(s == mine)
        def _():
            start = pl.multiple_of(which_ref[0] * TOK, TOK)
            probe_ref[...] = x[pl.ds(start, TOK), :]

        def norm_rows(i, carry):
            rows = pl.ds(pl.multiple_of(i * 16, 16), 16)
            normed, spread = normalize(x[rows, :].astype(f32))
            nb[s, rows, :] = normed.astype(bf16)
            inv[s, rows, :] = jnp.broadcast_to(spread, (16, 128))
            return carry

        lax.fori_loop(0, ROWS // 16, norm_rows, 0)
        load(s).wait()
        pre_act = jnp.dot(nb[s], w[s, :, :HID], preferred_element_type=f32)
        pre[s] = pre_act
        hidden = gelu_parts(pre_act)[0].astype(bf16)
        hid[s] = hidden
        gain = gain_of(s)

        def columns(j, total):
            cols = pl.ds(pl.multiple_of(j * CHUNK, CHUNK), CHUNK)
            branch = contract_last(hidden, w[s, cols, HID:])
            x[:, cols] = (x[:, cols].astype(f32) + gain * branch).astype(bf16)
            return total + jnp.sum(w[s, cols, :HID].astype(f32), axis=0, keepdims=True)

        wsum[s] = lax.fori_loop(0, WIDTH // CHUNK, columns, jnp.zeros((1, HID), f32))
        return carry

    lax.fori_loop(0, SECTIONS, forward, 0)
    keep = valid_ref[:, 0:1] > 0.5

    def mask(j, carry):
        cols = pl.ds(pl.multiple_of(j * CHUNK, CHUNK), CHUNK)
        g[:, cols] = jnp.where(keep, x[:, cols].astype(f32), 0.0).astype(bf16)
        return carry

    lax.fori_loop(0, WIDTH // CHUNK, mask, 0)

    def inner_grads(s):
        gain = gain_of(s)

        def columns(j, total):
            cols = pl.ds(pl.multiple_of(j * CHUNK, CHUNK), CHUNK)
            out = (gain * g[:, cols].astype(f32)).astype(bf16)
            out_b[:, cols] = out
            return total + jnp.dot(out, w[s, cols, HID:], preferred_element_type=f32)

        hidden_grad = lax.fori_loop(0, WIDTH // CHUNK, columns, jnp.zeros((ROWS, HID), f32))
        return (gelu_parts(pre[s])[1] * hidden_grad).astype(bf16)

    def backward(i, carry):
        s = SECTIONS - 1 - i
        pre_b = inner_grads(s)
        pre_f = pre_b.astype(f32)
        grad_mean = jnp.sum(pre_f * wsum[s], axis=-1, keepdims=True) * (1.0 / WIDTH)
        cross_mean = jnp.sum(pre_f * pre[s], axis=-1, keepdims=True) * (1.0 / WIDTH)
        spread = inv[s, :, 0:1]

        def columns(j, carry):
            cols = pl.ds(pl.multiple_of(j * CHUNK, CHUNK), CHUNK)
            normed_grad = contract_last(pre_b, w[s, cols, :HID])
            normed = nb[s, :, cols].astype(f32)
            g[:, cols] = (
                g[:, cols].astype(f32) + spread * (normed_grad - grad_mean - normed * cross_mean)
            ).astype(bf16)
            return carry

        lax.fori_loop(0, WIDTH // CHUNK, columns, 0)
        return carry

    lax.fori_loop(0, SECTIONS - 1 - mine, backward, 0)
    pre_b = inner_grads(mine)
    hidden = hid[mine]

    def columns(j, carry):
        cols = pl.ds(pl.multiple_of(j * CHUNK, CHUNK), CHUNK)
        grad_ref[cols, :HID] = contract_first(pre_b, nb[mine, :, cols]).T.astype(bf16)
        grad_ref[cols, HID:] = contract_first(hidden, out_b[:, cols]).T.astype(bf16)
        return carry

    lax.fori_loop(0, WIDTH // CHUNK, columns, 0)


def relay(which, rows, all_weights, gains, valid):
    return pl.pallas_call(
        relay_kernel,
        out_shape=(
            jax.ShapeDtypeStruct((WIDTH, 2 * HID), bf16),
            jax.ShapeDtypeStruct((TOK, WIDTH), bf16),
        ),
        in_specs=[
            pl.BlockSpec(memory_space=pltpu.SMEM),
            pl.BlockSpec(memory_space=pl.ANY),
            pl.BlockSpec(memory_space=pl.ANY),
            pl.BlockSpec(memory_space=pltpu.VMEM),
            pl.BlockSpec(memory_space=pltpu.VMEM),
        ],
        out_specs=(
            pl.BlockSpec(memory_space=pltpu.VMEM),
            pl.BlockSpec(memory_space=pltpu.VMEM),
        ),
        scratch_shapes=[
            pltpu.VMEM((SECTIONS, WIDTH, 2 * HID), bf16),
            pltpu.VMEM((ROWS, WIDTH), bf16),
            pltpu.VMEM((ROWS, WIDTH), bf16),
            pltpu.VMEM((SECTIONS, ROWS, WIDTH), bf16),
            pltpu.VMEM((SECTIONS, ROWS, 128), f32),
            pltpu.VMEM((SECTIONS, ROWS, HID), f32),
            pltpu.VMEM((SECTIONS, ROWS, HID), bf16),
            pltpu.VMEM((ROWS, WIDTH), bf16),
            pltpu.VMEM((SECTIONS, 1, HID), f32),
            pltpu.SemaphoreType.DMA((SECTIONS,)),
            pltpu.SemaphoreType.DMA,
        ],
        compiler_params=pltpu.CompilerParams(vmem_limit_bytes=58 * 2**20),
        name="relay",
    )(which, rows, all_weights, gains, valid)


HALF = SHARD // 2
GROUP = SECTIONS * NX


def finish_kernel(
    grad_ref, master_ref, first_ref, second_ref, gain_ref, probe_ref,
    out_ref, new_master_ref, new_first_ref, new_second_ref,
    fresh, ra, rb, xa, xa_out, xb, tb, share, near, far,
    zs, zr, xs, xr, ns, nr, ms, mr, *ring_sems,
):
    me = Place()

    def group_at(i):
        ds, dx = i // NX, lax.rem(i, NX)
        return (lax.rem(me.s + ds, SECTIONS), me.z * NX + lax.rem(me.x + dx, NX))

    greet([group_at(i) for i in range(1, GROUP)] + [me.at_z(k) for k in range(1, NZ)])

    def target_z(flow, k):
        if flow == 0:
            return lax.rem(me.z + 9 - k, NZ)
        return lax.rem(me.z - 8 + k + NZ, NZ)

    def zcopy(flow, k, mode, first=False):
        to = me.at_z(1 if flow == 0 else -1)
        send, recv = zs.at[flow, k, mode], zr.at[flow, k, mode]
        if mode == 0:
            src = grad_ref.at[target_z(flow, k), :, pl.ds(0, HALF), :] if first else ra.at[flow, k - 1]
            return remote(src, ra.at[flow, k], send, recv, to)
        src = tb.at[target_z(flow, k)] if first else rb.at[flow, k - 1]
        return remote(src, rb.at[flow, k], send, recv, to)

    def xbcopy(dx):
        src = grad_ref.at[:, lax.rem(me.x + dx, NX), pl.ds(HALF, HALF), :]
        return remote(src, xb.at[dx], xs.at[1, dx], xr.at[1, dx], me.at_x(dx))

    def xacopy(dx):
        src = xa_out.at[lax.rem(me.x + dx, NX)]
        return remote(src, xa.at[dx], xs.at[0, dx], xr.at[0, dx], me.at_x(dx))

    for flow in range(2):
        zcopy(flow, 1, 0, True).start()
    for dx in range(1, NX):
        xbcopy(dx).start()

    def step_a(flow, k):
        zcopy(flow, k, 0).wait_recv()

        @pl.when(k < (8 if flow == 0 else 7))
        def _():
            own = grad_ref[target_z(flow, k + 1), :, pl.ds(0, HALF), :].astype(f32)
            ra[flow, k] = (ra[flow, k].astype(f32) + own).astype(bf16)
            zcopy(flow, k + 1, 0).start()

    def step_b(flow, k):
        zcopy(flow, k, 1).wait_recv()

        @pl.when(k < (8 if flow == 0 else 7))
        def _():
            rb[flow, k] = (rb[flow, k].astype(f32) + tb[target_z(flow, k + 1)].astype(f32)).astype(bf16)
            zcopy(flow, k + 1, 1).start()

    def begin_b():
        for dx in range(1, NX):
            xbcopy(dx).wait_recv()

        def add(z, carry):
            total = grad_ref[z, me.x, pl.ds(HALF, HALF), :].astype(f32)
            for dx in range(1, NX):
                total = total + xb[dx, z].astype(f32)
            tb[z] = total.astype(bf16)
            return carry

        lax.fori_loop(0, NZ, add, 0)
        for flow in range(2):
            zcopy(flow, 1, 1, True).start()

    def ring(k, carry):
        @pl.when(k <= 8)
        def _():
            step_a(0, k)

        @pl.when(k <= 7)
        def _():
            step_a(1, k)

        @pl.when(k == 3)
        def _():
            begin_b()

        @pl.when(k == 8)
        def _():
            def total(x, carry):
                block = (
                    grad_ref[me.z, x, pl.ds(0, HALF), :].astype(f32)
                    + ra[0, 8, x].astype(f32)
                    + ra[1, 7, x].astype(f32)
                )
                xa_out[x] = block.astype(bf16)
                return carry

            lax.fori_loop(0, NX, total, 0)
            for dx in range(1, NX):
                xacopy(dx).start()

        @pl.when(k > 3)
        def _():
            step_b(0, k - 3)

        @pl.when((k > 3) & (k < 11))
        def _():
            step_b(1, k - 3)

        return carry

    lax.fori_loop(1, 12, ring, 0)
    share[pl.ds(HALF, HALF), :] = tb[me.z].astype(f32) + rb[0, 8].astype(f32) + rb[1, 7].astype(f32)
    for dx in range(1, NX):
        xacopy(dx).wait_recv()
    total = xa_out[me.x].astype(f32)
    for dx in range(1, NX):
        total = total + xa[dx].astype(f32)
    share[pl.ds(0, HALF), :] = total

    squares = jnp.zeros((8, 128), f32)
    for i in range(SHARD // 8):
        for j in range(2):
            tile = share[pl.ds(i * 8, 8), pl.ds(j * 128, 128)]
            squares = squares + tile * tile
    near[0] = squares

    def ncopy(i):
        return remote(near.at[0], near.at[i], ns.at[i], nr.at[i], group_at(i))

    def mcopy(k):
        return remote(far.at[0], far.at[k], ms.at[k], mr.at[k], me.at_z(k))

    def n_start(i, carry):
        ncopy(i).start()
        return carry

    def n_wait(i, carry):
        ncopy(i).wait()
        return carry

    def m_start(i, carry):
        mcopy(i).start()
        return carry

    def m_wait(i, carry):
        mcopy(i).wait()
        return carry

    lax.fori_loop(1, GROUP, n_start, 0)
    lax.fori_loop(1, GROUP, n_wait, 0)
    far[0] = jnp.sum(near[...], axis=0)
    lax.fori_loop(1, NZ, m_start, 0)
    lax.fori_loop(1, NZ, m_wait, 0)
    norm_sq = jnp.sum(jnp.sum(far[...], axis=0), keepdims=True)
    clip_factor = 1.0 / jnp.maximum(jnp.sqrt(norm_sq), 1.0)
    clipped = share[...] * clip_factor
    master_now = master_ref[...]
    new_first = beta_one * first_ref[...] + (1.0 - beta_one) * clipped
    new_second = beta_two * second_ref[...] + (1.0 - beta_two) * clipped * clipped
    new_master = master_now - learn_rate * (
        new_first / (jnp.sqrt(new_second) + eps_adam) + decay_rate * master_now
    )
    fresh[me.z, me.x] = new_master.astype(bf16)
    new_master_ref[...] = new_master
    new_first_ref[...] = new_first
    new_second_ref[...] = new_second

    def block(z, x, lo, n):
        if x is None:
            return fresh.at[z, :, pl.ds(lo, n), :]
        return fresh.at[z, x, pl.ds(lo, n), :]

    ring_gather(me, block, HALF, *ring_sems, lambda flow, k: None)

    def drain(k, carry):
        for flow in range(2):

            @pl.when(k <= (8 if flow == 0 else 7))
            def _():
                for mode in range(2):
                    zcopy(flow, k, mode).wait_send()

        return carry

    lax.fori_loop(2, 9, drain, 0)
    for flow in range(2):
        for mode in range(2):
            zcopy(flow, 1, mode, True).wait_send()
    for dx in range(1, NX):
        xbcopy(dx).wait_send()
        xacopy(dx).wait_send()

    values = probe_ref[...].astype(f32)
    normed = normalize(values)[0].astype(bf16)
    pre_act = jnp.zeros((TOK, HID), f32)
    for z in range(NZ):
        part = fresh[z, :, :, :HID].reshape(256, HID)
        pre_act = pre_act + jnp.dot(normed[:, z * 256 : (z + 1) * 256], part, preferred_element_type=f32)
    hidden = gelu_parts(pre_act)[0].astype(bf16)
    gain = gain_ref[0:1, 0:1]
    for z in range(NZ):
        part = fresh[z, :, :, HID:].reshape(256, HID)
        cols = slice(z * 256, (z + 1) * 256)
        out_ref[:, cols] = (values[:, cols] + gain * contract_last(hidden, part)).astype(bf16)


def finish(grad, master, first_moment, second_moment, gain_tile, probe_in):
    state = jax.ShapeDtypeStruct((SHARD, 2 * HID), f32)
    vmem = pl.BlockSpec(memory_space=pltpu.VMEM)
    return pl.pallas_call(
        finish_kernel,
        out_shape=(jax.ShapeDtypeStruct((TOK, WIDTH), bf16), state, state, state),
        in_specs=[vmem] * 6,
        out_specs=(vmem,) * 4,
        scratch_shapes=[
            pltpu.VMEM((NZ, NX, SHARD, 2 * HID), bf16),
            pltpu.VMEM((2, 9, NX, HALF, 2 * HID), bf16),
            pltpu.VMEM((2, 9, HALF, 2 * HID), bf16),
            pltpu.VMEM((NX, HALF, 2 * HID), bf16),
            pltpu.VMEM((NX, HALF, 2 * HID), bf16),
            pltpu.VMEM((NX, NZ, HALF, 2 * HID), bf16),
            pltpu.VMEM((NZ, HALF, 2 * HID), bf16),
            pltpu.VMEM((SHARD, 2 * HID), f32),
            pltpu.VMEM((GROUP, 8, 128), f32),
            pltpu.VMEM((NZ, 8, 128), f32),
            pltpu.SemaphoreType.DMA((2, 9, 2)),
            pltpu.SemaphoreType.DMA((2, 9, 2)),
            pltpu.SemaphoreType.DMA((2, NX)),
            pltpu.SemaphoreType.DMA((2, NX)),
            pltpu.SemaphoreType.DMA((GROUP,)),
            pltpu.SemaphoreType.DMA((GROUP,)),
            pltpu.SemaphoreType.DMA((NZ,)),
            pltpu.SemaphoreType.DMA((NZ,)),
            *GATHER_SEMS,
        ],
        compiler_params=pltpu.CompilerParams(
            collective_id=1, has_side_effects=True, vmem_limit_bytes=40 * 2**20
        ),
        name="finish",
    )(grad, master, first_moment, second_moment, gain_tile, probe_in)


def shards(inputs, stashed, master, first_moment, second_moment, counts, plan, layer_index):
    gain_tile = jnp.full((8, 128), lax.rsqrt(1.0 + layer_index.astype(f32) / 8.0)[0], f32)
    all_weights, gains = gather_all(stashed[0], gain_tile)
    row_pos = lax.broadcasted_iota(jnp.int32, (16, TOK), 1)
    valid = (row_pos < counts[0][:, None]).astype(f32).reshape(ROWS, 1)
    grad, probe_in = relay(
        plan[15:],
        inputs.reshape(ROWS, WIDTH),
        all_weights.reshape(2, NY, WIDTH, 2 * HID),
        gains,
        jnp.broadcast_to(valid, (ROWS, 128)),
    )
    probe_out, new_master, new_first, new_second = finish(
        grad.reshape(NZ, NX, SHARD, 2 * HID), master[0], first_moment[0], second_moment[0], gain_tile, probe_in
    )
    return (probe_out[None], new_master[None], new_first[None], new_second[None])


def solution(mesh):
    in_specs = (
        P(None, "dp", None),
        P("section", "dp", None),
        P("section", "dp", None),
        P("section", "dp", None),
        P("section", "dp", None),
        P("dp", None),
        P(),
        P("section"),
    )
    out_specs = (
        P("section", "dp", None),
        P("section", "dp", None),
        P("section", "dp", None),
        P("section", "dp", None),
    )
    return jax.shard_map(shards, mesh=mesh, in_specs=in_specs, out_specs=out_specs, check_vma=False)
```

```python
import functools

import jax
import jax.numpy as jnp
from jax import lax
from jax.experimental import pallas as pl
from jax.experimental.pallas import tpu as pltpu
from jax.sharding import PartitionSpec as P

eps_norm = 1e-05
beta_one = 0.9
beta_two = 0.95
eps_adam = 1e-08
learn_rate = 0.002
decay_rate = 0.1

MESH = pl.DeviceIdType.MESH
WIDTH = 4096
HID = 128
ROWS = 256
TOK = 16
SECTIONS = 8
SHARD = 64
NZ = 16
NX = 4
NY = 4
f32 = jnp.float32
bf16 = jnp.bfloat16


class Place:

    def __init__(self):
        self.s = lax.axis_index("section")
        self.d = lax.axis_index("dp")
        self.c = lax.rem(self.s, 2)
        self.y = self.s // 2
        self.z = self.d // NX
        self.x = lax.rem(self.d, NX)

    def at_z(self, k):
        return (self.s, lax.rem(self.z + k + 2 * NZ, NZ) * NX + self.x)

    def at_x(self, k):
        return (self.s, self.z * NX + lax.rem(self.x + k + NX, NX))

    def at_y(self, k):
        return (lax.rem(self.y + k + NY, NY) * 2 + self.c, self.d)

    def sibling(self):
        return (self.y * 2 + 1 - self.c, self.d)


def greet(partners):
    barrier = pltpu.get_barrier_semaphore()
    for partner in partners:
        pl.semaphore_signal(barrier, inc=1, device_id=partner, device_id_type=MESH)
    pl.semaphore_wait(barrier, len(partners))


def remote(src, dst, send, recv, to):
    return pltpu.make_async_remote_copy(
        src_ref=src, dst_ref=dst, send_sem=send, recv_sem=recv, device_id=to, device_id_type=MESH
    )


def ring_gather(me, block, rz, zs, zr, xzs, xzr, xs, xr, fs, fr, done):
    rx = SHARD - rz

    def zblock(z):
        return block(z, None, 0, rz)

    def xblock(z, x):
        return block(z, x, rz, rx)

    def zcopy(flow, k, mode):
        z = lax.rem(me.z - (k - 1) + 2 * NZ, NZ) if flow == 0 else lax.rem(me.z + (k - 1), NZ)
        part = zblock(z) if mode == 0 else xblock(z, me.x)
        return remote(part, part, zs.at[flow, k, mode], zr.at[flow, k, mode], me.at_z(1 if flow == 0 else -1))

    def xcopy(flow, k, side):
        z = lax.rem(me.z - k + 2 * NZ, NZ) if flow == 0 else lax.rem(me.z + k, NZ)
        part = xblock(z, me.x)
        return remote(part, part, xs.at[flow, k, side], xr.at[flow, k, side], me.at_x(1 if side == 0 else -1))

    def fcopy(flow, k):
        z = lax.rem(me.z - k + 2 * NZ, NZ) if flow == 0 else lax.rem(me.z + k, NZ)
        came = -1 if flow == 0 else 1
        part = xblock(z, lax.rem(me.x + came + NX, NX))
        return remote(part, part, fs.at[flow, k], fr.at[flow, k], me.at_x(-came))

    def first(dx):
        part = block(me.z, me.x, 0, rz)
        return remote(part, part, xzs.at[dx], xzr.at[dx], me.at_x(dx))

    for flow in range(2):
        zcopy(flow, 1, 1).start()
    for dx in range(1, NX):
        first(dx).start()
    for side in range(2):
        xcopy(0, 0, side).start()
    for dx in range(1, NX):
        first(dx).wait_recv()
    for flow in range(2):
        zcopy(flow, 1, 0).start()

    def stage_a(flow, k):
        for mode in (1, 0):
            zcopy(flow, k, mode).wait_recv()

            @pl.when(k < (8 if flow == 0 else 7))
            def _():
                zcopy(flow, k + 1, mode).start()

            if mode == 1:
                for side in range(2):
                    xcopy(flow, k, side).start()

    def stage_b(flow, k):
        for side in range(2):
            xcopy(flow, k, side).wait_recv()
        fcopy(flow, k).start()

    def stage_c(flow, k):
        fcopy(flow, k).wait_recv()
        done(flow, k)

    def step(k, carry):
        stage_a(0, k)

        @pl.when(k < 8)
        def _():
            stage_a(1, k)

        stage_b(0, k - 1)

        @pl.when(k > 1)
        def _():
            stage_b(1, k - 1)
            stage_c(0, k - 2)

        @pl.when(k > 2)
        def _():
            stage_c(1, k - 2)

        return carry

    lax.fori_loop(1, 9, step, 0)
    stage_b(0, 8)
    stage_c(0, 7)
    stage_c(1, 7)
    stage_c(0, 8)

    def drain(k, carry):
        for flow in range(2):

            @pl.when((k >= 1) & (k <= (8 if flow == 0 else 7)))
            def _():
                for mode in range(2):
                    zcopy(flow, k, mode).wait_send()

            @pl.when((k <= (8 if flow == 0 else 7)) & (k >= flow))
            def _():
                for side in range(2):
                    xcopy(flow, k, side).wait_send()
                fcopy(flow, k).wait_send()

        return carry

    lax.fori_loop(0, 9, drain, 0)
    for dx in range(1, NX):
        first(dx).wait_send()


GATHER_SEMS = [
    pltpu.SemaphoreType.DMA((2, 9, 2)),
    pltpu.SemaphoreType.DMA((2, 9, 2)),
    pltpu.SemaphoreType.DMA((NX,)),
    pltpu.SemaphoreType.DMA((NX,)),
    pltpu.SemaphoreType.DMA((2, 9, 2)),
    pltpu.SemaphoreType.DMA((2, 9, 2)),
    pltpu.SemaphoreType.DMA((2, 9)),
    pltpu.SemaphoreType.DMA((2, 9)),
]


def gather_all_kernel(w_ref, gain_ref, all_ref, gains_ref, ys, yr, gs, gr, ss, sr, own, *ring_sems):
    me = Place()
    greet(
        [me.at_y(k) for k in range(1, NY)]
        + [me.at_x(k) for k in range(1, NX)]
        + [me.at_z(1), me.at_z(-1), me.sibling()]
    )

    def ycopy(k):
        return remote(w_ref, all_ref.at[me.c, me.y, me.z, me.x], ys.at[k], yr.at[k], me.at_y(k))

    def gcopy(k):
        part = gains_ref.at[me.c, me.y]
        return remote(gain_ref, part, gs.at[k], gr.at[k], me.at_y(k))

    for k in range(1, NY):
        ycopy(k).start()
        gcopy(k).start()
    keep = pltpu.make_async_copy(w_ref, all_ref.at[me.c, me.y, me.z, me.x], own.at[0])
    keep_gain = pltpu.make_async_copy(gain_ref, gains_ref.at[me.c, me.y], own.at[1])
    keep.start()
    keep_gain.start()
    for k in range(1, NY):
        ycopy(k).wait_recv()
        gcopy(k).wait_recv()
    keep.wait()
    keep_gain.wait()
    gains = remote(gains_ref.at[me.c], gains_ref.at[me.c], ss.at[2, 0], sr.at[2, 0], me.sibling())
    gains.start()

    def block(z, x, lo, n):
        if x is None:
            return all_ref.at[me.c, :, z, :, pl.ds(lo, n), :]
        return all_ref.at[me.c, :, z, x, pl.ds(lo, n), :]

    def side_copy(flow, k):
        z = lax.rem(me.z - k + 2 * NZ, NZ) if flow == 0 else lax.rem(me.z + k, NZ)
        part = all_ref.at[me.c, :, z]
        return remote(part, part, ss.at[flow, k], sr.at[flow, k], me.sibling())

    ring_gather(me, block, 32, *ring_sems, lambda flow, k: side_copy(flow, k).start())

    def finish(k, carry):
        for flow in range(2):

            @pl.when((k >= flow) & (k <= (8 if flow == 0 else 7)))
            def _():
                side_copy(flow, k).wait()

        return carry

    lax.fori_loop(0, 9, finish, 0)
    gains.wait()
    for k in range(1, NY):
        ycopy(k).wait_send()
        gcopy(k).wait_send()


def gather_all(shard, gain_tile):
    return pl.pallas_call(
        gather_all_kernel,
        out_shape=(
            jax.ShapeDtypeStruct((2, NY, NZ, NX, SHARD, 2 * HID), bf16),
            jax.ShapeDtypeStruct((2, NY, 8, 128), f32),
        ),
        in_specs=[pl.BlockSpec(memory_space=pltpu.VMEM)] * 2,
        out_specs=(pl.BlockSpec(memory_space=pl.ANY), pl.BlockSpec(memory_space=pltpu.VMEM)),
        scratch_shapes=[
            pltpu.SemaphoreType.DMA((NY,)),
            pltpu.SemaphoreType.DMA((NY,)),
            pltpu.SemaphoreType.DMA((NY,)),
            pltpu.SemaphoreType.DMA((NY,)),
            pltpu.SemaphoreType.DMA((3, 9)),
            pltpu.SemaphoreType.DMA((3, 9)),
            pltpu.SemaphoreType.DMA((2,)),
            *GATHER_SEMS,
        ],
        compiler_params=pltpu.CompilerParams(collective_id=0, has_side_effects=True),
        name="gather_all",
    )(shard, gain_tile)


def normalize(values):
    centred = values - jnp.mean(values, axis=-1, keepdims=True)
    inv_spread = lax.rsqrt(jnp.mean(centred * centred, axis=-1, keepdims=True) + eps_norm)
    return (centred * inv_spread, inv_spread)


def contract_last(lhs_array, rhs_array):
    return lax.dot_general(
        lhs_array, rhs_array, (((1,), (1,)), ((), ())), preferred_element_type=f32
    )


def contract_first(lhs_array, rhs_array):
    return lax.dot_general(
        lhs_array, rhs_array, (((0,), (0,)), ((), ())), preferred_element_type=f32
    )


root_two_over_pi = 0.7978845608028654
cubic = 0.044715


def gelu_parts(v):
    t = jnp.tanh(root_two_over_pi * (v + cubic * (v * v * v)))
    cdf = 0.5 * (1.0 + t)
    slope = cdf + 0.5 * v * (1.0 - t * t) * (root_two_over_pi * (1.0 + 3.0 * cubic * v * v))
    return v * cdf, slope


OWN = ROWS // 2
CHUNK = 512
CHUNKS = WIDTH // CHUNK
PIECES = 4
PIECE = WIDTH // PIECES


def tiled(a):
    return jnp.concatenate([a] * (CHUNK // 128), axis=1)


def folded(a):
    total = a[:, 0:128]
    for i in range(1, a.shape[1] // 128):
        total = total + a[:, i * 128 : (i + 1) * 128]
    return total


def row_mean(a):
    return jnp.broadcast_to(jnp.sum(a, axis=-1, keepdims=True) * (1.0 / WIDTH), (OWN, 128))


def relay_kernel(
    x_hbm, all_hbm, gains_ref, valid_ref, grad_ref, probe_ref,
    w, x, g, cb, inv, pre, hid, wsum, out, pg, cb_in, hid_in, out_in, pg_in, pr, pr_in,
    w_sem, x_sem, fs, fr, bs, br,
):
    me = Place()
    mine = me.s
    sib = me.y * 2 + 1 - me.c
    greet([me.sibling()])

    def load(s):
        return pltpu.make_async_copy(all_hbm.at[lax.rem(s, 2), s // 2], w.at[s], w_sem.at[s])

    get_x = pltpu.make_async_copy(
        x_hbm.at[pl.ds(pl.multiple_of(me.c * OWN, OWN), OWN)], x, x_sem
    )
    get_x.start()
    for s in range(SECTIONS):
        load(s).start()
    get_x.wait()

    def send_cb():
        return remote(cb.at[sib], cb_in, fs.at[0], fr.at[0], me.sibling())

    def send_hid():
        return remote(hid.at[sib], hid_in, fs.at[1], fr.at[1], me.sibling())

    def send_pr():
        return remote(pr, pr_in, fs.at[2], fr.at[2], me.sibling())

    def send_out(p):
        cols = pl.ds(p * PIECE, PIECE)
        return remote(out.at[1 - me.c, :, cols], out_in.at[:, cols], bs.at[p], br.at[p], me.sibling())

    def send_pg():
        return remote(pg.at[1 - me.c], pg_in, bs.at[PIECES], br.at[PIECES], me.sibling())

    def gain_of(s):
        return gains_ref[lax.rem(s, 2), s // 2, 0:1, :]

    def cols_of(j):
        return slice(j * CHUNK, (j + 1) * CHUNK)

    def picked(ref):
        for j in range(CHUNKS):
            cols = cols_of(j)
            rows = jnp.zeros((TOK, CHUNK), f32)
            for i in range(OWN // TOK):
                part = pl.ds(i * TOK, TOK)
                chosen = valid_ref[1, pl.ds(pl.multiple_of(me.c * OWN + i * TOK, TOK), TOK), :]
                rows = rows + tiled(chosen) * x[part, cols].astype(f32)
            ref[:, cols] = rows.astype(bf16)

    total = jnp.zeros((OWN, 128), f32)
    for j in range(CHUNKS):
        total = total + folded(x[:, cols_of(j)].astype(f32))

    def forward(s, total):
        @pl.when(s == mine)
        def _():
            picked(probe_ref)

        @pl.when(s == sib)
        def _():
            picked(pr)
            send_pr().start()

        load(s).wait()
        mean = tiled(row_mean(total))
        squares = jnp.zeros((OWN, 128), f32)
        acc = jnp.zeros((OWN, HID), f32)
        columns = jnp.zeros((8, 128), f32)
        for j in range(CHUNKS):
            cols = cols_of(j)
            centred = x[:, cols].astype(f32) - mean
            squares = squares + folded(centred * centred)
            low = centred.astype(bf16)
            cb[s, :, cols] = low
            part = w[s, cols, :HID]
            acc = acc + jnp.dot(low, part, preferred_element_type=f32)
            columns = columns + jnp.sum(part.astype(f32).reshape(CHUNK // 8, 8, HID), axis=0)
        wsum[s] = columns
        spread = lax.rsqrt(row_mean(squares) + eps_norm)
        inv[s] = spread
        pre_act = acc * spread
        pre[s] = pre_act
        hidden = gelu_parts(pre_act)[0].astype(bf16)
        hid[s] = hidden

        @pl.when(s == sib)
        def _():
            send_cb().start()
            send_hid().start()

        gain = tiled(gain_of(s))
        total = jnp.zeros((OWN, 128), f32)
        for j in range(CHUNKS):
            cols = cols_of(j)
            branch = contract_last(hidden, w[s, cols, HID:])
            low = (x[:, cols].astype(f32) + gain * branch).astype(bf16)
            x[:, cols] = low
            total = total + folded(low.astype(f32))
        return total

    lax.fori_loop(0, SECTIONS, forward, total)

    keep = tiled(valid_ref[0, pl.ds(pl.multiple_of(me.c * OWN, OWN), OWN), :]) > 0.5
    last = SECTIONS - 1
    gain = tiled(gain_of(last))
    hidden_grad = jnp.zeros((OWN, HID), f32)
    for j in range(CHUNKS):
        cols = cols_of(j)
        low = jnp.where(keep, x[:, cols].astype(f32), 0.0).astype(bf16)
        g[:, cols] = low
        scaled = (gain * low.astype(f32)).astype(bf16)
        out[last % 2, :, cols] = scaled
        hidden_grad = hidden_grad + jnp.dot(scaled, w[last, cols, HID:], preferred_element_type=f32)

    @pl.when(sib == last)
    def _():
        for p in range(PIECES):
            send_out(p).start()

    def inner(s, hidden_grad):
        pre_act = pre[s]
        scaled = (inv[s] * (gelu_parts(pre_act)[1] * hidden_grad)).astype(bf16)
        pg[lax.rem(s, 2)] = scaled

        @pl.when(s == sib)
        def _():
            send_pg().start()

        return scaled, pre_act

    def backward(i, hidden_grad):
        s = last - i
        scaled_pre, pre_act = inner(s, hidden_grad)
        pre_f = scaled_pre.astype(f32)
        shift = tiled(row_mean(pre_f * jnp.sum(wsum[s], axis=0, keepdims=True)))
        slope = tiled(row_mean(pre_f * pre_act) * inv[s])
        gain = tiled(gain_of(s - 1))
        slot = lax.rem(s + 1, 2)
        hidden_grad = jnp.zeros((OWN, HID), f32)
        for j in range(CHUNKS):
            cols = cols_of(j)
            normed_grad = contract_last(scaled_pre, w[s, cols, :HID])
            low = (
                g[:, cols].astype(f32) + (normed_grad - shift - cb[s, :, cols].astype(f32) * slope)
            ).astype(bf16)
            g[:, cols] = low
            scaled = (gain * low.astype(f32)).astype(bf16)
            out[slot, :, cols] = scaled
            hidden_grad = hidden_grad + jnp.dot(scaled, w[s - 1, cols, HID:], preferred_element_type=f32)
            if (j + 1) * CHUNK % PIECE == 0:

                @pl.when(s - 1 == sib)
                def _():
                    send_out((j + 1) * CHUNK // PIECE - 1).start()

        return hidden_grad

    hidden_grad = lax.fori_loop(0, last - me.y * 2, backward, hidden_grad)
    inner(me.y * 2, hidden_grad)

    send_pr().wait()
    probe_ref[...] = (probe_ref[...].astype(f32) + pr_in[...].astype(f32)).astype(bf16)
    send_cb().wait()
    send_hid().wait()
    send_pg().wait()
    for p in range(PIECES):
        send_out(p).wait()
    pg_a, pg_b, hid_a, hid_b = pg[me.c], pg_in[...], hid[mine], hid_in[...]
    for j in range(CHUNKS):
        cols = cols_of(j)
        first = contract_first(pg_a, cb[mine, :, cols]) + contract_first(pg_b, cb_in[:, cols])
        grad_ref[cols, :HID] = first.astype(bf16).T
        second = contract_first(hid_a, out[me.c, :, cols]) + contract_first(hid_b, out_in[:, cols])
        grad_ref[cols, HID:] = second.astype(bf16).T


def relay(rows, all_weights, gains, valid):
    return pl.pallas_call(
        relay_kernel,
        out_shape=(
            jax.ShapeDtypeStruct((WIDTH, 2 * HID), bf16),
            jax.ShapeDtypeStruct((TOK, WIDTH), bf16),
        ),
        in_specs=[
            pl.BlockSpec(memory_space=pl.ANY),
            pl.BlockSpec(memory_space=pl.ANY),
            pl.BlockSpec(memory_space=pltpu.VMEM),
            pl.BlockSpec(memory_space=pltpu.VMEM),
        ],
        out_specs=(
            pl.BlockSpec(memory_space=pltpu.VMEM),
            pl.BlockSpec(memory_space=pltpu.VMEM),
        ),
        scratch_shapes=[
            pltpu.VMEM((SECTIONS, WIDTH, 2 * HID), bf16),
            pltpu.VMEM((OWN, WIDTH), bf16),
            pltpu.VMEM((OWN, WIDTH), bf16),
            pltpu.VMEM((SECTIONS, OWN, WIDTH), bf16),
            pltpu.VMEM((SECTIONS, OWN, 128), f32),
            pltpu.VMEM((SECTIONS, OWN, HID), f32),
            pltpu.VMEM((SECTIONS, OWN, HID), bf16),
            pltpu.VMEM((SECTIONS, 8, HID), f32),
            pltpu.VMEM((2, OWN, WIDTH), bf16),
            pltpu.VMEM((2, OWN, HID), bf16),
            pltpu.VMEM((OWN, WIDTH), bf16),
            pltpu.VMEM((OWN, HID), bf16),
            pltpu.VMEM((OWN, WIDTH), bf16),
            pltpu.VMEM((OWN, HID), bf16),
            pltpu.VMEM((TOK, WIDTH), bf16),
            pltpu.VMEM((TOK, WIDTH), bf16),
            pltpu.SemaphoreType.DMA((SECTIONS,)),
            pltpu.SemaphoreType.DMA,
            pltpu.SemaphoreType.DMA((3,)),
            pltpu.SemaphoreType.DMA((3,)),
            pltpu.SemaphoreType.DMA((PIECES + 1,)),
            pltpu.SemaphoreType.DMA((PIECES + 1,)),
        ],
        compiler_params=pltpu.CompilerParams(
            collective_id=2, has_side_effects=True, vmem_limit_bytes=58 * 2**20
        ),
        name="relay",
    )(rows, all_weights, gains, valid)


HALF = SHARD // 2
GROUP = SECTIONS * NX


def finish_kernel(
    grad_ref, master_ref, first_ref, second_ref, gain_ref, probe_ref,
    out_ref, new_master_ref, new_first_ref, new_second_ref,
    fresh, ra, rb, xa, xa_out, xb, tb, share, near, far,
    zs, zr, xs, xr, ns, nr, ms, mr, *ring_sems,
):
    me = Place()

    def group_at(i):
        ds, dx = i // NX, lax.rem(i, NX)
        return (lax.rem(me.s + ds, SECTIONS), me.z * NX + lax.rem(me.x + dx, NX))

    greet([group_at(i) for i in range(1, GROUP)] + [me.at_z(k) for k in range(1, NZ)])

    def target_z(flow, k):
        if flow == 0:
            return lax.rem(me.z + 9 - k, NZ)
        return lax.rem(me.z - 8 + k + NZ, NZ)

    def zcopy(flow, k, mode, first=False):
        to = me.at_z(1 if flow == 0 else -1)
        send, recv = zs.at[flow, k, mode], zr.at[flow, k, mode]
        if mode == 0:
            src = grad_ref.at[target_z(flow, k), :, pl.ds(0, HALF), :] if first else ra.at[flow, k - 1]
            return remote(src, ra.at[flow, k], send, recv, to)
        src = tb.at[target_z(flow, k)] if first else rb.at[flow, k - 1]
        return remote(src, rb.at[flow, k], send, recv, to)

    def xbcopy(dx):
        src = grad_ref.at[:, lax.rem(me.x + dx, NX), pl.ds(HALF, HALF), :]
        return remote(src, xb.at[dx], xs.at[1, dx], xr.at[1, dx], me.at_x(dx))

    def xacopy(dx):
        src = xa_out.at[lax.rem(me.x + dx, NX)]
        return remote(src, xa.at[dx], xs.at[0, dx], xr.at[0, dx], me.at_x(dx))

    for flow in range(2):
        zcopy(flow, 1, 0, True).start()
    for dx in range(1, NX):
        xbcopy(dx).start()

    def step_a(flow, k):
        zcopy(flow, k, 0).wait_recv()

        @pl.when(k < (8 if flow == 0 else 7))
        def _():
            own = grad_ref[target_z(flow, k + 1), :, pl.ds(0, HALF), :].astype(f32)
            ra[flow, k] = (ra[flow, k].astype(f32) + own).astype(bf16)
            zcopy(flow, k + 1, 0).start()

    def step_b(flow, k):
        zcopy(flow, k, 1).wait_recv()

        @pl.when(k < (8 if flow == 0 else 7))
        def _():
            rb[flow, k] = (rb[flow, k].astype(f32) + tb[target_z(flow, k + 1)].astype(f32)).astype(bf16)
            zcopy(flow, k + 1, 1).start()

    def begin_b():
        for dx in range(1, NX):
            xbcopy(dx).wait_recv()

        def add(z, carry):
            total = grad_ref[z, me.x, pl.ds(HALF, HALF), :].astype(f32)
            for dx in range(1, NX):
                total = total + xb[dx, z].astype(f32)
            tb[z] = total.astype(bf16)
            return carry

        lax.fori_loop(0, NZ, add, 0)
        for flow in range(2):
            zcopy(flow, 1, 1, True).start()

    def ring(k, carry):
        @pl.when(k <= 8)
        def _():
            step_a(0, k)

        @pl.when(k <= 7)
        def _():
            step_a(1, k)

        @pl.when(k == 3)
        def _():
            begin_b()

        @pl.when(k == 8)
        def _():
            def total(x, carry):
                block = (
                    grad_ref[me.z, x, pl.ds(0, HALF), :].astype(f32)
                    + ra[0, 8, x].astype(f32)
                    + ra[1, 7, x].astype(f32)
                )
                xa_out[x] = block.astype(bf16)
                return carry

            lax.fori_loop(0, NX, total, 0)
            for dx in range(1, NX):
                xacopy(dx).start()

        @pl.when(k > 3)
        def _():
            step_b(0, k - 3)

        @pl.when((k > 3) & (k < 11))
        def _():
            step_b(1, k - 3)

        return carry

    lax.fori_loop(1, 12, ring, 0)
    share[pl.ds(HALF, HALF), :] = tb[me.z].astype(f32) + rb[0, 8].astype(f32) + rb[1, 7].astype(f32)
    for dx in range(1, NX):
        xacopy(dx).wait_recv()
    total = xa_out[me.x].astype(f32)
    for dx in range(1, NX):
        total = total + xa[dx].astype(f32)
    share[pl.ds(0, HALF), :] = total

    squares = jnp.zeros((8, 128), f32)
    for i in range(SHARD // 8):
        for j in range(2):
            tile = share[pl.ds(i * 8, 8), pl.ds(j * 128, 128)]
            squares = squares + tile * tile
    near[0] = squares

    def ncopy(i):
        return remote(near.at[0], near.at[i], ns.at[i], nr.at[i], group_at(i))

    def mcopy(k):
        return remote(far.at[0], far.at[k], ms.at[k], mr.at[k], me.at_z(k))

    def n_start(i, carry):
        ncopy(i).start()
        return carry

    def n_wait(i, carry):
        ncopy(i).wait()
        return carry

    def m_start(i, carry):
        mcopy(i).start()
        return carry

    def m_wait(i, carry):
        mcopy(i).wait()
        return carry

    lax.fori_loop(1, GROUP, n_start, 0)
    lax.fori_loop(1, GROUP, n_wait, 0)
    far[0] = jnp.sum(near[...], axis=0)
    lax.fori_loop(1, NZ, m_start, 0)
    lax.fori_loop(1, NZ, m_wait, 0)
    norm_sq = jnp.sum(jnp.sum(far[...], axis=0), keepdims=True)
    clip_factor = 1.0 / jnp.maximum(jnp.sqrt(norm_sq), 1.0)
    clipped = share[...] * clip_factor
    master_now = master_ref[...]
    new_first = beta_one * first_ref[...] + (1.0 - beta_one) * clipped
    new_second = beta_two * second_ref[...] + (1.0 - beta_two) * clipped * clipped
    new_master = master_now - learn_rate * (
        new_first / (jnp.sqrt(new_second) + eps_adam) + decay_rate * master_now
    )
    fresh[me.z, me.x] = new_master.astype(bf16)
    new_master_ref[...] = new_master
    new_first_ref[...] = new_first
    new_second_ref[...] = new_second

    def block(z, x, lo, n):
        if x is None:
            return fresh.at[z, :, pl.ds(lo, n), :]
        return fresh.at[z, x, pl.ds(lo, n), :]

    ring_gather(me, block, HALF, *ring_sems, lambda flow, k: None)

    def drain(k, carry):
        for flow in range(2):

            @pl.when(k <= (8 if flow == 0 else 7))
            def _():
                for mode in range(2):
                    zcopy(flow, k, mode).wait_send()

        return carry

    lax.fori_loop(2, 9, drain, 0)
    for flow in range(2):
        for mode in range(2):
            zcopy(flow, 1, mode, True).wait_send()
    for dx in range(1, NX):
        xbcopy(dx).wait_send()
        xacopy(dx).wait_send()

    values = probe_ref[...].astype(f32)
    normed = normalize(values)[0].astype(bf16)
    pre_act = jnp.zeros((TOK, HID), f32)
    for z in range(NZ):
        part = fresh[z, :, :, :HID].reshape(256, HID)
        pre_act = pre_act + jnp.dot(normed[:, z * 256 : (z + 1) * 256], part, preferred_element_type=f32)
    hidden = gelu_parts(pre_act)[0].astype(bf16)
    gain = gain_ref[0:1, 0:1]
    for z in range(NZ):
        part = fresh[z, :, :, HID:].reshape(256, HID)
        cols = slice(z * 256, (z + 1) * 256)
        out_ref[:, cols] = (values[:, cols] + gain * contract_last(hidden, part)).astype(bf16)


def finish(grad, master, first_moment, second_moment, gain_tile, probe_in):
    state = jax.ShapeDtypeStruct((SHARD, 2 * HID), f32)
    vmem = pl.BlockSpec(memory_space=pltpu.VMEM)
    return pl.pallas_call(
        finish_kernel,
        out_shape=(jax.ShapeDtypeStruct((TOK, WIDTH), bf16), state, state, state),
        in_specs=[vmem] * 6,
        out_specs=(vmem,) * 4,
        scratch_shapes=[
            pltpu.VMEM((NZ, NX, SHARD, 2 * HID), bf16),
            pltpu.VMEM((2, 9, NX, HALF, 2 * HID), bf16),
            pltpu.VMEM((2, 9, HALF, 2 * HID), bf16),
            pltpu.VMEM((NX, HALF, 2 * HID), bf16),
            pltpu.VMEM((NX, HALF, 2 * HID), bf16),
            pltpu.VMEM((NX, NZ, HALF, 2 * HID), bf16),
            pltpu.VMEM((NZ, HALF, 2 * HID), bf16),
            pltpu.VMEM((SHARD, 2 * HID), f32),
            pltpu.VMEM((GROUP, 8, 128), f32),
            pltpu.VMEM((NZ, 8, 128), f32),
            pltpu.SemaphoreType.DMA((2, 9, 2)),
            pltpu.SemaphoreType.DMA((2, 9, 2)),
            pltpu.SemaphoreType.DMA((2, NX)),
            pltpu.SemaphoreType.DMA((2, NX)),
            pltpu.SemaphoreType.DMA((GROUP,)),
            pltpu.SemaphoreType.DMA((GROUP,)),
            pltpu.SemaphoreType.DMA((NZ,)),
            pltpu.SemaphoreType.DMA((NZ,)),
            *GATHER_SEMS,
        ],
        compiler_params=pltpu.CompilerParams(
            collective_id=1, has_side_effects=True, vmem_limit_bytes=40 * 2**20
        ),
        name="finish",
    )(grad, master, first_moment, second_moment, gain_tile, probe_in)


def shards(inputs, stashed, master, first_moment, second_moment, counts, plan, layer_index):
    gain_tile = jnp.full((8, 128), lax.rsqrt(1.0 + layer_index.astype(f32) / 8.0)[0], f32)
    all_weights, gains = gather_all(stashed[0], gain_tile)
    row_pos = lax.broadcasted_iota(jnp.int32, (16, TOK), 1)
    valid = row_pos < counts[0][:, None]
    chosen = lax.broadcasted_iota(jnp.int32, (16, TOK), 0) == plan[15]
    marks = jnp.stack([valid, chosen]).astype(f32).reshape(2, ROWS, 1)
    grad, probe_in = relay(
        inputs.reshape(ROWS, WIDTH),
        all_weights.reshape(2, NY, WIDTH, 2 * HID),
        gains,
        jnp.broadcast_to(marks, (2, ROWS, 128)),
    )
    probe_out, new_master, new_first, new_second = finish(
        grad.reshape(NZ, NX, SHARD, 2 * HID), master[0], first_moment[0], second_moment[0], gain_tile, probe_in
    )
    return (probe_out[None], new_master[None], new_first[None], new_second[None])


def solution(mesh):
    in_specs = (
        P(None, "dp", None),
        P("section", "dp", None),
        P("section", "dp", None),
        P("section", "dp", None),
        P("section", "dp", None),
        P("dp", None),
        P(),
        P("section"),
    )
    out_specs = (
        P("section", "dp", None),
        P("section", "dp", None),
        P("section", "dp", None),
        P("section", "dp", None),
    )
    return jax.shard_map(shards, mesh=mesh, in_specs=in_specs, out_specs=out_specs, check_vma=False)
```

```python
import functools

import jax
import jax.numpy as jnp
from jax import lax
from jax.experimental import pallas as pl
from jax.experimental.pallas import tpu as pltpu
from jax.sharding import PartitionSpec as P

eps_norm = 1e-05
beta_one = 0.9
beta_two = 0.95
eps_adam = 1e-08
learn_rate = 0.002
decay_rate = 0.1

MESH = pl.DeviceIdType.MESH
WIDTH = 4096
HID = 128
ROWS = 256
TOK = 16
SECTIONS = 8
SHARD = 64
NZ = 16
NX = 4
NY = 4
f32 = jnp.float32
bf16 = jnp.bfloat16


class Place:

    def __init__(self):
        self.s = lax.axis_index("section")
        self.d = lax.axis_index("dp")
        self.c = lax.rem(self.s, 2)
        self.y = self.s // 2
        self.z = self.d // NX
        self.x = lax.rem(self.d, NX)

    def at_z(self, k):
        return (self.s, lax.rem(self.z + k + 2 * NZ, NZ) * NX + self.x)

    def at_x(self, k):
        return (self.s, self.z * NX + lax.rem(self.x + k + NX, NX))

    def at_y(self, k):
        return (lax.rem(self.y + k + NY, NY) * 2 + self.c, self.d)

    def sibling(self):
        return (self.y * 2 + 1 - self.c, self.d)


def greet(partners):
    barrier = pltpu.get_barrier_semaphore()
    for partner in partners:
        pl.semaphore_signal(barrier, inc=1, device_id=partner, device_id_type=MESH)
    pl.semaphore_wait(barrier, len(partners))


def remote(src, dst, send, recv, to):
    return pltpu.make_async_remote_copy(
        src_ref=src, dst_ref=dst, send_sem=send, recv_sem=recv, device_id=to, device_id_type=MESH
    )


def block_z(me, flow, k):
    if flow == 0:
        return lax.rem(me.z - k + 2 * NZ, NZ)
    return lax.rem(me.z + k, NZ)


def last_of(flow):
    return 8 if flow == 0 else 7


def when_in(flow, k, lowest):
    low = max(flow, lowest)
    return pl.when((k >= low) & (k <= last_of(flow)))


class OverX:
    def __init__(self, me, part, at, here, sems):
        self.me, self.part, self.at, self.here = me, part, at, here
        self.ss, self.sr, self.fs, self.fr = sems

    def copy(self, flow, k, side):
        ref = self.part(block_z(self.me, flow, k), self.here)
        to = self.at(1 if side == 0 else -1)
        return remote(ref, ref, self.ss.at[flow, k, side], self.sr.at[flow, k, side], to)

    def onward(self, flow, k):
        came = -1 if flow == 0 else 1
        ref = self.part(block_z(self.me, flow, k), lax.rem(self.here + came + 4, 4))
        return remote(ref, ref, self.fs.at[flow, k], self.fr.at[flow, k], self.at(-came))

    def send(self, flow, k):
        for side in range(2):
            self.copy(flow, k, side).start()

    def pass_on(self, k):
        for flow in range(2):

            @when_in(flow, k, 0)
            def _():
                for side in range(2):
                    self.copy(flow, k, side).wait_recv()
                self.onward(flow, k).start()

    def wait(self, flow, k):
        self.onward(flow, k).wait_recv()

    def drain(self, flow, k):
        for side in range(2):
            self.copy(flow, k, side).wait_send()
        self.onward(flow, k).wait_send()


class RoundZ:
    def __init__(self, me, part, sems, stride):
        self.me, self.part, self.stride = me, part, stride
        self.zs, self.zr = sems[0], sems[1]
        self.over = OverX(me, part, me.at_x, me.x, sems[2:])

    def copy(self, flow, k, hop=1):
        ref = self.part(block_z(self.me, flow, k - hop), self.me.x)
        to = self.me.at_z(hop if flow == 0 else -hop)
        return remote(ref, ref, self.zs.at[flow, k], self.zr.at[flow, k], to)

    def begin(self):
        for hop in range(1, self.stride + 1):
            for flow in range(2):
                self.copy(flow, hop, hop).start()
        self.over.send(0, 0)

    def step(self, j):
        far = j * self.stride
        for flow in range(2):

            @when_in(flow, far, 1)
            def _():
                self.copy(flow, far, self.stride).wait_recv()

                for hop in range(1, self.stride + 1):

                    @pl.when(far + hop <= last_of(flow))
                    def _():
                        self.copy(flow, far + hop, hop).start()

                self.over.send(flow, far)

        if self.stride == 2:
            for flow in range(2):

                @when_in(flow, far - 1, 1)
                def _():
                    self.copy(flow, far - 1, 1).wait_recv()
                    self.over.send(flow, far - 1)

    def steps_of(self, j):
        return [j * self.stride - i for i in range(self.stride)]

    def pass_on(self, j):
        for k in self.steps_of(j):
            self.over.pass_on(k)

    def wait(self, j):
        for k in self.steps_of(j):
            for flow in range(2):

                @when_in(flow, k, 0)
                def _():
                    self.over.wait(flow, k)

    def drain(self, j):
        for i, k in enumerate(self.steps_of(j)):
            for flow in range(2):

                @when_in(flow, k, 1)
                def _():
                    self.copy(flow, k, self.stride - i).wait_send()

                @when_in(flow, k, 0)
                def _():
                    self.over.drain(flow, k)


class BlocksRoundZ:
    def __init__(self, me, part, block, sems, stride):
        self.me, self.part, self.block, self.stride = me, part, block, stride
        self.xs, self.xr, self.zs, self.zr = sems

    def first(self, dx):
        ref = self.part(self.me.z, self.me.x)
        return remote(ref, ref, self.xs.at[dx], self.xr.at[dx], self.me.at_x(dx))

    def copy(self, flow, k, hop, piece):
        ref = self.block(block_z(self.me, flow, k - hop), piece)
        to = self.me.at_z(hop if flow == 0 else -hop)
        return remote(ref, ref, self.zs.at[flow, k, piece], self.zr.at[flow, k, piece], to)

    def begin(self):
        for dx in range(1, NX):
            self.first(dx).start()

    def launch(self):
        for dx in range(1, NX):
            self.first(dx).wait_recv()
        for piece in range(2):
            for hop in range(1, self.stride + 1):
                for flow in range(2):
                    self.copy(flow, hop, hop, piece).start()

    def step(self, j):
        far = j * self.stride
        for piece in range(2):
            for flow in range(2):
                end = 8 if flow == piece else 7

                @pl.when((far >= 1) & (far <= end))
                def _():
                    self.copy(flow, far, self.stride, piece).wait_recv()

                    for hop in range(1, self.stride + 1):

                        @pl.when(far + hop <= end)
                        def _():
                            self.copy(flow, far + hop, hop, piece).start()

        if self.stride == 2:
            for piece in range(2):
                for flow in range(2):

                    @pl.when((far >= 2) & (far <= 8))
                    def _():
                        self.copy(flow, far - 1, 1, piece).wait_recv()

    def drain(self, j):
        for i in range(self.stride):
            k = j * self.stride - i
            for piece in range(2):
                for flow in range(2):

                    @pl.when((k >= 1) & (k <= (8 if flow == piece else 7)))
                    def _():
                        self.copy(flow, k, self.stride - i, piece).wait_send()

    def finish(self):
        for dx in range(1, NX):
            self.first(dx).wait_send()


DMA = pltpu.SemaphoreType.DMA
ROUND_SEMS = [DMA((2, 9)), DMA((2, 9)), DMA((2, 9, 2)), DMA((2, 9, 2)), DMA((2, 9)), DMA((2, 9))]
BLOCK_SEMS = [DMA((NX,)), DMA((NX,)), DMA((2, 9, 2)), DMA((2, 9, 2))]
OVER_SEMS = [DMA((2, 9, 2)), DMA((2, 9, 2)), DMA((2, 9)), DMA((2, 9))]

ROWS_XZ, ROWS_ZX, ROWS_ZXY = 16, 16, 32


def gather_all(me, w_ref, gain_ref, all_ref, gains_ref, ys, yr, gs, gr, ss, sr, own, *sems):
    early = ROWS_XZ + ROWS_ZX

    def ycopy(k):
        rows = pl.ds(0, early)
        dst = all_ref.at[me.c, me.y, me.z, me.x, rows]
        return remote(w_ref.at[rows], dst, ys.at[k], yr.at[k], me.at_y(k))

    def gcopy(k):
        return remote(gain_ref, gains_ref.at[me.c, me.y], gs.at[k], gr.at[k], me.at_y(k))

    keep = pltpu.make_async_copy(w_ref, all_ref.at[me.c, me.y, me.z, me.x], own.at[0])
    keep_gain = pltpu.make_async_copy(gain_ref, gains_ref.at[me.c, me.y], own.at[1])
    keep.start()
    keep_gain.start()
    for k in range(1, NY):
        ycopy(k).start()
        gcopy(k).start()
    keep.wait()

    def late_part(z, x):
        return all_ref.at[me.c, me.y, z, x, pl.ds(early, ROWS_ZXY)]

    def late_column(z, y):
        return all_ref.at[me.c, y, z, :, pl.ds(early, ROWS_ZXY)]

    def mid_part(z, x):
        return all_ref.at[me.c, :, z, x, pl.ds(ROWS_XZ, ROWS_ZX)]

    def early_part(z, x):
        return all_ref.at[me.c, :, z, x, pl.ds(0, ROWS_XZ)]

    def early_block(z, piece):
        return all_ref.at[me.c, pl.ds(2 * piece, 2), z, :, pl.ds(0, ROWS_XZ)]

    late = RoundZ(me, late_part, sems[0:6], 1)
    mid = RoundZ(me, mid_part, sems[6:12], 1)
    blocks = BlocksRoundZ(me, early_part, early_block, sems[12:16], 1)
    over_y = OverX(me, late_column, me.at_y, me.y, sems[16:20])

    def side_copy(flow, k):
        part = all_ref.at[me.c, :, block_z(me, flow, k)]
        return remote(part, part, ss.at[flow, k], sr.at[flow, k], me.sibling())

    late.begin()
    for k in range(1, NY):
        ycopy(k).wait_recv()
    blocks.begin()
    mid.begin()
    keep_gain.wait()
    for k in range(1, NY):
        gcopy(k).wait_recv()
    gains = remote(gains_ref.at[me.c], gains_ref.at[me.c], ss.at[2, 0], sr.at[2, 0], me.sibling())
    gains.start()

    def drain(k):
        late.drain(k)
        mid.drain(k)
        blocks.drain(k)
        for flow in range(2):

            @when_in(flow, k, 0)
            def _():
                over_y.drain(flow, k)

    def step(t, carry):
        late.step(t)
        mid.step(t - 1)
        late.pass_on(t - 1)
        mid.pass_on(t - 2)
        late.wait(t - 2)
        for flow in range(2):

            @when_in(flow, t - 2, 0)
            def _():
                over_y.send(flow, t - 2)

        mid.wait(t - 3)
        over_y.pass_on(t - 3)

        @pl.when(t == 2)
        def _():
            blocks.launch()

        blocks.step(t - 2)
        for flow in range(2):

            @when_in(flow, t - 4, 0)
            def _():
                over_y.wait(flow, t - 4)
                side_copy(flow, t - 4).start()

        drain(t - 6)
        return carry

    lax.fori_loop(1, 13, step, 0)

    for k in (7, 8):
        drain(k)
    blocks.finish()

    def finish(k, carry):
        for flow in range(2):

            @when_in(flow, k, 0)
            def _():
                side_copy(flow, k).wait()

        return carry

    lax.fori_loop(0, 9, finish, 0)
    gains.wait()
    for k in range(1, NY):
        ycopy(k).wait_send()
        gcopy(k).wait_send()


def normalize(values):
    centred = values - jnp.mean(values, axis=-1, keepdims=True)
    inv_spread = lax.rsqrt(jnp.mean(centred * centred, axis=-1, keepdims=True) + eps_norm)
    return (centred * inv_spread, inv_spread)


def contract_last(lhs_array, rhs_array):
    return lax.dot_general(
        lhs_array, rhs_array, (((1,), (1,)), ((), ())), preferred_element_type=f32
    )


def contract_first(lhs_array, rhs_array):
    return lax.dot_general(
        lhs_array, rhs_array, (((0,), (0,)), ((), ())), preferred_element_type=f32
    )


root_two_over_pi = 0.7978845608028654
cubic = 0.044715


def gelu_parts(v):
    t = jnp.tanh(root_two_over_pi * (v + cubic * (v * v * v)))
    cdf = 0.5 * (1.0 + t)
    slope = cdf + 0.5 * v * (1.0 - t * t) * (root_two_over_pi * (1.0 + 3.0 * cubic * v * v))
    return v * cdf, slope


OWN = ROWS // 2
CHUNK = 512
CHUNKS = WIDTH // CHUNK
PIECES = 4
PIECE = WIDTH // PIECES


def tiled(a):
    return jnp.concatenate([a] * (CHUNK // 128), axis=1)


def folded(a):
    total = a[:, 0:128]
    for i in range(1, a.shape[1] // 128):
        total = total + a[:, i * 128 : (i + 1) * 128]
    return total


def row_mean(a):
    return jnp.broadcast_to(jnp.sum(a, axis=-1, keepdims=True) * (1.0 / WIDTH), (OWN, 128))


def relay(
    me, w, gains_ref, valid_ref, grad_ref, probe_ref,
    x, g, cb, inv, pre, hid, wsum, out, pg, cb_in, hid_in, out_in, pg_in, pr, pr_in,
    fs, fr, bs, br,
):
    mine = me.s
    sib = me.y * 2 + 1 - me.c

    def span(j):
        return slice(j * (CHUNK // 256), (j + 1) * (CHUNK // 256))

    def weight(s, j, half):
        cols = slice(half * HID, (half + 1) * HID)
        return w[lax.rem(s, 2), s // 2, span(j), :, :, cols].reshape(CHUNK, HID)

    def send_cb():
        return remote(cb.at[sib], cb_in, fs.at[0], fr.at[0], me.sibling())

    def send_hid():
        return remote(hid.at[sib], hid_in, fs.at[1], fr.at[1], me.sibling())

    def send_pr():
        return remote(pr, pr_in, fs.at[2], fr.at[2], me.sibling())

    def send_out(p):
        cols = pl.ds(p * PIECE, PIECE)
        return remote(out.at[1 - me.c, :, cols], out_in.at[:, cols], bs.at[p], br.at[p], me.sibling())

    def send_pg():
        return remote(pg.at[1 - me.c], pg_in, bs.at[PIECES], br.at[PIECES], me.sibling())

    def gain_of(s):
        return gains_ref[lax.rem(s, 2), s // 2, 0:1, :]

    def cols_of(j):
        return slice(j * CHUNK, (j + 1) * CHUNK)

    def picked(ref):
        for j in range(CHUNKS):
            cols = cols_of(j)
            rows = jnp.zeros((TOK, CHUNK), f32)
            for i in range(OWN // TOK):
                part = pl.ds(i * TOK, TOK)
                chosen = valid_ref[1, pl.ds(pl.multiple_of(me.c * OWN + i * TOK, TOK), TOK), :]
                rows = rows + tiled(chosen) * x[part, cols].astype(f32)
            ref[:, cols] = rows.astype(bf16)

    total = jnp.zeros((OWN, 128), f32)
    for j in range(CHUNKS):
        total = total + folded(x[:, cols_of(j)].astype(f32))

    def forward(s, total):
        @pl.when(s == mine)
        def _():
            picked(probe_ref)

        @pl.when(s == sib)
        def _():
            picked(pr)
            send_pr().start()

        mean = tiled(row_mean(total))
        squares = jnp.zeros((OWN, 128), f32)
        acc = jnp.zeros((OWN, HID), f32)
        columns = jnp.zeros((8, 128), f32)
        for j in range(CHUNKS):
            cols = cols_of(j)
            centred = x[:, cols].astype(f32) - mean
            squares = squares + folded(centred * centred)
            low = centred.astype(bf16)
            cb[s, :, cols] = low
            part = weight(s, j, 0)
            acc = acc + jnp.dot(low, part, preferred_element_type=f32)
            columns = columns + jnp.sum(part.astype(f32).reshape(CHUNK // 8, 8, HID), axis=0)
        wsum[s] = columns
        spread = lax.rsqrt(row_mean(squares) + eps_norm)
        inv[s] = spread
        pre_act = acc * spread
        pre[s] = pre_act
        hidden = gelu_parts(pre_act)[0].astype(bf16)
        hid[s] = hidden

        @pl.when(s == sib)
        def _():
            send_cb().start()
            send_hid().start()

        gain = tiled(gain_of(s))
        total = jnp.zeros((OWN, 128), f32)
        for j in range(CHUNKS):
            cols = cols_of(j)
            branch = contract_last(hidden, weight(s, j, 1))
            low = (x[:, cols].astype(f32) + gain * branch).astype(bf16)
            x[:, cols] = low
            total = total + folded(low.astype(f32))
        return total

    lax.fori_loop(0, SECTIONS, forward, total)

    keep = tiled(valid_ref[0, pl.ds(pl.multiple_of(me.c * OWN, OWN), OWN), :]) > 0.5
    last = SECTIONS - 1
    gain = tiled(gain_of(last))
    hidden_grad = jnp.zeros((OWN, HID), f32)
    for j in range(CHUNKS):
        cols = cols_of(j)
        low = jnp.where(keep, x[:, cols].astype(f32), 0.0).astype(bf16)
        g[:, cols] = low
        scaled = (gain * low.astype(f32)).astype(bf16)
        out[1, :, cols] = scaled
        hidden_grad = hidden_grad + jnp.dot(scaled, weight(last, j, 1), preferred_element_type=f32)

    @pl.when(sib == last)
    def _():
        for p in range(PIECES):
            send_out(p).start()

    def inner(s, hidden_grad):
        pre_act = pre[s]
        scaled = (inv[s] * (gelu_parts(pre_act)[1] * hidden_grad)).astype(bf16)
        pg[lax.rem(s, 2)] = scaled

        @pl.when(s == sib)
        def _():
            send_pg().start()

        return scaled, pre_act

    def backward(i, hidden_grad):
        s = last - i
        scaled_pre, pre_act = inner(s, hidden_grad)
        pre_f = scaled_pre.astype(f32)
        shift = tiled(row_mean(pre_f * jnp.sum(wsum[s], axis=0, keepdims=True)))
        slope = tiled(row_mean(pre_f * pre_act) * inv[s])
        gain = tiled(gain_of(s - 1))
        slot = lax.rem(s + 1, 2)
        hidden_grad = jnp.zeros((OWN, HID), f32)
        for j in range(CHUNKS):
            cols = cols_of(j)
            normed_grad = contract_last(scaled_pre, weight(s, j, 0))
            low = (
                g[:, cols].astype(f32) + (normed_grad - shift - cb[s, :, cols].astype(f32) * slope)
            ).astype(bf16)
            g[:, cols] = low
            scaled = (gain * low.astype(f32)).astype(bf16)
            out[slot, :, cols] = scaled
            hidden_grad = hidden_grad + jnp.dot(scaled, weight(s - 1, j, 1), preferred_element_type=f32)
            if (j + 1) * CHUNK % PIECE == 0:

                @pl.when(s - 1 == sib)
                def _():
                    send_out((j + 1) * CHUNK // PIECE - 1).start()

        return hidden_grad

    hidden_grad = lax.fori_loop(0, last - me.y * 2, backward, hidden_grad)
    inner(me.y * 2, hidden_grad)

    send_pr().wait()
    probe_ref[...] = (probe_ref[...].astype(f32) + pr_in[...].astype(f32)).astype(bf16)
    send_cb().wait()
    send_hid().wait()
    send_pg().wait()
    for p in range(PIECES):
        send_out(p).wait()
    pg_a, pg_b, hid_a, hid_b = pg[me.c], pg_in[...], hid[mine], hid_in[...]
    for j in range(CHUNKS):
        cols = cols_of(j)
        first = contract_first(pg_a, cb[mine, :, cols]) + contract_first(pg_b, cb_in[:, cols])
        grad_ref[span(j), :, :, :HID] = first.astype(bf16).T.reshape(CHUNK // 256, NX, SHARD, HID)
        second = contract_first(hid_a, out[me.c, :, cols]) + contract_first(hid_b, out_in[:, cols])
        grad_ref[span(j), :, :, HID:] = second.astype(bf16).T.reshape(CHUNK // 256, NX, SHARD, HID)


ROWS_Z, ROWS_X = 32, 32
FRESH_XZ, FRESH_ZX = 16, 48
GROUP = SECTIONS * NX


class SumRoundZ:
    def __init__(self, me, own, held, sems, index):
        self.me, self.own, self.held, self.index = me, own, held, index
        self.zs, self.zr = sems

    def target(self, flow, k):
        return block_z(self.me, 1 - flow, k)

    def copy(self, flow, k):
        first = k % 2 == 1 or k == 8
        hop = 1 if k % 2 else 2
        to = self.me.at_z(hop if flow == 0 else -hop)
        src = self.own(self.target(flow, k)) if first else self.held(flow, k + 2 if k < 6 or flow == 0 else 7)
        return remote(src, self.held(flow, k), self.zs.at[flow, k, self.index], self.zr.at[flow, k, self.index], to)

    def begin(self):
        for k in (8, 7, 5, 3, 1):
            for flow in range(2):
                if k <= last_of(flow):
                    self.copy(flow, k).start()

    def step(self, k):
        for flow in range(2):
            into = k + 2 if k < 6 or flow == 0 else 7
            for i in ((7, 8) if k == 6 else (k + 1, k + 2)):
                if i <= last_of(flow):
                    self.copy(flow, i).wait_recv()
            own = self.own(self.target(flow, k))
            total = own[...].astype(f32) + self.held(flow, into)[...].astype(f32)
            if into != k + 1:
                total = total + self.held(flow, k + 1)[...].astype(f32)
            self.held(flow, into)[...] = total.astype(bf16)
            self.copy(flow, k).start()

    def wait(self):
        for flow in range(2):
            for k in (1, 2):
                self.copy(flow, k).wait_recv()

    def result(self):
        total = self.own(self.me.z)[...].astype(f32)
        for flow in range(2):
            for k in (1, 2):
                total = total + self.held(flow, k)[...].astype(f32)
        return total

    def drain(self):
        for flow in range(2):
            for k in range(1, last_of(flow) + 1):
                self.copy(flow, k).wait_send()


def finish(
    me, grad_ref, master_ref, first_ref, second_ref, gain_ref, probe_ref,
    out_ref, new_master_ref, new_first_ref, new_second_ref,
    fresh, ra, rb, xa, xa_out, xb, tb, share, near, far,
    zs, zr, xs, xr, ns, nr, ms, mr, *sems,
):
    def group_at(i):
        ds, dx = i // NX, lax.rem(i, NX)
        return (lax.rem(me.s + ds, SECTIONS), me.z * NX + lax.rem(me.x + dx, NX))

    def xbcopy(dx):
        src = grad_ref.at[:, lax.rem(me.x + dx, NX), pl.ds(ROWS_Z, ROWS_X), :]
        return remote(src, xb.at[dx], xs.at[1, dx], xr.at[1, dx], me.at_x(dx))

    def xacopy(dx):
        src = xa_out.at[lax.rem(me.x + dx, NX)]
        return remote(src, xa.at[dx], xs.at[0, dx], xr.at[0, dx], me.at_x(dx))

    def piece_sum(piece):
        pair = pl.ds(2 * piece, 2)
        return SumRoundZ(
            me,
            lambda z: grad_ref.at[z, pair, pl.ds(0, ROWS_Z), :],
            lambda flow, k: ra.at[flow, k, pair],
            (zs, zr),
            piece,
        )

    pieces = [piece_sum(0), piece_sum(1)]
    late = SumRoundZ(me, lambda z: tb.at[z], lambda flow, k: rb.at[flow, k], (zs, zr), 2)
    for piece in pieces:
        piece.begin()
    for dx in range(1, NX):
        xbcopy(dx).start()
    for piece in pieces:
        piece.step(6)
    for piece in pieces:
        piece.step(4)
    for dx in range(1, NX):
        xbcopy(dx).wait_recv()

    def add(z, carry):
        total = grad_ref[z, me.x, pl.ds(ROWS_Z, ROWS_X), :].astype(f32)
        for dx in range(1, NX):
            total = total + xb[dx, z].astype(f32)
        tb[z] = total.astype(bf16)
        return carry

    lax.fori_loop(0, NZ, add, 0)
    late.begin()
    for piece in pieces:
        piece.step(2)
    late.step(6)
    for i, piece in enumerate(pieces):
        piece.wait()
        xa_out[pl.ds(2 * i, 2)] = piece.result().astype(bf16)
    for dx in range(1, NX):
        xacopy(dx).start()
    late.step(4)
    late.step(2)
    for dx in range(1, NX):
        xacopy(dx).wait_recv()
    total = xa_out[me.x].astype(f32)
    for dx in range(1, NX):
        total = total + xa[dx].astype(f32)
    share[pl.ds(0, ROWS_Z), :] = total
    late.wait()
    share[pl.ds(ROWS_Z, ROWS_X), :] = late.result()

    squares = jnp.zeros((8, 128), f32)
    for i in range(SHARD // 8):
        for j in range(2):
            tile = share[pl.ds(i * 8, 8), pl.ds(j * 128, 128)]
            squares = squares + tile * tile
    near[0] = squares

    def ncopy(i):
        return remote(near.at[0], near.at[i], ns.at[i], nr.at[i], group_at(i))

    def mcopy(k):
        return remote(far.at[0], far.at[k], ms.at[k], mr.at[k], me.at_z(k))

    def n_start(i, carry):
        ncopy(i).start()
        return carry

    def n_wait(i, carry):
        ncopy(i).wait()
        return carry

    def m_start(i, carry):
        mcopy(i).start()
        return carry

    def m_wait(i, carry):
        mcopy(i).wait()
        return carry

    lax.fori_loop(1, GROUP, n_start, 0)
    lax.fori_loop(1, GROUP, n_wait, 0)
    far[0] = jnp.sum(near[...], axis=0)
    lax.fori_loop(1, NZ, m_start, 0)
    lax.fori_loop(1, NZ, m_wait, 0)
    norm_sq = jnp.sum(jnp.sum(far[...], axis=0), keepdims=True)

    clip_factor = 1.0 / jnp.maximum(jnp.sqrt(norm_sq), 1.0)
    clipped = share[...] * clip_factor
    master_now = master_ref[...]
    new_first = beta_one * first_ref[...] + (1.0 - beta_one) * clipped
    new_second = beta_two * second_ref[...] + (1.0 - beta_two) * clipped * clipped
    new_master = master_now - learn_rate * (
        new_first / (jnp.sqrt(new_second) + eps_adam) + decay_rate * master_now
    )
    fresh[me.z, me.x] = new_master.astype(bf16)
    new_master_ref[...] = new_master
    new_first_ref[...] = new_first
    new_second_ref[...] = new_second

    def early_part(z, x):
        return fresh.at[z, x, pl.ds(0, FRESH_XZ)]

    def early_block(z, piece):
        return fresh.at[z, pl.ds(2 * piece, 2), pl.ds(0, FRESH_XZ)]

    def mid_part(z, x):
        return fresh.at[z, x, pl.ds(FRESH_XZ, FRESH_ZX)]

    mid = RoundZ(me, mid_part, sems[0:6], 2)
    blocks = BlocksRoundZ(me, early_part, early_block, sems[6:10], 2)
    blocks.begin()
    mid.begin()
    blocks.launch()

    def step(t, carry):
        mid.step(t)
        blocks.step(t)
        mid.pass_on(t - 1)
        mid.wait(t - 2)
        return carry

    lax.fori_loop(1, 7, step, 0)
    values = probe_ref[...].astype(f32)
    normed = normalize(values)[0].astype(bf16)
    pre_act = jnp.zeros((TOK, HID), f32)
    for z in range(NZ):
        part = fresh[z, :, :, :HID].reshape(256, HID)
        pre_act = pre_act + jnp.dot(normed[:, z * 256 : (z + 1) * 256], part, preferred_element_type=f32)
    hidden = gelu_parts(pre_act)[0].astype(bf16)
    gain = gain_ref[0:1, 0:1]
    for z in range(NZ):
        part = fresh[z, :, :, HID:].reshape(256, HID)
        cols = slice(z * 256, (z + 1) * 256)
        out_ref[:, cols] = (values[:, cols] + gain * contract_last(hidden, part)).astype(bf16)
    def drain(t, carry):
        mid.drain(t)
        blocks.drain(t)
        return carry

    lax.fori_loop(0, 5, drain, 0)
    blocks.finish()
    for piece in pieces:
        piece.drain()
    late.drain()
    for dx in range(1, NX):
        xbcopy(dx).wait_send()
        xacopy(dx).wait_send()


def partners(me):
    ys = [me.at_y(k) for k in range(1, NY)]
    xs = [me.at_x(k) for k in range(1, NX)]
    return ys + xs + [me.at_z(k) for k in (1, 2, -1, -2)] + [me.sibling()]


N_GATHER, N_RELAY, N_FINISH = 27, 4, 18


def step_kernel(
    w_ref, gain_ref, x_hbm, marks_ref, master_ref, first_ref, second_ref,
    out_ref, new_master_ref, new_first_ref, new_second_ref,
    w, gains, grad, probe,
    x, g, cb, inv, pre, hid, wsum, out, pg, cb_in, hid_in, out_in, pg_in, pr, pr_in,
    fresh, ra, rb, xa, xa_out, xb, tb, share, near, far,
    x_sem, *sems,
):
    me = Place()
    get_x = pltpu.make_async_copy(
        x_hbm.at[pl.ds(pl.multiple_of(me.c * OWN, OWN), OWN)], x, x_sem
    )
    get_x.start()
    greet(partners(me))
    gather_all(me, w_ref, gain_ref, w, gains, *sems[:N_GATHER])
    get_x.wait()
    relay(
        me, w, gains, marks_ref, grad, probe,
        x, g, cb, inv, pre, hid, wsum, out, pg, cb_in, hid_in, out_in, pg_in, pr, pr_in,
        *sems[N_GATHER : N_GATHER + N_RELAY],
    )
    finish(
        me, grad, master_ref, first_ref, second_ref, gain_ref, probe,
        out_ref, new_master_ref, new_first_ref, new_second_ref,
        fresh, ra, rb, xa, xa_out, xb, tb, share, near, far,
        *sems[N_GATHER + N_RELAY :],
    )


def shards(inputs, stashed, master, first_moment, second_moment, counts, plan, layer_index):
    gain_tile = jnp.full((8, 128), lax.rsqrt(1.0 + layer_index.astype(f32) / 8.0)[0], f32)
    row_pos = lax.broadcasted_iota(jnp.int32, (16, TOK), 1)
    valid = row_pos < counts[0][:, None]
    chosen = lax.broadcasted_iota(jnp.int32, (16, TOK), 0) == plan[15]
    marks = jnp.stack([valid, chosen]).astype(f32).reshape(2, ROWS, 1)
    state = jax.ShapeDtypeStruct((SHARD, 2 * HID), f32)
    vmem = pl.BlockSpec(memory_space=pltpu.VMEM)
    chunks = (NZ, NX, SHARD, 2 * HID)
    probe_out, new_master, new_first, new_second = pl.pallas_call(
        step_kernel,
        out_shape=(jax.ShapeDtypeStruct((TOK, WIDTH), bf16), state, state, state),
        in_specs=[vmem, vmem, pl.BlockSpec(memory_space=pl.ANY), vmem, vmem, vmem, vmem],
        out_specs=(vmem,) * 4,
        scratch_shapes=[
            pltpu.VMEM((2, NY, *chunks), bf16),
            pltpu.VMEM((2, NY, 8, 128), f32),
            pltpu.VMEM(chunks, bf16),
            pltpu.VMEM((TOK, WIDTH), bf16),
            pltpu.VMEM((OWN, WIDTH), bf16),
            pltpu.VMEM((OWN, WIDTH), bf16),
            pltpu.VMEM((SECTIONS, OWN, WIDTH), bf16),
            pltpu.VMEM((SECTIONS, OWN, 128), f32),
            pltpu.VMEM((SECTIONS, OWN, HID), f32),
            pltpu.VMEM((SECTIONS, OWN, HID), bf16),
            pltpu.VMEM((SECTIONS, 8, HID), f32),
            pltpu.VMEM((2, OWN, WIDTH), bf16),
            pltpu.VMEM((2, OWN, HID), bf16),
            pltpu.VMEM((OWN, WIDTH), bf16),
            pltpu.VMEM((OWN, HID), bf16),
            pltpu.VMEM((OWN, WIDTH), bf16),
            pltpu.VMEM((OWN, HID), bf16),
            pltpu.VMEM((TOK, WIDTH), bf16),
            pltpu.VMEM((TOK, WIDTH), bf16),
            pltpu.VMEM(chunks, bf16),
            pltpu.VMEM((2, 9, NX, ROWS_Z, 2 * HID), bf16),
            pltpu.VMEM((2, 9, ROWS_X, 2 * HID), bf16),
            pltpu.VMEM((NX, ROWS_Z, 2 * HID), bf16),
            pltpu.VMEM((NX, ROWS_Z, 2 * HID), bf16),
            pltpu.VMEM((NX, NZ, ROWS_X, 2 * HID), bf16),
            pltpu.VMEM((NZ, ROWS_X, 2 * HID), bf16),
            pltpu.VMEM((SHARD, 2 * HID), f32),
            pltpu.VMEM((GROUP, 8, 128), f32),
            pltpu.VMEM((NZ, 8, 128), f32),
            DMA,
            *[DMA((NY,))] * 4,
            *[DMA((3, 9))] * 2,
            DMA((2,)),
            *ROUND_SEMS,
            *ROUND_SEMS,
            *BLOCK_SEMS,
            *OVER_SEMS,
            *[DMA((3,))] * 2,
            *[DMA((PIECES + 1,))] * 2,
            *[DMA((2, 9, 3))] * 2,
            *[DMA((2, NX))] * 2,
            *[DMA((GROUP,))] * 2,
            *[DMA((NZ,))] * 2,
            *ROUND_SEMS,
            *BLOCK_SEMS,
        ],
        compiler_params=pltpu.CompilerParams(
            collective_id=0, has_side_effects=True, vmem_limit_bytes=60 * 2**20
        ),
        name="optimizer_step",
    )(
        stashed[0], gain_tile, inputs.reshape(ROWS, WIDTH),
        jnp.broadcast_to(marks, (2, ROWS, 128)), master[0], first_moment[0], second_moment[0],
    )
    return (probe_out[None], new_master[None], new_first[None], new_second[None])


def solution(mesh):
    in_specs = (
        P(None, "dp", None),
        P("section", "dp", None),
        P("section", "dp", None),
        P("section", "dp", None),
        P("section", "dp", None),
        P("dp", None),
        P(),
        P("section"),
    )
    out_specs = (
        P("section", "dp", None),
        P("section", "dp", None),
        P("section", "dp", None),
        P("section", "dp", None),
    )
    return jax.shard_map(shards, mesh=mesh, in_specs=in_specs, out_specs=out_specs, check_vma=False)
```

```python
import functools

import jax
import jax.numpy as jnp
from jax import lax
from jax.experimental import pallas as pl
from jax.experimental.pallas import tpu as pltpu
from jax.sharding import PartitionSpec as P

eps_norm = 1e-05
beta_one = 0.9
beta_two = 0.95
eps_adam = 1e-08
learn_rate = 0.002
decay_rate = 0.1

MESH = pl.DeviceIdType.MESH
WIDTH = 4096
HID = 128
ROWS = 256
TOK = 16
SECTIONS = 8
SHARD = 64
NZ = 16
NX = 4
NY = 4
f32 = jnp.float32
bf16 = jnp.bfloat16


class Place:

    def __init__(self):
        self.s = lax.axis_index("section")
        self.d = lax.axis_index("dp")
        self.c = lax.rem(self.s, 2)
        self.y = self.s // 2
        self.z = self.d // NX
        self.x = lax.rem(self.d, NX)

    def at_z(self, k):
        return (self.s, lax.rem(self.z + k + 2 * NZ, NZ) * NX + self.x)

    def at_x(self, k):
        return (self.s, self.z * NX + lax.rem(self.x + k + NX, NX))

    def at_y(self, k):
        return (lax.rem(self.y + k + NY, NY) * 2 + self.c, self.d)

    def sibling(self):
        return (self.y * 2 + 1 - self.c, self.d)


def greet(partners):
    barrier = pltpu.get_barrier_semaphore()
    for partner in partners:
        pl.semaphore_signal(barrier, inc=1, device_id=partner, device_id_type=MESH)
    pl.semaphore_wait(barrier, len(partners))


def remote(src, dst, send, recv, to):
    return pltpu.make_async_remote_copy(
        src_ref=src, dst_ref=dst, send_sem=send, recv_sem=recv, device_id=to, device_id_type=MESH
    )


def block_z(me, flow, k):
    if flow == 0:
        return lax.rem(me.z - k + 2 * NZ, NZ)
    return lax.rem(me.z + k, NZ)


def last_of(flow):
    return 8 if flow == 0 else 7


def inside(flow, k, lowest):
    return max(flow, lowest) <= k <= last_of(flow)


class OverX:
    def __init__(self, me, part, at, here, sems):
        self.me, self.part, self.at, self.here = me, part, at, here
        self.ss, self.sr, self.fs, self.fr = sems

    def copy(self, flow, k, side):
        ref = self.part(block_z(self.me, flow, k), self.here)
        to = self.at(1 if side == 0 else -1)
        return remote(ref, ref, self.ss.at[flow, k, side], self.sr.at[flow, k, side], to)

    def onward(self, flow, k):
        came = -1 if flow == 0 else 1
        ref = self.part(block_z(self.me, flow, k), lax.rem(self.here + came + 4, 4))
        return remote(ref, ref, self.fs.at[flow, k], self.fr.at[flow, k], self.at(-came))

    def send(self, flow, k):
        for side in range(2):
            self.copy(flow, k, side).start()

    def pass_on(self, k):
        for flow in range(2):
            if inside(flow, k, 0):
                for side in range(2):
                    self.copy(flow, k, side).wait_recv()
                self.onward(flow, k).start()

    def wait(self, flow, k):
        self.onward(flow, k).wait_recv()

    def drain(self, flow, k):
        for side in range(2):
            self.copy(flow, k, side).wait_send()
        self.onward(flow, k).wait_send()


class RoundZ:
    def __init__(self, me, part, sems, stride):
        self.me, self.part, self.stride = me, part, stride
        self.zs, self.zr = sems[0], sems[1]
        self.over = OverX(me, part, me.at_x, me.x, sems[2:])

    def copy(self, flow, k, hop=1):
        ref = self.part(block_z(self.me, flow, k - hop), self.me.x)
        to = self.me.at_z(hop if flow == 0 else -hop)
        return remote(ref, ref, self.zs.at[flow, k], self.zr.at[flow, k], to)

    def begin(self):
        for hop in range(1, self.stride + 1):
            for flow in range(2):
                self.copy(flow, hop, hop).start()
        self.over.send(0, 0)

    def step(self, j):
        far = j * self.stride
        for flow in range(2):
            if inside(flow, far, 1):
                self.copy(flow, far, self.stride).wait_recv()

                for hop in range(1, self.stride + 1):
                    if far + hop <= last_of(flow):
                        self.copy(flow, far + hop, hop).start()

                self.over.send(flow, far)

        if self.stride == 2:
            for flow in range(2):
                if inside(flow, far - 1, 1):
                    self.copy(flow, far - 1, 1).wait_recv()
                    self.over.send(flow, far - 1)

    def steps_of(self, j):
        return [j * self.stride - i for i in range(self.stride)]

    def pass_on(self, j):
        for k in self.steps_of(j):
            self.over.pass_on(k)

    def wait(self, j):
        for k in self.steps_of(j):
            for flow in range(2):
                if inside(flow, k, 0):
                    self.over.wait(flow, k)

    def drain(self, j):
        for i, k in enumerate(self.steps_of(j)):
            for flow in range(2):
                if inside(flow, k, 1):
                    self.copy(flow, k, self.stride - i).wait_send()
                if inside(flow, k, 0):
                    self.over.drain(flow, k)


class BlocksRoundZ:
    def __init__(self, me, part, block, sems, stride):
        self.me, self.part, self.block, self.stride = me, part, block, stride
        self.xs, self.xr, self.zs, self.zr = sems

    def first(self, dx):
        ref = self.part(self.me.z, self.me.x)
        return remote(ref, ref, self.xs.at[dx], self.xr.at[dx], self.me.at_x(dx))

    def copy(self, flow, k, hop, piece):
        ref = self.block(block_z(self.me, flow, k - hop), piece)
        to = self.me.at_z(hop if flow == 0 else -hop)
        return remote(ref, ref, self.zs.at[flow, k, piece], self.zr.at[flow, k, piece], to)

    def begin(self):
        for dx in range(1, NX):
            self.first(dx).start()

    def launch(self):
        for dx in range(1, NX):
            self.first(dx).wait_recv()
        for piece in range(2):
            for hop in range(1, self.stride + 1):
                for flow in range(2):
                    self.copy(flow, hop, hop, piece).start()

    def step(self, j):
        far = j * self.stride
        for piece in range(2):
            for flow in range(2):
                end = 8 if flow == piece else 7
                if 1 <= far <= end:
                    self.copy(flow, far, self.stride, piece).wait_recv()

                    for hop in range(1, self.stride + 1):
                        if far + hop <= end:
                            self.copy(flow, far + hop, hop, piece).start()

        if self.stride == 2:
            for piece in range(2):
                for flow in range(2):
                    if 2 <= far <= 8:
                        self.copy(flow, far - 1, 1, piece).wait_recv()

    def drain(self, j):
        for i in range(self.stride):
            k = j * self.stride - i
            for piece in range(2):
                for flow in range(2):
                    if 1 <= k <= (8 if flow == piece else 7):
                        self.copy(flow, k, self.stride - i, piece).wait_send()

    def finish(self):
        for dx in range(1, NX):
            self.first(dx).wait_send()


DMA = pltpu.SemaphoreType.DMA
ROUND_SEMS = [DMA((2, 9)), DMA((2, 9)), DMA((2, 9, 2)), DMA((2, 9, 2)), DMA((2, 9)), DMA((2, 9))]
BLOCK_SEMS = [DMA((NX,)), DMA((NX,)), DMA((2, 9, 2)), DMA((2, 9, 2))]
OVER_SEMS = [DMA((2, 9, 2)), DMA((2, 9, 2)), DMA((2, 9)), DMA((2, 9))]

ROWS_XZ, ROWS_ZX, ROWS_ZXY = 16, 16, 32


def gather_all(me, w_ref, keep, ready, all_ref, gains_ref, gain_ref, ys, yr, gs, gr, ss, sr, *sems):
    early = ROWS_XZ + ROWS_ZX

    def ycopy(k):
        rows = pl.ds(0, early)
        dst = all_ref.at[me.c, me.y, me.z, me.x, rows]
        return remote(w_ref.at[rows], dst, ys.at[k], yr.at[k], me.at_y(k))

    def gcopy(k):
        part = gains_ref.at[me.c, me.y]
        return remote(part, part, gs.at[k], gr.at[k], me.at_y(k))

    for k in range(1, NY):
        ycopy(k).start()
    keep.wait()

    def late_part(z, x):
        return all_ref.at[me.c, me.y, z, x, pl.ds(early, ROWS_ZXY)]

    def late_column(z, y):
        return all_ref.at[me.c, y, z, :, pl.ds(early, ROWS_ZXY)]

    def mid_part(z, x):
        return all_ref.at[me.c, :, z, x, pl.ds(ROWS_XZ, ROWS_ZX)]

    def early_part(z, x):
        return all_ref.at[me.c, :, z, x, pl.ds(0, ROWS_XZ)]

    def early_block(z, piece):
        return all_ref.at[me.c, pl.ds(2 * piece, 2), z, :, pl.ds(0, ROWS_XZ)]

    late = RoundZ(me, late_part, sems[0:6], 2)
    mid = RoundZ(me, mid_part, sems[6:12], 1)
    blocks = BlocksRoundZ(me, early_part, early_block, sems[12:16], 1)
    over_y = OverX(me, late_column, me.at_y, me.y, sems[16:20])

    def side_copy(flow, k):
        part = all_ref.at[me.c, :, block_z(me, flow, k)]
        return remote(part, part, ss.at[flow, k], sr.at[flow, k], me.sibling())

    def both(k):
        return [flow for flow in range(2) if inside(flow, k, 0)]

    late.begin()
    for k in range(1, NY):
        ycopy(k).wait_recv()
    blocks.begin()
    mid.begin()
    ready()
    gains_ref[me.c, me.y] = gain_ref[...]
    for k in range(1, NY):
        gcopy(k).start()
    gains = remote(gains_ref.at[me.c], gains_ref.at[me.c], ss.at[2, 0], sr.at[2, 0], me.sibling())

    def drain(k):
        mid.drain(k)
        blocks.drain(k)
        for flow in both(k):
            over_y.drain(flow, k)

    passed = [max(0, min(9, (t - 2) * 9 // 7)) for t in range(12)]
    for t in range(1, 11):
        late.step(t)
        mid.step(t)
        late.pass_on(t - 1)
        mid.pass_on(t - 1)
        late.wait(t - 2)
        for k in late.steps_of(t - 2):
            for flow in both(k):
                over_y.send(flow, k)
        for k in range(passed[t - 1], passed[t]):
            over_y.pass_on(k)
        blocks.step(t - 1)
        if t == 1:
            blocks.launch()
        if t == 4:
            for k in range(1, NY):
                gcopy(k).wait_recv()
            gains.start()
        mid.wait(t - 2)
        for k in range(passed[max(t - 2, 0)], passed[t - 1]):
            for flow in both(k):
                over_y.wait(flow, k)
                side_copy(flow, k).start()
        if t >= 6:
            drain(t - 6)
            late.drain(t - 6)

    for k in range(9):
        for flow in both(k):
            side_copy(flow, k).wait_recv()
    gains.wait_recv()

    def settle():
        for k in range(5, 9):
            drain(k)
        for k in range(9):
            for flow in both(k):
                side_copy(flow, k).wait_send()
        blocks.finish()
        gains.wait_send()
        for k in range(1, NY):
            ycopy(k).wait_send()
            gcopy(k).wait_send()

    return settle


def normalize(values):
    centred = values - jnp.mean(values, axis=-1, keepdims=True)
    inv_spread = lax.rsqrt(jnp.mean(centred * centred, axis=-1, keepdims=True) + eps_norm)
    return (centred * inv_spread, inv_spread)


def contract_last(lhs_array, rhs_array):
    return lax.dot_general(
        lhs_array, rhs_array, (((1,), (1,)), ((), ())), preferred_element_type=f32
    )


def contract_first(lhs_array, rhs_array):
    return lax.dot_general(
        lhs_array, rhs_array, (((0,), (0,)), ((), ())), preferred_element_type=f32
    )


root_two_over_pi = 0.7978845608028654
cubic = 0.044715


def gelu_parts(v):
    t = jnp.tanh(root_two_over_pi * (v + cubic * (v * v * v)))
    cdf = 0.5 * (1.0 + t)
    slope = cdf + 0.5 * v * (1.0 - t * t) * (root_two_over_pi * (1.0 + 3.0 * cubic * v * v))
    return v * cdf, slope


OWN = ROWS // 2
SELF = 11
FAR = 7
CHUNK = 1024
CHUNKS = WIDTH // CHUNK
PIECES = 4
PIECE = WIDTH // PIECES


def tiled(a):
    return jnp.concatenate([a] * (CHUNK // 128), axis=1)


def folded(a):
    total = a[:, 0:128]
    for i in range(1, a.shape[1] // 128):
        total = total + a[:, i * 128 : (i + 1) * 128]
    return total


def row_mean(a):
    return jnp.broadcast_to(jnp.sum(a, axis=-1, keepdims=True) * (1.0 / WIDTH), (OWN, 128))


def relay(
    me, w, gains_ref, valid_ref, grad_ref, probe_ref,
    x, g, cb, inv, pre, hid, wsum, out, pg, cb_in, hid_in, out_in, pg_in, pr, pr_in,
    fs, fr, bs, br,
):
    mine = me.s
    sib = me.y * 2 + 1 - me.c

    def span(j):
        return slice(j * (CHUNK // 256), (j + 1) * (CHUNK // 256))

    def weight(s, j, half):
        cols = slice(half * HID, (half + 1) * HID)
        return w[lax.rem(s, 2), s // 2, span(j), :, :, cols].reshape(CHUNK, HID)

    def send_cb():
        return remote(cb.at[sib], cb_in, fs.at[0], fr.at[0], me.sibling())

    def send_hid():
        return remote(hid.at[sib], hid_in, fs.at[1], fr.at[1], me.sibling())

    def send_pr():
        return remote(pr, pr_in, fs.at[2], fr.at[2], me.sibling())

    def send_out(p):
        cols = pl.ds(p * PIECE, PIECE)
        return remote(out.at[1 - me.c, :, cols], out_in.at[:, cols], bs.at[p], br.at[p], me.sibling())

    def send_pg():
        return remote(pg.at[1 - me.c], pg_in, bs.at[PIECES], br.at[PIECES], me.sibling())

    def gain_of(s):
        return gains_ref[lax.rem(s, 2), s // 2, 0:1, :]

    def cols_of(j):
        return slice(j * CHUNK, (j + 1) * CHUNK)

    def picked(ref):
        for j in range(CHUNKS):
            cols = cols_of(j)
            rows = jnp.zeros((TOK, CHUNK), f32)
            for i in range(OWN // TOK):
                part = pl.ds(i * TOK, TOK)
                chosen = valid_ref[1, pl.ds(pl.multiple_of(me.c * OWN + i * TOK, TOK), TOK), :]
                rows = rows + tiled(chosen) * x[part, cols].astype(f32)
            ref[:, cols] = rows.astype(bf16)

    total = jnp.zeros((OWN, 128), f32)
    for j in range(CHUNKS):
        total = total + folded(x[:, cols_of(j)].astype(f32))

    def forward(s, total):
        @pl.when(s == mine)
        def _():
            picked(probe_ref)

        @pl.when(s == sib)
        def _():
            picked(pr)
            send_pr().start()

        mean = tiled(row_mean(total))
        squares = jnp.zeros((OWN, 128), f32)
        acc = jnp.zeros((OWN + 16, HID), f32)
        ones = jnp.ones((16, CHUNK), bf16)
        for j in range(CHUNKS):
            cols = cols_of(j)
            centred = x[:, cols].astype(f32) - mean
            squares = squares + folded(centred * centred)
            low = centred.astype(bf16)
            cb[s, :, cols] = low
            part = weight(s, j, 0)
            acc = acc + jnp.dot(jnp.concatenate([low, ones], axis=0), part, preferred_element_type=f32)
        wsum[s] = acc[OWN : OWN + 8]
        acc = acc[:OWN]
        spread = lax.rsqrt(row_mean(squares) + eps_norm)
        inv[s] = spread
        pre_act = acc * spread
        pre[s] = pre_act
        hidden = gelu_parts(pre_act)[0].astype(bf16)
        hid[s] = hidden

        @pl.when(s == sib)
        def _():
            send_cb().start()
            send_hid().start()

        gain = tiled(gain_of(s))
        total = jnp.zeros((OWN, 128), f32)
        for j in range(CHUNKS):
            cols = cols_of(j)
            branch = contract_last(hidden, weight(s, j, 1))
            low = (x[:, cols].astype(f32) + gain * branch).astype(bf16)
            x[:, cols] = low
            total = total + folded(low.astype(f32))
        return total

    lax.fori_loop(0, SECTIONS, forward, total)

    keep = tiled(valid_ref[0, pl.ds(pl.multiple_of(me.c * OWN, OWN), OWN), :]) > 0.5
    last = SECTIONS - 1
    gain = tiled(gain_of(last))
    hidden_grad = jnp.zeros((OWN, HID), f32)
    for j in range(CHUNKS):
        cols = cols_of(j)
        low = jnp.where(keep, x[:, cols].astype(f32), 0.0).astype(bf16)
        g[:, cols] = low
        scaled = (gain * low.astype(f32)).astype(bf16)
        out[1, :, cols] = scaled
        hidden_grad = hidden_grad + jnp.dot(scaled, weight(last, j, 1), preferred_element_type=f32)

    @pl.when(sib == last)
    def _():
        for p in range(PIECES):
            send_out(p).start()

    def inner(s, hidden_grad):
        pre_act = pre[s]
        scaled = (inv[s] * (gelu_parts(pre_act)[1] * hidden_grad)).astype(bf16)
        pg[lax.rem(s, 2)] = scaled

        @pl.when(s == sib)
        def _():
            send_pg().start()

        return scaled, pre_act

    def backward(i, hidden_grad):
        s = last - i
        scaled_pre, pre_act = inner(s, hidden_grad)
        pre_f = scaled_pre.astype(f32)
        shift = tiled(row_mean(pre_f * wsum[s, 0:1]))
        slope = tiled(row_mean(pre_f * pre_act) * inv[s])
        gain = tiled(gain_of(s - 1))
        slot = lax.rem(s + 1, 2)
        hidden_grad = jnp.zeros((OWN, HID), f32)
        for j in range(CHUNKS):
            cols = cols_of(j)
            normed_grad = contract_last(scaled_pre, weight(s, j, 0))
            low = (
                g[:, cols].astype(f32) + (normed_grad - shift - cb[s, :, cols].astype(f32) * slope)
            ).astype(bf16)
            g[:, cols] = low
            scaled = (gain * low.astype(f32)).astype(bf16)
            out[slot, :, cols] = scaled
            hidden_grad = hidden_grad + jnp.dot(scaled, weight(s - 1, j, 1), preferred_element_type=f32)
            if (j + 1) * CHUNK % PIECE == 0:

                @pl.when(s - 1 == sib)
                def _():
                    send_out((j + 1) * CHUNK // PIECE - 1).start()

        return hidden_grad

    hidden_grad = lax.fori_loop(0, last - me.y * 2, backward, hidden_grad)
    inner(me.y * 2, hidden_grad)

    send_pr().wait()
    probe_ref[...] = (probe_ref[...].astype(f32) + pr_in[...].astype(f32)).astype(bf16)
    send_cb().wait()
    send_hid().wait()
    send_pg().wait()
    for p in range(PIECES):
        send_out(p).wait()
    def store(j, half, columns):
        rows = columns.astype(bf16).T.reshape(CHUNK // 256, NX, SHARD, HID)
        for i in range(CHUNK // 256):
            slot = lax.rem(j * (CHUNK // 256) + i - me.z + SELF + NZ, NZ)
            grad_ref[slot, :, :, pl.ds(half * HID, HID)] = rows[i]

    pg_a, pg_b, hid_a, hid_b = pg[me.c], pg_in[...], hid[mine], hid_in[...]
    for j in range(CHUNKS):
        cols = cols_of(j)
        first = contract_first(pg_a, cb[mine, :, cols]) + contract_first(pg_b, cb_in[:, cols])
        store(j, 0, first)
        second = contract_first(hid_a, out[me.c, :, cols]) + contract_first(hid_b, out_in[:, cols])
        store(j, 1, second)


ROWS_Z, ROWS_X = 32, 32
FRESH_XZ, FRESH_ZX = 16, 48
GROUP = SECTIONS * NX


class SumRoundZ:
    def __init__(self, me, own, held, sems, index):
        self.me, self.own, self.held, self.index = me, own, held, index
        self.zs, self.zr = sems

    def slot(self, flow, k):
        return (SELF + k if flow == 0 else SELF - k) % NZ

    def copy(self, flow, k):
        first = k % 2 == 1 or k == 8
        hop = 1 if k % 2 else 2
        to = self.me.at_z(hop if flow == 0 else -hop)
        src = self.own(self.slot(flow, k)) if first else self.held(flow, k + 2 if k < 6 or flow == 0 else 7)
        return remote(src, self.held(flow, k), self.zs.at[flow, k, self.index], self.zr.at[flow, k, self.index], to)

    def begin(self, *distances):
        for k in distances:
            for flow in range(2):
                if k <= last_of(flow):
                    self.copy(flow, k).start()

    def step(self, k):
        for flow in range(2):
            into = k + 2 if k < 6 or flow == 0 else 7
            for i in ((7, 8) if k == 6 else (k + 1, k + 2)):
                if i <= last_of(flow):
                    self.copy(flow, i).wait_recv()
            own = self.own(self.slot(flow, k))
            total = own[...].astype(f32) + self.held(flow, into)[...].astype(f32)
            if into != k + 1:
                total = total + self.held(flow, k + 1)[...].astype(f32)
            self.held(flow, into)[...] = total.astype(bf16)
            self.copy(flow, k).start()

    def wait(self):
        for flow in range(2):
            for k in (1, 2):
                self.copy(flow, k).wait_recv()

    def result(self):
        total = self.own(SELF)[...].astype(f32)
        for flow in range(2):
            for k in (1, 2):
                total = total + self.held(flow, k)[...].astype(f32)
        return total

    def drain(self):
        for flow in range(2):
            for k in range(1, last_of(flow) + 1):
                self.copy(flow, k).wait_send()


def finish(
    me, settle, put, grad_ref, master_ref, first_ref, second_ref, gain_ref, probe_ref,
    out_ref, new_master_ref, new_first_ref, new_second_ref,
    fresh, ra, rb, xa, xa_out, xb, tb, share, near, far,
    zs, zr, xs, xr, ns, nr, ms, mr, *sems,
):
    def group_at(i):
        ds, dx = i // NX, i % NX
        return (lax.rem(me.s + ds, SECTIONS), me.z * NX + lax.rem(me.x + dx, NX))

    def xbcopy(dx, part):
        span = slice(0, FAR) if part == 0 else slice(FAR, NZ)
        src = grad_ref.at[span, lax.rem(me.x + dx, NX), pl.ds(ROWS_Z, ROWS_X), :]
        sem = (1 + part, dx)
        return remote(src, xb.at[dx, span], xs.at[sem], xr.at[sem], me.at_x(dx))

    def xacopy(dx):
        src = xa_out.at[lax.rem(me.x + dx, NX)]
        return remote(src, xa.at[dx], xs.at[0, dx], xr.at[0, dx], me.at_x(dx))

    def piece_sum(piece):
        pair = pl.ds(2 * piece, 2)
        return SumRoundZ(
            me,
            lambda z: grad_ref.at[z, pair, pl.ds(0, ROWS_Z), :],
            lambda flow, k: ra.at[flow, k, pair],
            (zs, zr),
            piece,
        )

    pieces = [piece_sum(0), piece_sum(1)]
    late = SumRoundZ(me, lambda z: tb.at[z], lambda flow, k: rb.at[flow, k], (zs, zr), 2)
    def add(part):
        for dx in range(1, NX):
            xbcopy(dx, part).wait_recv()
        for z in range(FAR) if part == 0 else range(FAR, NZ):
            total = grad_ref[z, me.x, pl.ds(ROWS_Z, ROWS_X), :].astype(f32)
            for dx in range(1, NX):
                total = total + xb[dx, z].astype(f32)
            tb[z] = total.astype(bf16)

    for piece in pieces:
        piece.begin(8, 7)
    for part in range(2):
        for dx in range(1, NX):
            xbcopy(dx, part).start()
        if part == 0:
            for piece in pieces:
                piece.begin(5)
    settle()
    for piece in pieces:
        piece.step(6)
    for piece in pieces:
        piece.begin(3)
    add(0)
    late.begin(8, 7, 5)
    for piece in pieces:
        piece.step(4)
    for piece in pieces:
        piece.begin(1)
    late.step(6)
    add(1)
    late.begin(3, 1)
    for piece in pieces:
        piece.step(2)
    late.step(4)
    for i, piece in enumerate(pieces):
        piece.wait()
        xa_out[pl.ds(2 * i, 2)] = piece.result().astype(bf16)
    for dx in range(1, NX):
        xacopy(dx).start()
    late.step(2)
    for dx in range(1, NX):
        xacopy(dx).wait_recv()
    total = xa_out[me.x].astype(f32)
    for dx in range(1, NX):
        total = total + xa[dx].astype(f32)
    share[pl.ds(0, ROWS_Z), :] = total
    late.wait()
    share[pl.ds(ROWS_Z, ROWS_X), :] = late.result()

    squares = jnp.zeros((8, 128), f32)
    for i in range(SHARD // 8):
        for j in range(2):
            tile = share[pl.ds(i * 8, 8), pl.ds(j * 128, 128)]
            squares = squares + tile * tile
    near[0] = squares

    def ncopy(i):
        return remote(near.at[0], near.at[i], ns.at[i], nr.at[i], group_at(i))

    def mcopy(k):
        return remote(far.at[0], far.at[k], ms.at[k], mr.at[k], me.at_z(k))

    def n_wait(i, carry):
        ncopy(i).wait_recv()
        return carry

    def n_sent(i, carry):
        ncopy(i).wait_send()
        return carry

    def m_sent(i, carry):
        mcopy(i).wait_send()
        return carry

    def m_wait(i, carry):
        mcopy(i).wait_recv()
        return carry

    for i in range(1, GROUP):
        ncopy(i).start()
    lax.fori_loop(1, GROUP, n_wait, 0)
    far[0] = jnp.sum(near[...], axis=0)
    for k in (8, 7, 9, 6, 10, 5, 11, 4, 12, 3, 13, 2, 14, 1, 15):
        mcopy(k).start()
    lax.fori_loop(1, NZ, m_wait, 0)
    norm_sq = jnp.sum(jnp.sum(far[...], axis=0), keepdims=True)

    clip_factor = 1.0 / jnp.maximum(jnp.sqrt(norm_sq), 1.0)
    clipped = share[...] * clip_factor
    master_now = master_ref[...]
    new_first = beta_one * first_ref[...] + (1.0 - beta_one) * clipped
    new_second = beta_two * second_ref[...] + (1.0 - beta_two) * clipped * clipped
    new_master = master_now - learn_rate * (
        new_first / (jnp.sqrt(new_second) + eps_adam) + decay_rate * master_now
    )
    fresh[me.z, me.x] = new_master.astype(bf16)
    new_master_ref[...] = new_master
    new_first_ref[...] = new_first
    new_second_ref[...] = new_second

    def early_part(z, x):
        return fresh.at[z, x, pl.ds(0, FRESH_XZ)]

    def early_block(z, piece):
        return fresh.at[z, pl.ds(2 * piece, 2), pl.ds(0, FRESH_XZ)]

    def mid_part(z, x):
        return fresh.at[z, x, pl.ds(FRESH_XZ, FRESH_ZX)]

    mid = RoundZ(me, mid_part, sems[0:6], 2)
    blocks = BlocksRoundZ(me, early_part, early_block, sems[6:10], 2)
    blocks.begin()
    mid.begin()
    for copy in put:
        copy.start()
    for piece in pieces:
        piece.drain()
    late.drain()
    for dx in range(1, NX):
        xbcopy(dx, 0).wait_send()
        xbcopy(dx, 1).wait_send()
        xacopy(dx).wait_send()
    blocks.launch()
    lax.fori_loop(1, GROUP, n_sent, 0)
    lax.fori_loop(1, NZ, m_sent, 0)

    for t in range(1, 7):
        mid.step(t)
        blocks.step(t)
        mid.pass_on(t - 1)
        mid.wait(t - 2)
        if t >= 3:
            mid.drain(t - 3)
            blocks.drain(t - 3)

    values = probe_ref[...].astype(f32)
    normed = normalize(values)[0].astype(bf16)
    pre_act = jnp.zeros((TOK, HID), f32)
    for z in range(NZ):
        part = fresh[z, :, :, :HID].reshape(256, HID)
        pre_act = pre_act + jnp.dot(normed[:, z * 256 : (z + 1) * 256], part, preferred_element_type=f32)
    hidden = gelu_parts(pre_act)[0].astype(bf16)
    gain = gain_ref[0:1, 0:1]
    for z in range(NZ):
        part = fresh[z, :, :, HID:].reshape(256, HID)
        cols = slice(z * 256, (z + 1) * 256)
        out_ref[:, cols] = (values[:, cols] + gain * contract_last(hidden, part)).astype(bf16)
    mid.drain(4)
    blocks.drain(4)
    blocks.finish()


def partners(me):
    ys = [me.at_y(k) for k in range(1, NY)]
    xs = [me.at_x(k) for k in range(1, NX)]
    return ys + xs + [me.at_z(k) for k in (1, 2, -1, -2)] + [me.sibling()]


N_GATHER, N_RELAY = 26, 4


def step_kernel(
    w_ref, depth_hbm, counts_hbm, plan_hbm, x_hbm, master_hbm, first_hbm, second_hbm,
    out_ref, new_master_hbm, new_first_hbm, new_second_hbm,
    w, gains, grad, probe, gain_ref, marks_ref, master_ref, first_ref, second_ref,
    depth_ref, counts_ref, plan_ref, new_master_ref, new_first_ref, new_second_ref,
    x, g, cb, inv, pre, hid, wsum, out, pg, cb_in, hid_in, out_in, pg_in, pr, pr_in,
    fresh, ra, rb, xa, xa_out, xb, tb, share, near, far,
    x_sem, *sems,
):
    me = Place()
    get_x = pltpu.make_async_copy(
        x_hbm.at[pl.ds(pl.multiple_of(me.c * OWN, OWN), OWN)], x, x_sem.at[0]
    )
    state = [
        pltpu.make_async_copy(src, dst, x_sem.at[i + 1])
        for i, (src, dst) in enumerate(
            (
                (depth_hbm, depth_ref),
                (counts_hbm, counts_ref),
                (plan_hbm, plan_ref),
                (master_hbm, master_ref),
                (first_hbm, first_ref),
                (second_hbm, second_ref),
            )
        )
    ]
    keep = pltpu.make_async_copy(w_ref, w.at[me.c, me.y, me.z, me.x], x_sem.at[7])
    keep.start()
    for get in state[:3]:
        get.start()
    get_x.start()
    for get in state[3:]:
        get.start()
    greet(partners(me))

    def ready():
        for get in state[:3]:
            get.wait()
        gain_ref[...] = jnp.broadcast_to(lax.rsqrt(1.0 + depth_ref[...].astype(f32) / 8.0), (8, 128))
        place_in_block = lax.broadcasted_iota(jnp.int32, (TOK, 128), 0)
        for m in range(ROWS // TOK):
            rows = pl.ds(m * TOK, TOK)
            marks_ref[0, rows, :] = (place_in_block < counts_ref[0:1, m : m + 1]).astype(f32)
            planned = jnp.broadcast_to((plan_ref[0:1, 15:16] == m).astype(f32), (TOK, 128))
            marks_ref[1, rows, :] = planned

    settle = gather_all(me, w_ref, keep, ready, w, gains, gain_ref, *sems[:N_GATHER])
    get_x.wait()
    for get in state[3:]:
        get.wait()
    relay(
        me, w, gains, marks_ref, grad, probe,
        x, g, cb, inv, pre, hid, wsum, out, pg, cb_in, hid_in, out_in, pg_in, pr, pr_in,
        *sems[N_GATHER : N_GATHER + N_RELAY],
    )
    put = [
        pltpu.make_async_copy(src, dst, x_sem.at[i])
        for i, (src, dst) in enumerate(
            (
                (new_master_ref, new_master_hbm),
                (new_first_ref, new_first_hbm),
                (new_second_ref, new_second_hbm),
            )
        )
    ]
    finish(
        me, settle, put, grad, master_ref, first_ref, second_ref, gain_ref, probe,
        out_ref, new_master_ref, new_first_ref, new_second_ref,
        fresh, ra, rb, xa, xa_out, xb, tb, share, near, far,
        *sems[N_GATHER + N_RELAY :],
    )
    for copy in put:
        copy.wait()


def hand_out_kernel(*refs):
    for i in range(4):
        refs[4 + i][...] = refs[i][...]


def shards(inputs, stashed, master, first_moment, second_moment, counts, plan, layer_index):
    state = jax.ShapeDtypeStruct((SHARD, 2 * HID), f32)
    vmem = pl.BlockSpec(memory_space=pltpu.VMEM)
    anywhere = pl.BlockSpec(memory_space=pl.ANY)
    chunks = (NZ, NX, SHARD, 2 * HID)
    probe_out, new_master, new_first, new_second = pl.pallas_call(
        step_kernel,
        out_shape=(jax.ShapeDtypeStruct((TOK, WIDTH), bf16), state, state, state),
        in_specs=[anywhere] * 8,
        out_specs=(vmem, anywhere, anywhere, anywhere),
        scratch_shapes=[
            pltpu.VMEM((2, NY, *chunks), bf16),
            pltpu.VMEM((2, NY, 8, 128), f32),
            pltpu.VMEM(chunks, bf16),
            pltpu.VMEM((TOK, WIDTH), bf16),
            pltpu.VMEM((8, 128), f32),
            pltpu.VMEM((2, ROWS, 128), f32),
            *[pltpu.VMEM((SHARD, 2 * HID), f32)] * 3,
            pltpu.VMEM((1, 1), jnp.int32),
            *[pltpu.VMEM((1, ROWS // TOK), jnp.int32)] * 2,
            *[pltpu.VMEM((SHARD, 2 * HID), f32)] * 3,
            pltpu.VMEM((OWN, WIDTH), bf16),
            pltpu.VMEM((OWN, WIDTH), bf16),
            pltpu.VMEM((SECTIONS, OWN, WIDTH), bf16),
            pltpu.VMEM((SECTIONS, OWN, 128), f32),
            pltpu.VMEM((SECTIONS, OWN, HID), f32),
            pltpu.VMEM((SECTIONS, OWN, HID), bf16),
            pltpu.VMEM((SECTIONS, 8, HID), f32),
            pltpu.VMEM((2, OWN, WIDTH), bf16),
            pltpu.VMEM((2, OWN, HID), bf16),
            pltpu.VMEM((OWN, WIDTH), bf16),
            pltpu.VMEM((OWN, HID), bf16),
            pltpu.VMEM((OWN, WIDTH), bf16),
            pltpu.VMEM((OWN, HID), bf16),
            pltpu.VMEM((TOK, WIDTH), bf16),
            pltpu.VMEM((TOK, WIDTH), bf16),
            pltpu.VMEM(chunks, bf16),
            pltpu.VMEM((2, 9, NX, ROWS_Z, 2 * HID), bf16),
            pltpu.VMEM((2, 9, ROWS_X, 2 * HID), bf16),
            pltpu.VMEM((NX, ROWS_Z, 2 * HID), bf16),
            pltpu.VMEM((NX, ROWS_Z, 2 * HID), bf16),
            pltpu.VMEM((NX, NZ, ROWS_X, 2 * HID), bf16),
            pltpu.VMEM((NZ, ROWS_X, 2 * HID), bf16),
            pltpu.VMEM((SHARD, 2 * HID), f32),
            pltpu.VMEM((GROUP, 8, 128), f32),
            pltpu.VMEM((NZ, 8, 128), f32),
            DMA((8,)),
            *[DMA((NY,))] * 4,
            *[DMA((3, 9))] * 2,
            *ROUND_SEMS,
            *ROUND_SEMS,
            *BLOCK_SEMS,
            *OVER_SEMS,
            *[DMA((3,))] * 2,
            *[DMA((PIECES + 1,))] * 2,
            *[DMA((2, 9, 3))] * 2,
            *[DMA((3, NX))] * 2,
            *[DMA((GROUP,))] * 2,
            *[DMA((NZ,))] * 2,
            *ROUND_SEMS,
            *BLOCK_SEMS,
        ],
        compiler_params=pltpu.CompilerParams(
            collective_id=0, has_side_effects=True, vmem_limit_bytes=60 * 2**20
        ),
        name="optimizer_step",
    )(
        stashed[0], layer_index.reshape(1, 1), counts, plan.reshape(1, 16),
        inputs.reshape(ROWS, WIDTH), master[0], first_moment[0], second_moment[0],
    )
    results = (probe_out[None], new_master[None], new_first[None], new_second[None])
    return pl.pallas_call(
        hand_out_kernel,
        out_shape=tuple(jax.ShapeDtypeStruct(r.shape, r.dtype) for r in results),
        in_specs=[vmem] * 4,
        out_specs=(vmem,) * 4,
        compiler_params=pltpu.CompilerParams(vmem_limit_bytes=60 * 2**20),
        name="hand_out",
    )(*results)


def solution(mesh):
    in_specs = (
        P(None, "dp", None),
        P("section", "dp", None),
        P("section", "dp", None),
        P("section", "dp", None),
        P("section", "dp", None),
        P("dp", None),
        P(),
        P("section"),
    )
    out_specs = (
        P("section", "dp", None),
        P("section", "dp", None),
        P("section", "dp", None),
        P("section", "dp", None),
    )
    return jax.shard_map(shards, mesh=mesh, in_specs=in_specs, out_specs=out_specs, check_vma=False)
```

```python
import functools

import jax
import jax.numpy as jnp
from jax import lax
from jax.experimental import pallas as pl
from jax.experimental.pallas import tpu as pltpu
from jax.sharding import PartitionSpec as P

eps_norm = 1e-05
beta_one = 0.9
beta_two = 0.95
eps_adam = 1e-08
learn_rate = 0.002
decay_rate = 0.1

MESH = pl.DeviceIdType.MESH
WIDTH = 4096
HID = 128
ROWS = 256
TOK = 16
SECTIONS = 8
SHARD = 64
NZ = 16
NX = 4
NY = 4
f32 = jnp.float32
bf16 = jnp.bfloat16


class Place:

    def __init__(self):
        self.s = lax.axis_index("section")
        self.d = lax.axis_index("dp")
        self.c = lax.rem(self.s, 2)
        self.y = self.s // 2
        self.z = self.d // NX
        self.x = lax.rem(self.d, NX)

    def at_z(self, k):
        return (self.s, lax.rem(self.z + k + 2 * NZ, NZ) * NX + self.x)

    def at_x(self, k):
        return (self.s, self.z * NX + lax.rem(self.x + k + NX, NX))

    def at_y(self, k):
        return (lax.rem(self.y + k + NY, NY) * 2 + self.c, self.d)

    def sibling(self):
        return (self.y * 2 + 1 - self.c, self.d)


def greet(partners):
    barrier = pltpu.get_barrier_semaphore()
    for partner in partners:
        pl.semaphore_signal(barrier, inc=1, device_id=partner, device_id_type=MESH)
    pl.semaphore_wait(barrier, len(partners))


def remote(src, dst, send, recv, to):
    return pltpu.make_async_remote_copy(
        src_ref=src, dst_ref=dst, send_sem=send, recv_sem=recv, device_id=to, device_id_type=MESH
    )


def block_z(me, flow, k):
    if flow == 0:
        return lax.rem(me.z - k + 2 * NZ, NZ)
    return lax.rem(me.z + k, NZ)


def last_of(flow):
    return 8 if flow == 0 else 7


def inside(flow, k, lowest):
    return max(flow, lowest) <= k <= last_of(flow)


class OverX:
    def __init__(self, me, part, at, here, sems):
        self.me, self.part, self.at, self.here = me, part, at, here
        self.ss, self.sr, self.fs, self.fr = sems

    def copy(self, flow, k, side):
        ref = self.part(block_z(self.me, flow, k), self.here)
        to = self.at(1 if side == 0 else -1)
        return remote(ref, ref, self.ss.at[flow, k, side], self.sr.at[flow, k, side], to)

    def onward(self, flow, k):
        came = -1 if flow == 0 else 1
        ref = self.part(block_z(self.me, flow, k), lax.rem(self.here + came + 4, 4))
        return remote(ref, ref, self.fs.at[flow, k], self.fr.at[flow, k], self.at(-came))

    def send(self, flow, k):
        for side in range(2):
            self.copy(flow, k, side).start()

    def pass_on(self, k):
        for flow in range(2):
            if inside(flow, k, 0):
                for side in range(2):
                    self.copy(flow, k, side).wait_recv()
                self.onward(flow, k).start()

    def wait(self, flow, k):
        self.onward(flow, k).wait_recv()

    def drain(self, flow, k):
        for side in range(2):
            self.copy(flow, k, side).wait_send()
        self.onward(flow, k).wait_send()


class RoundZ:
    def __init__(self, me, part, sems, stride):
        self.me, self.part, self.stride = me, part, stride
        self.zs, self.zr = sems[0], sems[1]
        self.over = OverX(me, part, me.at_x, me.x, sems[2:])

    def copy(self, flow, k, hop=1):
        ref = self.part(block_z(self.me, flow, k - hop), self.me.x)
        to = self.me.at_z(hop if flow == 0 else -hop)
        return remote(ref, ref, self.zs.at[flow, k], self.zr.at[flow, k], to)

    def begin(self):
        for hop in range(1, self.stride + 1):
            for flow in range(2):
                self.copy(flow, hop, hop).start()
        self.over.send(0, 0)

    def step(self, j):
        far = j * self.stride
        for flow in range(2):
            if inside(flow, far, 1):
                self.copy(flow, far, self.stride).wait_recv()

                for hop in range(1, self.stride + 1):
                    if far + hop <= last_of(flow):
                        self.copy(flow, far + hop, hop).start()

                self.over.send(flow, far)

        if self.stride == 2:
            for flow in range(2):
                if inside(flow, far - 1, 1):
                    self.copy(flow, far - 1, 1).wait_recv()
                    self.over.send(flow, far - 1)

    def steps_of(self, j):
        return [j * self.stride - i for i in range(self.stride)]

    def pass_on(self, j):
        for k in self.steps_of(j):
            self.over.pass_on(k)

    def wait(self, j):
        for k in self.steps_of(j):
            for flow in range(2):
                if inside(flow, k, 0):
                    self.over.wait(flow, k)

    def drain(self, j):
        for i, k in enumerate(self.steps_of(j)):
            for flow in range(2):
                if inside(flow, k, 1):
                    self.copy(flow, k, self.stride - i).wait_send()
                if inside(flow, k, 0):
                    self.over.drain(flow, k)


class BlocksRoundZ:
    def __init__(self, me, part, block, sems, stride):
        self.me, self.part, self.block, self.stride = me, part, block, stride
        self.xs, self.xr, self.zs, self.zr = sems

    def first(self, dx):
        ref = self.part(self.me.z, self.me.x)
        return remote(ref, ref, self.xs.at[dx], self.xr.at[dx], self.me.at_x(dx))

    def copy(self, flow, k, hop, piece):
        ref = self.block(block_z(self.me, flow, k - hop), piece)
        to = self.me.at_z(hop if flow == 0 else -hop)
        return remote(ref, ref, self.zs.at[flow, k, piece], self.zr.at[flow, k, piece], to)

    def begin(self):
        for dx in range(1, NX):
            self.first(dx).start()

    def launch(self):
        for dx in range(1, NX):
            self.first(dx).wait_recv()
        for piece in range(2):
            for hop in range(1, self.stride + 1):
                for flow in range(2):
                    self.copy(flow, hop, hop, piece).start()

    def step(self, j):
        far = j * self.stride
        for piece in range(2):
            for flow in range(2):
                end = 8 if flow == piece else 7
                if 1 <= far <= end:
                    self.copy(flow, far, self.stride, piece).wait_recv()

                    for hop in range(1, self.stride + 1):
                        if far + hop <= end:
                            self.copy(flow, far + hop, hop, piece).start()

        if self.stride == 2:
            for piece in range(2):
                for flow in range(2):
                    if 2 <= far <= 8:
                        self.copy(flow, far - 1, 1, piece).wait_recv()

    def drain(self, j):
        for i in range(self.stride):
            k = j * self.stride - i
            for piece in range(2):
                for flow in range(2):
                    if 1 <= k <= (8 if flow == piece else 7):
                        self.copy(flow, k, self.stride - i, piece).wait_send()

    def finish(self):
        for dx in range(1, NX):
            self.first(dx).wait_send()


DMA = pltpu.SemaphoreType.DMA
ROUND_SEMS = [DMA((2, 9)), DMA((2, 9)), DMA((2, 9, 2)), DMA((2, 9, 2)), DMA((2, 9)), DMA((2, 9))]
BLOCK_SEMS = [DMA((NX,)), DMA((NX,)), DMA((2, 9, 2)), DMA((2, 9, 2))]
OVER_SEMS = [DMA((2, 9, 2)), DMA((2, 9, 2)), DMA((2, 9)), DMA((2, 9))]

ROWS_XZ, ROWS_ZX, ROWS_ZXY = 16, 16, 32


def gather_all(me, w_ref, keep, ready, all_ref, gains_ref, gain_ref, ys, yr, gs, gr, ss, sr, *sems):
    early = ROWS_XZ + ROWS_ZX

    def ycopy(k):
        rows = pl.ds(0, early)
        dst = all_ref.at[me.c, me.y, me.z, me.x, rows]
        return remote(w_ref.at[rows], dst, ys.at[k], yr.at[k], me.at_y(k))

    def gcopy(k):
        part = gains_ref.at[me.c, me.y]
        return remote(part, part, gs.at[k], gr.at[k], me.at_y(k))

    for k in range(1, NY):
        ycopy(k).start()
    keep.wait()

    def late_part(z, x):
        return all_ref.at[me.c, me.y, z, x, pl.ds(early, ROWS_ZXY)]

    def late_column(z, y):
        return all_ref.at[me.c, y, z, :, pl.ds(early, ROWS_ZXY)]

    def mid_part(z, x):
        return all_ref.at[me.c, :, z, x, pl.ds(ROWS_XZ, ROWS_ZX)]

    def early_part(z, x):
        return all_ref.at[me.c, :, z, x, pl.ds(0, ROWS_XZ)]

    def early_block(z, piece):
        return all_ref.at[me.c, pl.ds(2 * piece, 2), z, :, pl.ds(0, ROWS_XZ)]

    late = RoundZ(me, late_part, sems[0:6], 1)
    mid = RoundZ(me, mid_part, sems[6:12], 1)
    blocks = BlocksRoundZ(me, early_part, early_block, sems[12:16], 1)
    over_y = OverX(me, late_column, me.at_y, me.y, sems[16:20])

    def side_copy(flow, k):
        part = all_ref.at[me.c, :, block_z(me, flow, k)]
        return remote(part, part, ss.at[flow, k], sr.at[flow, k], me.sibling())

    def both(k):
        return [flow for flow in range(2) if inside(flow, k, 0)]

    late.begin()
    for k in range(1, NY):
        ycopy(k).wait_recv()
    blocks.begin()
    mid.begin()
    ready()
    gains_ref[me.c, me.y] = gain_ref[...]
    for k in range(1, NY):
        gcopy(k).start()
    gains = remote(gains_ref.at[me.c], gains_ref.at[me.c], ss.at[2, 0], sr.at[2, 0], me.sibling())

    def drain(k):
        mid.drain(k)
        blocks.drain(k)
        for flow in both(k):
            over_y.drain(flow, k)

    for t in range(1, 13):
        late.step(t)
        mid.step(t - 1)
        late.pass_on(t - 1)
        mid.pass_on(t - 2)
        late.wait(t - 2)
        for flow in both(t - 2):
            over_y.send(flow, t - 2)
        mid.wait(t - 3)
        over_y.pass_on(t - 3)
        if t == 2:
            blocks.launch()
        blocks.step(t - 2)
        if t == 4:
            for k in range(1, NY):
                gcopy(k).wait_recv()
            gains.start()
        for flow in both(t - 4):
            over_y.wait(flow, t - 4)
            side_copy(flow, t - 4).start()
        if t >= 6:
            drain(t - 6)
            late.drain(t - 6)

    for k in range(9):
        for flow in both(k):
            side_copy(flow, k).wait_recv()
    gains.wait_recv()

    def settle():
        for k in range(7, 9):
            drain(k)
            late.drain(k)
        for k in range(9):
            for flow in both(k):
                side_copy(flow, k).wait_send()
        blocks.finish()
        gains.wait_send()
        for k in range(1, NY):
            ycopy(k).wait_send()
            gcopy(k).wait_send()

    return settle


def normalize(values):
    centred = values - jnp.mean(values, axis=-1, keepdims=True)
    inv_spread = lax.rsqrt(jnp.mean(centred * centred, axis=-1, keepdims=True) + eps_norm)
    return (centred * inv_spread, inv_spread)


def contract_last(lhs_array, rhs_array):
    return lax.dot_general(
        lhs_array, rhs_array, (((1,), (1,)), ((), ())), preferred_element_type=f32
    )


def contract_first(lhs_array, rhs_array):
    return lax.dot_general(
        lhs_array, rhs_array, (((0,), (0,)), ((), ())), preferred_element_type=f32
    )


root_two_over_pi = 0.7978845608028654
cubic = 0.044715


def gelu_parts(v):
    t = jnp.tanh(root_two_over_pi * (v + cubic * (v * v * v)))
    cdf = 0.5 * (1.0 + t)
    slope = cdf + 0.5 * v * (1.0 - t * t) * (root_two_over_pi * (1.0 + 3.0 * cubic * v * v))
    return v * cdf, slope


OWN = ROWS // 2
SELF = 11
FAR = 7
CHUNK = 1024
CHUNKS = WIDTH // CHUNK
PIECES = 4
PIECE = WIDTH // PIECES


def tiled(a):
    return jnp.concatenate([a] * (CHUNK // 128), axis=1)


def folded(a):
    total = a[:, 0:128]
    for i in range(1, a.shape[1] // 128):
        total = total + a[:, i * 128 : (i + 1) * 128]
    return total


def row_mean(a):
    return jnp.broadcast_to(jnp.sum(a, axis=-1, keepdims=True) * (1.0 / WIDTH), (OWN, 128))


def relay(
    me, w, gains_ref, valid_ref, grad_ref, probe_ref,
    x, g, cb, inv, pre, hid, wsum, out, pg, cb_in, hid_in, out_in, pg_in, pr, pr_in,
    fs, fr, bs, br,
):
    mine = me.s
    sib = me.y * 2 + 1 - me.c

    def span(j):
        return slice(j * (CHUNK // 256), (j + 1) * (CHUNK // 256))

    def weight(s, j, half):
        cols = slice(half * HID, (half + 1) * HID)
        return w[lax.rem(s, 2), s // 2, span(j), :, :, cols].reshape(CHUNK, HID)

    def send_cb():
        return remote(cb.at[sib], cb_in, fs.at[0], fr.at[0], me.sibling())

    def send_hid():
        return remote(hid.at[sib], hid_in, fs.at[1], fr.at[1], me.sibling())

    def send_pr():
        return remote(pr, pr_in, fs.at[2], fr.at[2], me.sibling())

    def send_out(p):
        cols = pl.ds(p * PIECE, PIECE)
        return remote(out.at[1 - me.c, :, cols], out_in.at[:, cols], bs.at[p], br.at[p], me.sibling())

    def send_pg():
        return remote(pg.at[1 - me.c], pg_in, bs.at[PIECES], br.at[PIECES], me.sibling())

    def gain_of(s):
        return gains_ref[lax.rem(s, 2), s // 2, 0:1, :]

    def cols_of(j):
        return slice(j * CHUNK, (j + 1) * CHUNK)

    def picked(ref):
        for j in range(CHUNKS):
            cols = cols_of(j)
            rows = jnp.zeros((TOK, CHUNK), f32)
            for i in range(OWN // TOK):
                part = pl.ds(i * TOK, TOK)
                chosen = valid_ref[1, pl.ds(pl.multiple_of(me.c * OWN + i * TOK, TOK), TOK), :]
                rows = rows + tiled(chosen) * x[part, cols].astype(f32)
            ref[:, cols] = rows.astype(bf16)

    total = jnp.zeros((OWN, 128), f32)
    for j in range(CHUNKS):
        total = total + folded(x[:, cols_of(j)].astype(f32))

    def forward(s, total):
        @pl.when(s == mine)
        def _():
            picked(probe_ref)

        @pl.when(s == sib)
        def _():
            picked(pr)
            send_pr().start()

        mean = tiled(row_mean(total))
        squares = jnp.zeros((OWN, 128), f32)
        acc = jnp.zeros((OWN + 16, HID), f32)
        ones = jnp.ones((16, CHUNK), bf16)
        for j in range(CHUNKS):
            cols = cols_of(j)
            centred = x[:, cols].astype(f32) - mean
            squares = squares + folded(centred * centred)
            low = centred.astype(bf16)
            cb[s, :, cols] = low
            part = weight(s, j, 0)
            acc = acc + jnp.dot(jnp.concatenate([low, ones], axis=0), part, preferred_element_type=f32)
        wsum[s] = acc[OWN : OWN + 8]
        acc = acc[:OWN]
        spread = lax.rsqrt(row_mean(squares) + eps_norm)
        inv[s] = spread
        pre_act = acc * spread
        pre[s] = pre_act
        hidden = gelu_parts(pre_act)[0].astype(bf16)
        hid[s] = hidden

        @pl.when(s == sib)
        def _():
            send_cb().start()
            send_hid().start()

        gain = tiled(gain_of(s))
        total = jnp.zeros((OWN, 128), f32)
        for j in range(CHUNKS):
            cols = cols_of(j)
            branch = contract_last(hidden, weight(s, j, 1))
            low = (x[:, cols].astype(f32) + gain * branch).astype(bf16)
            x[:, cols] = low
            total = total + folded(low.astype(f32))
        return total

    lax.fori_loop(0, SECTIONS, forward, total)

    keep = tiled(valid_ref[0, pl.ds(pl.multiple_of(me.c * OWN, OWN), OWN), :]) > 0.5
    last = SECTIONS - 1
    gain = tiled(gain_of(last))
    hidden_grad = jnp.zeros((OWN, HID), f32)
    for j in range(CHUNKS):
        cols = cols_of(j)
        low = jnp.where(keep, x[:, cols].astype(f32), 0.0).astype(bf16)
        g[:, cols] = low
        scaled = (gain * low.astype(f32)).astype(bf16)
        out[1, :, cols] = scaled
        hidden_grad = hidden_grad + jnp.dot(scaled, weight(last, j, 1), preferred_element_type=f32)

    @pl.when(sib == last)
    def _():
        for p in range(PIECES):
            send_out(p).start()

    def inner(s, hidden_grad):
        pre_act = pre[s]
        scaled = (inv[s] * (gelu_parts(pre_act)[1] * hidden_grad)).astype(bf16)
        pg[lax.rem(s, 2)] = scaled

        @pl.when(s == sib)
        def _():
            send_pg().start()

        return scaled, pre_act

    def backward(i, hidden_grad):
        s = last - i
        scaled_pre, pre_act = inner(s, hidden_grad)
        pre_f = scaled_pre.astype(f32)
        shift = tiled(row_mean(pre_f * wsum[s, 0:1]))
        slope = tiled(row_mean(pre_f * pre_act) * inv[s])
        gain = tiled(gain_of(s - 1))
        slot = lax.rem(s + 1, 2)
        hidden_grad = jnp.zeros((OWN, HID), f32)
        for j in range(CHUNKS):
            cols = cols_of(j)
            normed_grad = contract_last(scaled_pre, weight(s, j, 0))
            low = (
                g[:, cols].astype(f32) + (normed_grad - shift - cb[s, :, cols].astype(f32) * slope)
            ).astype(bf16)
            g[:, cols] = low
            scaled = (gain * low.astype(f32)).astype(bf16)
            out[slot, :, cols] = scaled
            hidden_grad = hidden_grad + jnp.dot(scaled, weight(s - 1, j, 1), preferred_element_type=f32)
            if (j + 1) * CHUNK % PIECE == 0:

                @pl.when(s - 1 == sib)
                def _():
                    send_out((j + 1) * CHUNK // PIECE - 1).start()

        return hidden_grad

    hidden_grad = lax.fori_loop(0, last - me.y * 2, backward, hidden_grad)
    inner(me.y * 2, hidden_grad)

    send_pr().wait()
    probe_ref[...] = (probe_ref[...].astype(f32) + pr_in[...].astype(f32)).astype(bf16)
    send_cb().wait()
    send_hid().wait()
    send_pg().wait()
    for p in range(PIECES):
        send_out(p).wait()
    def store(j, half, columns):
        rows = columns.astype(bf16).T.reshape(CHUNK // 256, NX, SHARD, HID)
        for i in range(CHUNK // 256):
            slot = lax.rem(j * (CHUNK // 256) + i - me.z + SELF + NZ, NZ)
            grad_ref[slot, :, :, pl.ds(half * HID, HID)] = rows[i]

    pg_a, pg_b, hid_a, hid_b = pg[me.c], pg_in[...], hid[mine], hid_in[...]
    for j in range(CHUNKS):
        cols = cols_of(j)
        first = contract_first(pg_a, cb[mine, :, cols]) + contract_first(pg_b, cb_in[:, cols])
        store(j, 0, first)
        second = contract_first(hid_a, out[me.c, :, cols]) + contract_first(hid_b, out_in[:, cols])
        store(j, 1, second)


ROWS_Z, ROWS_X = 32, 32
FRESH_XZ, FRESH_ZX = 16, 48
GROUP = SECTIONS * NX


class SumRoundZ:
    def __init__(self, me, own, held, sems, index):
        self.me, self.own, self.held, self.index = me, own, held, index
        self.zs, self.zr = sems

    def slot(self, flow, k):
        return (SELF + k if flow == 0 else SELF - k) % NZ

    def copy(self, flow, k):
        first = k % 2 == 1 or k == 8
        hop = 1 if k % 2 else 2
        to = self.me.at_z(hop if flow == 0 else -hop)
        src = self.own(self.slot(flow, k)) if first else self.held(flow, k + 2 if k < 6 or flow == 0 else 7)
        return remote(src, self.held(flow, k), self.zs.at[flow, k, self.index], self.zr.at[flow, k, self.index], to)

    def begin(self, *distances):
        for k in distances:
            for flow in range(2):
                if k <= last_of(flow):
                    self.copy(flow, k).start()

    def step(self, k):
        for flow in range(2):
            into = k + 2 if k < 6 or flow == 0 else 7
            for i in ((7, 8) if k == 6 else (k + 1, k + 2)):
                if i <= last_of(flow):
                    self.copy(flow, i).wait_recv()
            own = self.own(self.slot(flow, k))
            total = own[...].astype(f32) + self.held(flow, into)[...].astype(f32)
            if into != k + 1:
                total = total + self.held(flow, k + 1)[...].astype(f32)
            self.held(flow, into)[...] = total.astype(bf16)
            self.copy(flow, k).start()

    def wait(self):
        for flow in range(2):
            for k in (1, 2):
                self.copy(flow, k).wait_recv()

    def result(self):
        total = self.own(SELF)[...].astype(f32)
        for flow in range(2):
            for k in (1, 2):
                total = total + self.held(flow, k)[...].astype(f32)
        return total

    def drain(self):
        for flow in range(2):
            for k in range(1, last_of(flow) + 1):
                self.copy(flow, k).wait_send()


def finish(
    me, settle, put, grad_ref, master_ref, first_ref, second_ref, gain_ref, probe_ref,
    out_ref, new_master_ref, new_first_ref, new_second_ref,
    fresh, ra, rb, xa, xa_out, xb, tb, share, near, far,
    zs, zr, xs, xr, ns, nr, ms, mr, *sems,
):
    def group_at(i):
        ds, dx = i // NX, i % NX
        return (lax.rem(me.s + ds, SECTIONS), me.z * NX + lax.rem(me.x + dx, NX))

    def xbcopy(dx, part):
        span = slice(0, FAR) if part == 0 else slice(FAR, NZ)
        src = grad_ref.at[span, lax.rem(me.x + dx, NX), pl.ds(ROWS_Z, ROWS_X), :]
        sem = (1 + part, dx)
        return remote(src, xb.at[dx, span], xs.at[sem], xr.at[sem], me.at_x(dx))

    def xacopy(dx):
        src = xa_out.at[lax.rem(me.x + dx, NX)]
        return remote(src, xa.at[dx], xs.at[0, dx], xr.at[0, dx], me.at_x(dx))

    def piece_sum(piece):
        pair = pl.ds(2 * piece, 2)
        return SumRoundZ(
            me,
            lambda z: grad_ref.at[z, pair, pl.ds(0, ROWS_Z), :],
            lambda flow, k: ra.at[flow, k, pair],
            (zs, zr),
            piece,
        )

    pieces = [piece_sum(0), piece_sum(1)]
    late = SumRoundZ(me, lambda z: tb.at[z], lambda flow, k: rb.at[flow, k], (zs, zr), 2)
    def add(part):
        for dx in range(1, NX):
            xbcopy(dx, part).wait_recv()
        for z in range(FAR) if part == 0 else range(FAR, NZ):
            total = grad_ref[z, me.x, pl.ds(ROWS_Z, ROWS_X), :].astype(f32)
            for dx in range(1, NX):
                total = total + xb[dx, z].astype(f32)
            tb[z] = total.astype(bf16)

    for piece in pieces:
        piece.begin(8, 7)
    for part in range(2):
        for dx in range(1, NX):
            xbcopy(dx, part).start()
        if part == 0:
            for piece in pieces:
                piece.begin(5)
    settle()
    for piece in pieces:
        piece.step(6)
    for piece in pieces:
        piece.begin(3)
    add(0)
    late.begin(8, 7, 5)
    for piece in pieces:
        piece.step(4)
    for piece in pieces:
        piece.begin(1)
    late.step(6)
    add(1)
    late.begin(3, 1)
    for piece in pieces:
        piece.step(2)
    late.step(4)
    for i, piece in enumerate(pieces):
        piece.wait()
        xa_out[pl.ds(2 * i, 2)] = piece.result().astype(bf16)
    for dx in range(1, NX):
        xacopy(dx).start()
    late.step(2)
    for dx in range(1, NX):
        xacopy(dx).wait_recv()
    total = xa_out[me.x].astype(f32)
    for dx in range(1, NX):
        total = total + xa[dx].astype(f32)
    share[pl.ds(0, ROWS_Z), :] = total
    late.wait()
    share[pl.ds(ROWS_Z, ROWS_X), :] = late.result()

    squares = jnp.zeros((8, 128), f32)
    for i in range(SHARD // 8):
        for j in range(2):
            tile = share[pl.ds(i * 8, 8), pl.ds(j * 128, 128)]
            squares = squares + tile * tile
    near[0] = squares

    def ncopy(i):
        return remote(near.at[0], near.at[i], ns.at[i], nr.at[i], group_at(i))

    def mcopy(k):
        return remote(far.at[0], far.at[k], ms.at[k], mr.at[k], me.at_z(k))

    def n_wait(i, carry):
        ncopy(i).wait_recv()
        return carry

    def n_sent(i, carry):
        ncopy(i).wait_send()
        return carry

    def m_sent(i, carry):
        mcopy(i).wait_send()
        return carry

    def m_wait(i, carry):
        mcopy(i).wait_recv()
        return carry

    for i in range(1, GROUP):
        ncopy(i).start()
    lax.fori_loop(1, GROUP, n_wait, 0)
    far[0] = jnp.sum(near[...], axis=0)
    for k in (8, 7, 9, 6, 10, 5, 11, 4, 12, 3, 13, 2, 14, 1, 15):
        mcopy(k).start()
    lax.fori_loop(1, NZ, m_wait, 0)
    norm_sq = jnp.sum(jnp.sum(far[...], axis=0), keepdims=True)

    clip_factor = 1.0 / jnp.maximum(jnp.sqrt(norm_sq), 1.0)
    clipped = share[...] * clip_factor
    master_now = master_ref[...]
    new_first = beta_one * first_ref[...] + (1.0 - beta_one) * clipped
    new_second = beta_two * second_ref[...] + (1.0 - beta_two) * clipped * clipped
    new_master = master_now - learn_rate * (
        new_first / (jnp.sqrt(new_second) + eps_adam) + decay_rate * master_now
    )
    fresh[me.z, me.x] = new_master.astype(bf16)
    new_master_ref[...] = new_master
    new_first_ref[...] = new_first
    new_second_ref[...] = new_second

    def early_part(z, x):
        return fresh.at[z, x, pl.ds(0, FRESH_XZ)]

    def early_block(z, piece):
        return fresh.at[z, pl.ds(2 * piece, 2), pl.ds(0, FRESH_XZ)]

    def mid_part(z, x):
        return fresh.at[z, x, pl.ds(FRESH_XZ, FRESH_ZX)]

    mid = RoundZ(me, mid_part, sems[0:6], 2)
    blocks = BlocksRoundZ(me, early_part, early_block, sems[6:10], 2)
    blocks.begin()
    mid.begin()
    for copy in put:
        copy.start()
    for piece in pieces:
        piece.drain()
    late.drain()
    for dx in range(1, NX):
        xbcopy(dx, 0).wait_send()
        xbcopy(dx, 1).wait_send()
        xacopy(dx).wait_send()
    blocks.launch()
    lax.fori_loop(1, GROUP, n_sent, 0)
    lax.fori_loop(1, NZ, m_sent, 0)

    for t in range(1, 7):
        mid.step(t)
        blocks.step(t)
        mid.pass_on(t - 1)
        mid.wait(t - 2)
        if t >= 3:
            mid.drain(t - 3)
            blocks.drain(t - 3)

    values = probe_ref[...].astype(f32)
    normed = normalize(values)[0].astype(bf16)
    pre_act = jnp.zeros((TOK, HID), f32)
    for z in range(NZ):
        part = fresh[z, :, :, :HID].reshape(256, HID)
        pre_act = pre_act + jnp.dot(normed[:, z * 256 : (z + 1) * 256], part, preferred_element_type=f32)
    hidden = gelu_parts(pre_act)[0].astype(bf16)
    gain = gain_ref[0:1, 0:1]
    for z in range(NZ):
        part = fresh[z, :, :, HID:].reshape(256, HID)
        cols = slice(z * 256, (z + 1) * 256)
        out_ref[:, cols] = (values[:, cols] + gain * contract_last(hidden, part)).astype(bf16)
    mid.drain(4)
    blocks.drain(4)
    blocks.finish()


def partners(me):
    ys = [me.at_y(k) for k in range(1, NY)]
    xs = [me.at_x(k) for k in range(1, NX)]
    return ys + xs + [me.at_z(k) for k in (1, 2, -1, -2)] + [me.sibling()]


N_GATHER, N_RELAY = 26, 4


def step_kernel(
    w_ref, depth_hbm, counts_hbm, plan_hbm, x_hbm, master_hbm, first_hbm, second_hbm,
    out_ref, new_master_hbm, new_first_hbm, new_second_hbm,
    w, gains, grad, probe, gain_ref, marks_ref, master_ref, first_ref, second_ref,
    depth_ref, counts_ref, plan_ref, new_master_ref, new_first_ref, new_second_ref,
    x, g, cb, inv, pre, hid, wsum, out, pg, cb_in, hid_in, out_in, pg_in, pr, pr_in,
    fresh, ra, rb, xa, xa_out, xb, tb, share, near, far,
    x_sem, *sems,
):
    me = Place()
    get_x = pltpu.make_async_copy(
        x_hbm.at[pl.ds(pl.multiple_of(me.c * OWN, OWN), OWN)], x, x_sem.at[0]
    )
    state = [
        pltpu.make_async_copy(src, dst, x_sem.at[i + 1])
        for i, (src, dst) in enumerate(
            (
                (depth_hbm, depth_ref),
                (counts_hbm, counts_ref),
                (plan_hbm, plan_ref),
                (master_hbm, master_ref),
                (first_hbm, first_ref),
                (second_hbm, second_ref),
            )
        )
    ]
    keep = pltpu.make_async_copy(w_ref, w.at[me.c, me.y, me.z, me.x], x_sem.at[7])
    keep.start()
    for get in state[:3]:
        get.start()
    get_x.start()
    for get in state[3:]:
        get.start()
    greet(partners(me))

    def ready():
        for get in state[:3]:
            get.wait()
        gain_ref[...] = jnp.broadcast_to(lax.rsqrt(1.0 + depth_ref[...].astype(f32) / 8.0), (8, 128))
        place_in_block = lax.broadcasted_iota(jnp.int32, (TOK, 128), 0)
        for m in range(ROWS // TOK):
            rows = pl.ds(m * TOK, TOK)
            marks_ref[0, rows, :] = (place_in_block < counts_ref[0:1, m : m + 1]).astype(f32)
            planned = jnp.broadcast_to((plan_ref[0:1, 15:16] == m).astype(f32), (TOK, 128))
            marks_ref[1, rows, :] = planned

    settle = gather_all(me, w_ref, keep, ready, w, gains, gain_ref, *sems[:N_GATHER])
    get_x.wait()
    for get in state[3:]:
        get.wait()
    relay(
        me, w, gains, marks_ref, grad, probe,
        x, g, cb, inv, pre, hid, wsum, out, pg, cb_in, hid_in, out_in, pg_in, pr, pr_in,
        *sems[N_GATHER : N_GATHER + N_RELAY],
    )
    put = [
        pltpu.make_async_copy(src, dst, x_sem.at[i])
        for i, (src, dst) in enumerate(
            (
                (new_master_ref, new_master_hbm),
                (new_first_ref, new_first_hbm),
                (new_second_ref, new_second_hbm),
            )
        )
    ]
    finish(
        me, settle, put, grad, master_ref, first_ref, second_ref, gain_ref, probe,
        out_ref, new_master_ref, new_first_ref, new_second_ref,
        fresh, ra, rb, xa, xa_out, xb, tb, share, near, far,
        *sems[N_GATHER + N_RELAY :],
    )
    for copy in put:
        copy.wait()


def hand_out_kernel(*refs):
    for i in range(4):
        refs[4 + i][...] = refs[i][...]


def shards(inputs, stashed, master, first_moment, second_moment, counts, plan, layer_index):
    state = jax.ShapeDtypeStruct((SHARD, 2 * HID), f32)
    vmem = pl.BlockSpec(memory_space=pltpu.VMEM)
    anywhere = pl.BlockSpec(memory_space=pl.ANY)
    chunks = (NZ, NX, SHARD, 2 * HID)
    probe_out, new_master, new_first, new_second = pl.pallas_call(
        step_kernel,
        out_shape=(jax.ShapeDtypeStruct((TOK, WIDTH), bf16), state, state, state),
        in_specs=[anywhere] * 8,
        out_specs=(vmem, anywhere, anywhere, anywhere),
        scratch_shapes=[
            pltpu.VMEM((2, NY, *chunks), bf16),
            pltpu.VMEM((2, NY, 8, 128), f32),
            pltpu.VMEM(chunks, bf16),
            pltpu.VMEM((TOK, WIDTH), bf16),
            pltpu.VMEM((8, 128), f32),
            pltpu.VMEM((2, ROWS, 128), f32),
            *[pltpu.VMEM((SHARD, 2 * HID), f32)] * 3,
            pltpu.VMEM((1, 1), jnp.int32),
            *[pltpu.VMEM((1, ROWS // TOK), jnp.int32)] * 2,
            *[pltpu.VMEM((SHARD, 2 * HID), f32)] * 3,
            pltpu.VMEM((OWN, WIDTH), bf16),
            pltpu.VMEM((OWN, WIDTH), bf16),
            pltpu.VMEM((SECTIONS, OWN, WIDTH), bf16),
            pltpu.VMEM((SECTIONS, OWN, 128), f32),
            pltpu.VMEM((SECTIONS, OWN, HID), f32),
            pltpu.VMEM((SECTIONS, OWN, HID), bf16),
            pltpu.VMEM((SECTIONS, 8, HID), f32),
            pltpu.VMEM((2, OWN, WIDTH), bf16),
            pltpu.VMEM((2, OWN, HID), bf16),
            pltpu.VMEM((OWN, WIDTH), bf16),
            pltpu.VMEM((OWN, HID), bf16),
            pltpu.VMEM((OWN, WIDTH), bf16),
            pltpu.VMEM((OWN, HID), bf16),
            pltpu.VMEM((TOK, WIDTH), bf16),
            pltpu.VMEM((TOK, WIDTH), bf16),
            pltpu.VMEM(chunks, bf16),
            pltpu.VMEM((2, 9, NX, ROWS_Z, 2 * HID), bf16),
            pltpu.VMEM((2, 9, ROWS_X, 2 * HID), bf16),
            pltpu.VMEM((NX, ROWS_Z, 2 * HID), bf16),
            pltpu.VMEM((NX, ROWS_Z, 2 * HID), bf16),
            pltpu.VMEM((NX, NZ, ROWS_X, 2 * HID), bf16),
            pltpu.VMEM((NZ, ROWS_X, 2 * HID), bf16),
            pltpu.VMEM((SHARD, 2 * HID), f32),
            pltpu.VMEM((GROUP, 8, 128), f32),
            pltpu.VMEM((NZ, 8, 128), f32),
            DMA((8,)),
            *[DMA((NY,))] * 4,
            *[DMA((3, 9))] * 2,
            *ROUND_SEMS,
            *ROUND_SEMS,
            *BLOCK_SEMS,
            *OVER_SEMS,
            *[DMA((3,))] * 2,
            *[DMA((PIECES + 1,))] * 2,
            *[DMA((2, 9, 3))] * 2,
            *[DMA((3, NX))] * 2,
            *[DMA((GROUP,))] * 2,
            *[DMA((NZ,))] * 2,
            *ROUND_SEMS,
            *BLOCK_SEMS,
        ],
        compiler_params=pltpu.CompilerParams(
            collective_id=0, has_side_effects=True, vmem_limit_bytes=60 * 2**20
        ),
        name="optimizer_step",
    )(
        stashed[0], layer_index.reshape(1, 1), counts, plan.reshape(1, 16),
        inputs.reshape(ROWS, WIDTH), master[0], first_moment[0], second_moment[0],
    )
    results = (probe_out[None], new_master[None], new_first[None], new_second[None])
    return pl.pallas_call(
        hand_out_kernel,
        out_shape=tuple(jax.ShapeDtypeStruct(r.shape, r.dtype) for r in results),
        in_specs=[vmem] * 4,
        out_specs=(vmem,) * 4,
        compiler_params=pltpu.CompilerParams(vmem_limit_bytes=60 * 2**20),
        name="hand_out",
    )(*results)


def solution(mesh):
    in_specs = (
        P(None, "dp", None),
        P("section", "dp", None),
        P("section", "dp", None),
        P("section", "dp", None),
        P("section", "dp", None),
        P("dp", None),
        P(),
        P("section"),
    )
    out_specs = (
        P("section", "dp", None),
        P("section", "dp", None),
        P("section", "dp", None),
        P("section", "dp", None),
    )
    return jax.shard_map(shards, mesh=mesh, in_specs=in_specs, out_specs=out_specs, check_vma=False)
```

```python
import functools

import jax
import jax.numpy as jnp
from jax import lax
from jax.experimental import pallas as pl
from jax.experimental.pallas import tpu as pltpu
from jax.sharding import PartitionSpec as P

eps_norm = 1e-05
beta_one = 0.9
beta_two = 0.95
eps_adam = 1e-08
learn_rate = 0.002
decay_rate = 0.1

MESH = pl.DeviceIdType.MESH
WIDTH = 4096
HID = 128
ROWS = 256
TOK = 16
SECTIONS = 8
SHARD = 64
NZ = 16
NX = 4
NY = 4
f32 = jnp.float32
bf16 = jnp.bfloat16


class Place:

    def __init__(self):
        self.s = lax.axis_index("section")
        self.d = lax.axis_index("dp")
        self.c = lax.rem(self.s, 2)
        self.y = self.s // 2
        self.z = self.d // NX
        self.x = lax.rem(self.d, NX)

    def at_z(self, k):
        return (self.s, lax.rem(self.z + k + 2 * NZ, NZ) * NX + self.x)

    def at_x(self, k):
        return (self.s, self.z * NX + lax.rem(self.x + k + NX, NX))

    def at_y(self, k):
        return (lax.rem(self.y + k + NY, NY) * 2 + self.c, self.d)

    def sibling(self):
        return (self.y * 2 + 1 - self.c, self.d)


def greet(partners):
    barrier = pltpu.get_barrier_semaphore()
    for partner in partners:
        pl.semaphore_signal(barrier, inc=1, device_id=partner, device_id_type=MESH)
    pl.semaphore_wait(barrier, len(partners))


def remote(src, dst, send, recv, to):
    return pltpu.make_async_remote_copy(
        src_ref=src, dst_ref=dst, send_sem=send, recv_sem=recv, device_id=to, device_id_type=MESH
    )


def block_z(me, flow, k):
    if flow == 0:
        return lax.rem(me.z - k + 2 * NZ, NZ)
    return lax.rem(me.z + k, NZ)


def last_of(flow):
    return 8 if flow == 0 else 7


def inside(flow, k, lowest):
    return max(flow, lowest) <= k <= last_of(flow)


class OverX:
    def __init__(self, me, part, at, here, sems):
        self.me, self.part, self.at, self.here = me, part, at, here
        self.ss, self.sr, self.fs, self.fr = sems

    def copy(self, flow, k, side):
        ref = self.part(block_z(self.me, flow, k), self.here)
        to = self.at(1 if side == 0 else -1)
        return remote(ref, ref, self.ss.at[flow, k, side], self.sr.at[flow, k, side], to)

    def onward(self, flow, k):
        came = -1 if flow == 0 else 1
        ref = self.part(block_z(self.me, flow, k), lax.rem(self.here + came + 4, 4))
        return remote(ref, ref, self.fs.at[flow, k], self.fr.at[flow, k], self.at(-came))

    def send(self, flow, k):
        for side in range(2):
            self.copy(flow, k, side).start()

    def pass_on(self, k):
        for flow in range(2):
            if inside(flow, k, 0):
                for side in range(2):
                    self.copy(flow, k, side).wait_recv()
                self.onward(flow, k).start()

    def wait(self, flow, k):
        self.onward(flow, k).wait_recv()

    def drain(self, flow, k):
        for side in range(2):
            self.copy(flow, k, side).wait_send()
        self.onward(flow, k).wait_send()


class RoundZ:
    def __init__(self, me, part, sems, stride):
        self.me, self.part, self.stride = me, part, stride
        self.zs, self.zr = sems[0], sems[1]
        self.over = OverX(me, part, me.at_x, me.x, sems[2:])

    def copy(self, flow, k, hop=1):
        ref = self.part(block_z(self.me, flow, k - hop), self.me.x)
        to = self.me.at_z(hop if flow == 0 else -hop)
        return remote(ref, ref, self.zs.at[flow, k], self.zr.at[flow, k], to)

    def begin(self):
        for hop in range(1, self.stride + 1):
            for flow in range(2):
                self.copy(flow, hop, hop).start()
        self.over.send(0, 0)

    def step(self, j):
        far = j * self.stride
        for flow in range(2):
            if inside(flow, far, 1):
                self.copy(flow, far, self.stride).wait_recv()

                for hop in range(1, self.stride + 1):
                    if far + hop <= last_of(flow):
                        self.copy(flow, far + hop, hop).start()

                self.over.send(flow, far)

        if self.stride == 2:
            for flow in range(2):
                if inside(flow, far - 1, 1):
                    self.copy(flow, far - 1, 1).wait_recv()
                    self.over.send(flow, far - 1)

    def steps_of(self, j):
        return [j * self.stride - i for i in range(self.stride)]

    def pass_on(self, j):
        for k in self.steps_of(j):
            self.over.pass_on(k)

    def wait(self, j):
        for k in self.steps_of(j):
            for flow in range(2):
                if inside(flow, k, 0):
                    self.over.wait(flow, k)

    def drain(self, j):
        for i, k in enumerate(self.steps_of(j)):
            for flow in range(2):
                if inside(flow, k, 1):
                    self.copy(flow, k, self.stride - i).wait_send()
                if inside(flow, k, 0):
                    self.over.drain(flow, k)


class BlocksRoundZ:
    def __init__(self, me, part, block, sems, stride):
        self.me, self.part, self.block, self.stride = me, part, block, stride
        self.xs, self.xr, self.zs, self.zr = sems

    def first(self, dx):
        ref = self.part(self.me.z, self.me.x)
        return remote(ref, ref, self.xs.at[dx], self.xr.at[dx], self.me.at_x(dx))

    def copy(self, flow, k, hop, piece):
        ref = self.block(block_z(self.me, flow, k - hop), piece)
        to = self.me.at_z(hop if flow == 0 else -hop)
        return remote(ref, ref, self.zs.at[flow, k, piece], self.zr.at[flow, k, piece], to)

    def begin(self):
        for dx in range(1, NX):
            self.first(dx).start()

    def launch(self):
        for dx in range(1, NX):
            self.first(dx).wait_recv()
        for piece in range(2):
            for hop in range(1, self.stride + 1):
                for flow in range(2):
                    self.copy(flow, hop, hop, piece).start()

    def step(self, j):
        far = j * self.stride
        for piece in range(2):
            for flow in range(2):
                end = 8 if flow == piece else 7
                if 1 <= far <= end:
                    self.copy(flow, far, self.stride, piece).wait_recv()

                    for hop in range(1, self.stride + 1):
                        if far + hop <= end:
                            self.copy(flow, far + hop, hop, piece).start()

        if self.stride == 2:
            for piece in range(2):
                for flow in range(2):
                    if 2 <= far <= 8:
                        self.copy(flow, far - 1, 1, piece).wait_recv()

    def drain(self, j):
        for i in range(self.stride):
            k = j * self.stride - i
            for piece in range(2):
                for flow in range(2):
                    if 1 <= k <= (8 if flow == piece else 7):
                        self.copy(flow, k, self.stride - i, piece).wait_send()

    def finish(self):
        for dx in range(1, NX):
            self.first(dx).wait_send()


DMA = pltpu.SemaphoreType.DMA
ROUND_SEMS = [DMA((2, 9)), DMA((2, 9)), DMA((2, 9, 2)), DMA((2, 9, 2)), DMA((2, 9)), DMA((2, 9))]
BLOCK_SEMS = [DMA((NX,)), DMA((NX,)), DMA((2, 9, 2)), DMA((2, 9, 2))]
OVER_SEMS = [DMA((2, 9, 2)), DMA((2, 9, 2)), DMA((2, 9)), DMA((2, 9))]

ROWS_XZ, ROWS_ZX, ROWS_ZXY = 16, 16, 32


def gather_all(me, w_ref, keep, ready, all_ref, gains_ref, gain_ref, ys, yr, gs, gr, ss, sr, *sems):
    early = ROWS_XZ + ROWS_ZX

    def ycopy(k):
        rows = pl.ds(0, early)
        dst = all_ref.at[me.c, me.y, me.z, me.x, rows]
        return remote(w_ref.at[rows], dst, ys.at[k], yr.at[k], me.at_y(k))

    def gcopy(k):
        part = gains_ref.at[me.c, me.y]
        return remote(part, part, gs.at[k], gr.at[k], me.at_y(k))

    for k in range(1, NY):
        ycopy(k).start()
    keep.wait()

    def late_part(z, x):
        return all_ref.at[me.c, me.y, z, x, pl.ds(early, ROWS_ZXY)]

    def late_column(z, y):
        return all_ref.at[me.c, y, z, :, pl.ds(early, ROWS_ZXY)]

    def mid_part(z, x):
        return all_ref.at[me.c, :, z, x, pl.ds(ROWS_XZ, ROWS_ZX)]

    def early_part(z, x):
        return all_ref.at[me.c, :, z, x, pl.ds(0, ROWS_XZ)]

    def early_block(z, piece):
        return all_ref.at[me.c, pl.ds(2 * piece, 2), z, :, pl.ds(0, ROWS_XZ)]

    late = RoundZ(me, late_part, sems[0:6], 1)
    mid = RoundZ(me, mid_part, sems[6:12], 1)
    blocks = BlocksRoundZ(me, early_part, early_block, sems[12:16], 1)
    over_y = OverX(me, late_column, me.at_y, me.y, sems[16:20])

    def side_copy(flow, k):
        part = all_ref.at[me.c, :, block_z(me, flow, k)]
        return remote(part, part, ss.at[flow, k], sr.at[flow, k], me.sibling())

    def both(k):
        return [flow for flow in range(2) if inside(flow, k, 0)]

    late.begin()
    for k in range(1, NY):
        ycopy(k).wait_recv()
    blocks.begin()
    mid.begin()
    ready()
    gains_ref[me.c, me.y] = gain_ref[...]
    for k in range(1, NY):
        gcopy(k).start()
    gains = remote(gains_ref.at[me.c], gains_ref.at[me.c], ss.at[2, 0], sr.at[2, 0], me.sibling())

    def drain(k):
        mid.drain(k)
        blocks.drain(k)
        for flow in both(k):
            over_y.drain(flow, k)

    for t in range(1, 13):
        late.step(t)
        mid.step(t - 1)
        late.pass_on(t - 1)
        mid.pass_on(t - 2)
        late.wait(t - 2)
        for flow in both(t - 2):
            over_y.send(flow, t - 2)
        mid.wait(t - 3)
        over_y.pass_on(t - 3)
        if t == 2:
            blocks.launch()
        blocks.step(t - 2)
        if t == 4:
            for k in range(1, NY):
                gcopy(k).wait_recv()
            gains.start()
        for flow in both(t - 4):
            over_y.wait(flow, t - 4)
            side_copy(flow, t - 4).start()
        if t >= 6:
            drain(t - 6)
            late.drain(t - 6)

    for k in range(9):
        for flow in both(k):
            side_copy(flow, k).wait_recv()
    gains.wait_recv()

    def settle():
        for k in range(7, 9):
            drain(k)
            late.drain(k)
        for k in range(9):
            for flow in both(k):
                side_copy(flow, k).wait_send()
        blocks.finish()
        gains.wait_send()
        for k in range(1, NY):
            ycopy(k).wait_send()
            gcopy(k).wait_send()

    return settle


def normalize(values):
    centred = values - jnp.mean(values, axis=-1, keepdims=True)
    inv_spread = lax.rsqrt(jnp.mean(centred * centred, axis=-1, keepdims=True) + eps_norm)
    return (centred * inv_spread, inv_spread)


def contract_last(lhs_array, rhs_array):
    return lax.dot_general(
        lhs_array, rhs_array, (((1,), (1,)), ((), ())), preferred_element_type=f32
    )


def contract_first(lhs_array, rhs_array):
    return lax.dot_general(
        lhs_array, rhs_array, (((0,), (0,)), ((), ())), preferred_element_type=f32
    )


root_two_over_pi = 0.7978845608028654
cubic = 0.044715


def gelu_parts(v):
    t = jnp.tanh(root_two_over_pi * (v + cubic * (v * v * v)))
    cdf = 0.5 * (1.0 + t)
    slope = cdf + 0.5 * v * (1.0 - t * t) * (root_two_over_pi * (1.0 + 3.0 * cubic * v * v))
    return v * cdf, slope


OWN = ROWS // 2
SELF = 11
FAR = 7
CHUNK = 1024
CHUNKS = WIDTH // CHUNK
PIECES = 4
PIECE = WIDTH // PIECES


def tiled(a):
    return jnp.concatenate([a] * (CHUNK // 128), axis=1)


def folded(a):
    total = a[:, 0:128]
    for i in range(1, a.shape[1] // 128):
        total = total + a[:, i * 128 : (i + 1) * 128]
    return total


def row_mean(a):
    return jnp.broadcast_to(jnp.sum(a, axis=-1, keepdims=True) * (1.0 / WIDTH), (OWN, 128))


def relay(
    me, w, gains_ref, valid_ref, grad_ref, probe_ref,
    x, g, cb, inv, pre, hid, wsum, out, pg, cb_in, hid_in, out_in, pg_in, pr, pr_in,
    fs, fr, bs, br,
):
    mine = me.s
    sib = me.y * 2 + 1 - me.c

    def span(j):
        return slice(j * (CHUNK // 256), (j + 1) * (CHUNK // 256))

    def weight(s, j, half):
        cols = slice(half * HID, (half + 1) * HID)
        return w[lax.rem(s, 2), s // 2, span(j), :, :, cols].reshape(CHUNK, HID)

    def send_cb():
        return remote(cb.at[sib], cb_in, fs.at[0], fr.at[0], me.sibling())

    def send_hid():
        return remote(hid.at[sib], hid_in, fs.at[1], fr.at[1], me.sibling())

    def send_pr():
        return remote(pr, pr_in, fs.at[2], fr.at[2], me.sibling())

    def send_out(p):
        cols = pl.ds(p * PIECE, PIECE)
        return remote(out.at[1 - me.c, :, cols], out_in.at[:, cols], bs.at[p], br.at[p], me.sibling())

    def send_pg():
        return remote(pg.at[1 - me.c], pg_in, bs.at[PIECES], br.at[PIECES], me.sibling())

    def gain_of(s):
        return gains_ref[lax.rem(s, 2), s // 2, 0:1, :]

    def cols_of(j):
        return slice(j * CHUNK, (j + 1) * CHUNK)

    def picked(ref):
        for j in range(CHUNKS):
            cols = cols_of(j)
            rows = jnp.zeros((TOK, CHUNK), f32)
            for i in range(OWN // TOK):
                part = pl.ds(i * TOK, TOK)
                chosen = valid_ref[1, pl.ds(pl.multiple_of(me.c * OWN + i * TOK, TOK), TOK), :]
                rows = rows + tiled(chosen) * x[part, cols].astype(f32)
            ref[:, cols] = rows.astype(bf16)

    total = jnp.zeros((OWN, 128), f32)
    for j in range(CHUNKS):
        total = total + folded(x[:, cols_of(j)].astype(f32))

    def forward(s, total):
        @pl.when(s == mine)
        def _():
            picked(probe_ref)

        @pl.when(s == sib)
        def _():
            picked(pr)
            send_pr().start()

        mean = tiled(row_mean(total))
        squares = jnp.zeros((OWN, 128), f32)
        acc = jnp.zeros((OWN + 16, HID), f32)
        ones = jnp.ones((16, CHUNK), bf16)
        for j in range(CHUNKS):
            cols = cols_of(j)
            centred = x[:, cols].astype(f32) - mean
            squares = squares + folded(centred * centred)
            low = centred.astype(bf16)
            cb[s, :, cols] = low
            part = weight(s, j, 0)
            acc = acc + jnp.dot(jnp.concatenate([low, ones], axis=0), part, preferred_element_type=f32)
        wsum[s] = acc[OWN : OWN + 8]
        acc = acc[:OWN]
        spread = lax.rsqrt(row_mean(squares) + eps_norm)
        inv[s] = spread
        pre_act = acc * spread
        pre[s] = pre_act
        hidden = gelu_parts(pre_act)[0].astype(bf16)
        hid[s] = hidden

        @pl.when(s == sib)
        def _():
            send_cb().start()
            send_hid().start()

        gain = tiled(gain_of(s))
        total = jnp.zeros((OWN, 128), f32)
        for j in range(CHUNKS):
            cols = cols_of(j)
            branch = contract_last(hidden, weight(s, j, 1))
            low = (x[:, cols].astype(f32) + gain * branch).astype(bf16)
            x[:, cols] = low
            total = total + folded(low.astype(f32))
        return total

    lax.fori_loop(0, SECTIONS, forward, total)

    keep = tiled(valid_ref[0, pl.ds(pl.multiple_of(me.c * OWN, OWN), OWN), :]) > 0.5
    last = SECTIONS - 1
    gain = tiled(gain_of(last))
    hidden_grad = jnp.zeros((OWN, HID), f32)
    for j in range(CHUNKS):
        cols = cols_of(j)
        low = jnp.where(keep, x[:, cols].astype(f32), 0.0).astype(bf16)
        g[:, cols] = low
        scaled = (gain * low.astype(f32)).astype(bf16)
        out[1, :, cols] = scaled
        hidden_grad = hidden_grad + jnp.dot(scaled, weight(last, j, 1), preferred_element_type=f32)

    @pl.when(sib == last)
    def _():
        for p in range(PIECES):
            send_out(p).start()

    def inner(s, hidden_grad):
        pre_act = pre[s]
        scaled = (inv[s] * (gelu_parts(pre_act)[1] * hidden_grad)).astype(bf16)
        pg[lax.rem(s, 2)] = scaled

        @pl.when(s == sib)
        def _():
            send_pg().start()

        return scaled, pre_act

    def backward(i, hidden_grad):
        s = last - i
        scaled_pre, pre_act = inner(s, hidden_grad)
        pre_f = scaled_pre.astype(f32)
        shift = tiled(row_mean(pre_f * wsum[s, 0:1]))
        slope = tiled(row_mean(pre_f * pre_act) * inv[s])
        gain = tiled(gain_of(s - 1))
        slot = lax.rem(s + 1, 2)
        hidden_grad = jnp.zeros((OWN, HID), f32)
        for j in range(CHUNKS):
            cols = cols_of(j)
            normed_grad = contract_last(scaled_pre, weight(s, j, 0))
            low = (
                g[:, cols].astype(f32) + (normed_grad - shift - cb[s, :, cols].astype(f32) * slope)
            ).astype(bf16)
            g[:, cols] = low
            scaled = (gain * low.astype(f32)).astype(bf16)
            out[slot, :, cols] = scaled
            hidden_grad = hidden_grad + jnp.dot(scaled, weight(s - 1, j, 1), preferred_element_type=f32)
            if (j + 1) * CHUNK % PIECE == 0:

                @pl.when(s - 1 == sib)
                def _():
                    send_out((j + 1) * CHUNK // PIECE - 1).start()

        return hidden_grad

    hidden_grad = lax.fori_loop(0, last - me.y * 2, backward, hidden_grad)
    inner(me.y * 2, hidden_grad)

    send_pr().wait()
    probe_ref[...] = (probe_ref[...].astype(f32) + pr_in[...].astype(f32)).astype(bf16)
    send_cb().wait()
    send_hid().wait()
    send_pg().wait()
    for p in range(PIECES):
        send_out(p).wait()
    def store(j, half, columns):
        rows = columns.astype(bf16).T.reshape(CHUNK // 256, NX, SHARD, HID)
        for i in range(CHUNK // 256):
            slot = lax.rem(j * (CHUNK // 256) + i - me.z + SELF + NZ, NZ)
            grad_ref[slot, :, :, pl.ds(half * HID, HID)] = rows[i]

    pg_a, pg_b, hid_a, hid_b = pg[me.c], pg_in[...], hid[mine], hid_in[...]
    for j in range(CHUNKS):
        cols = cols_of(j)
        first = contract_first(pg_a, cb[mine, :, cols]) + contract_first(pg_b, cb_in[:, cols])
        store(j, 0, first)
        second = contract_first(hid_a, out[me.c, :, cols]) + contract_first(hid_b, out_in[:, cols])
        store(j, 1, second)


ROWS_Z, ROWS_X = 32, 32
FRESH_XZ, FRESH_ZX = 16, 48
GROUP = SECTIONS * NX


class SumRoundZ:
    def __init__(self, me, own, held, sems, index):
        self.me, self.own, self.held, self.index = me, own, held, index
        self.zs, self.zr = sems

    def slot(self, flow, k):
        return (SELF + k if flow == 0 else SELF - k) % NZ

    def copy(self, flow, k):
        first = k % 2 == 1 or k == 8
        hop = 1 if k % 2 else 2
        to = self.me.at_z(hop if flow == 0 else -hop)
        src = self.own(self.slot(flow, k)) if first else self.held(flow, k + 2 if k < 6 or flow == 0 else 7)
        return remote(src, self.held(flow, k), self.zs.at[flow, k, self.index], self.zr.at[flow, k, self.index], to)

    def begin(self, *distances):
        for k in distances:
            for flow in range(2):
                if k <= last_of(flow):
                    self.copy(flow, k).start()

    def step(self, k):
        for flow in range(2):
            into = k + 2 if k < 6 or flow == 0 else 7
            for i in ((7, 8) if k == 6 else (k + 1, k + 2)):
                if i <= last_of(flow):
                    self.copy(flow, i).wait_recv()
            own = self.own(self.slot(flow, k))
            total = own[...].astype(f32) + self.held(flow, into)[...].astype(f32)
            if into != k + 1:
                total = total + self.held(flow, k + 1)[...].astype(f32)
            self.held(flow, into)[...] = total.astype(bf16)
            self.copy(flow, k).start()

    def wait(self):
        for flow in range(2):
            for k in (1, 2):
                self.copy(flow, k).wait_recv()

    def result(self):
        total = self.own(SELF)[...].astype(f32)
        for flow in range(2):
            for k in (1, 2):
                total = total + self.held(flow, k)[...].astype(f32)
        return total

    def drain(self):
        for flow in range(2):
            for k in range(1, last_of(flow) + 1):
                self.copy(flow, k).wait_send()


def finish(
    me, settle, put, grad_ref, master_ref, first_ref, second_ref, gain_ref, probe_ref,
    out_ref, new_master_ref, new_first_ref, new_second_ref,
    fresh, ra, rb, xa, xa_out, xb, tb, share, near, far,
    zs, zr, xs, xr, ns, nr, ms, mr, *sems,
):
    def group_at(i):
        ds, dx = i // NX, i % NX
        return (lax.rem(me.s + ds, SECTIONS), me.z * NX + lax.rem(me.x + dx, NX))

    def xbcopy(dx, part):
        span = slice(0, FAR) if part == 0 else slice(FAR, NZ)
        src = grad_ref.at[span, lax.rem(me.x + dx, NX), pl.ds(ROWS_Z, ROWS_X), :]
        sem = (1 + part, dx)
        return remote(src, xb.at[dx, span], xs.at[sem], xr.at[sem], me.at_x(dx))

    def xacopy(dx):
        src = xa_out.at[lax.rem(me.x + dx, NX)]
        return remote(src, xa.at[dx], xs.at[0, dx], xr.at[0, dx], me.at_x(dx))

    def piece_sum(piece):
        pair = pl.ds(2 * piece, 2)
        return SumRoundZ(
            me,
            lambda z: grad_ref.at[z, pair, pl.ds(0, ROWS_Z), :],
            lambda flow, k: ra.at[flow, k, pair],
            (zs, zr),
            piece,
        )

    pieces = [piece_sum(0), piece_sum(1)]
    late = SumRoundZ(me, lambda z: tb.at[z], lambda flow, k: rb.at[flow, k], (zs, zr), 2)
    def add(part):
        for dx in range(1, NX):
            xbcopy(dx, part).wait_recv()
        for z in range(FAR) if part == 0 else range(FAR, NZ):
            total = grad_ref[z, me.x, pl.ds(ROWS_Z, ROWS_X), :].astype(f32)
            for dx in range(1, NX):
                total = total + xb[dx, z].astype(f32)
            tb[z] = total.astype(bf16)

    for piece in pieces:
        piece.begin(8, 7)
    for part in range(2):
        for dx in range(1, NX):
            xbcopy(dx, part).start()
        if part == 0:
            for piece in pieces:
                piece.begin(5)
    settle()
    for piece in pieces:
        piece.step(6)
    for piece in pieces:
        piece.begin(3)
    add(0)
    late.begin(8, 7, 5)
    for piece in pieces:
        piece.step(4)
    for piece in pieces:
        piece.begin(1)
    late.step(6)
    add(1)
    late.begin(3, 1)
    for piece in pieces:
        piece.step(2)
    late.step(4)
    for i, piece in enumerate(pieces):
        piece.wait()
        xa_out[pl.ds(2 * i, 2)] = piece.result().astype(bf16)
    for dx in range(1, NX):
        xacopy(dx).start()
    late.step(2)
    for dx in range(1, NX):
        xacopy(dx).wait_recv()
    total = xa_out[me.x].astype(f32)
    for dx in range(1, NX):
        total = total + xa[dx].astype(f32)
    share[pl.ds(0, ROWS_Z), :] = total
    late.wait()
    share[pl.ds(ROWS_Z, ROWS_X), :] = late.result()

    squares = jnp.zeros((8, 128), f32)
    for i in range(SHARD // 8):
        for j in range(2):
            tile = share[pl.ds(i * 8, 8), pl.ds(j * 128, 128)]
            squares = squares + tile * tile
    near[0] = squares

    def ncopy(i):
        return remote(near.at[0], near.at[i], ns.at[i], nr.at[i], group_at(i))

    def mcopy(k):
        return remote(far.at[0], far.at[k], ms.at[k], mr.at[k], me.at_z(k))

    def n_wait(i, carry):
        ncopy(i).wait_recv()
        return carry

    def n_sent(i, carry):
        ncopy(i).wait_send()
        return carry

    def m_sent(i, carry):
        mcopy(i).wait_send()
        return carry

    def m_wait(i, carry):
        mcopy(i).wait_recv()
        return carry

    for i in range(1, GROUP):
        ncopy(i).start()
    lax.fori_loop(1, GROUP, n_wait, 0)
    far[0] = jnp.sum(near[...], axis=0)
    for k in (8, 7, 9, 6, 10, 5, 11, 4, 12, 3, 13, 2, 14, 1, 15):
        mcopy(k).start()
    normed = normalize(probe_ref[...].astype(f32))[0].astype(bf16)
    lax.fori_loop(1, NZ, m_wait, 0)
    norm_sq = jnp.sum(jnp.sum(far[...], axis=0), keepdims=True)

    clip_factor = 1.0 / jnp.maximum(jnp.sqrt(norm_sq), 1.0)
    clipped = share[...] * clip_factor
    master_now = master_ref[...]
    new_first = beta_one * first_ref[...] + (1.0 - beta_one) * clipped
    new_second = beta_two * second_ref[...] + (1.0 - beta_two) * clipped * clipped
    new_master = master_now - learn_rate * (
        new_first / (jnp.sqrt(new_second) + eps_adam) + decay_rate * master_now
    )
    fresh[me.z, me.x] = new_master.astype(bf16)
    new_master_ref[...] = new_master
    new_first_ref[...] = new_first
    new_second_ref[...] = new_second

    def early_part(z, x):
        return fresh.at[z, x, pl.ds(0, FRESH_XZ)]

    def early_block(z, piece):
        return fresh.at[z, pl.ds(2 * piece, 2), pl.ds(0, FRESH_XZ)]

    def mid_part(z, x):
        return fresh.at[z, x, pl.ds(FRESH_XZ, FRESH_ZX)]

    mid = RoundZ(me, mid_part, sems[0:6], 2)
    blocks = BlocksRoundZ(me, early_part, early_block, sems[6:10], 2)
    blocks.begin()
    mid.begin()
    for copy in put:
        copy.start()
    for piece in pieces:
        piece.drain()
    late.drain()
    for dx in range(1, NX):
        xbcopy(dx, 0).wait_send()
        xbcopy(dx, 1).wait_send()
        xacopy(dx).wait_send()
    blocks.launch()
    lax.fori_loop(1, GROUP, n_sent, 0)
    lax.fori_loop(1, NZ, m_sent, 0)

    for t in range(1, 7):
        mid.step(t)
        blocks.step(t)
        mid.pass_on(t - 1)
        mid.wait(t - 2)
        if t >= 3:
            mid.drain(t - 3)
            blocks.drain(t - 3)

    values = probe_ref[...].astype(f32)
    pre_act = jnp.zeros((TOK, HID), f32)
    for z in range(NZ):
        part = fresh[z, :, :, :HID].reshape(256, HID)
        pre_act = pre_act + jnp.dot(normed[:, z * 256 : (z + 1) * 256], part, preferred_element_type=f32)
    hidden = gelu_parts(pre_act)[0].astype(bf16)
    gain = gain_ref[0:1, 0:1]
    for z in range(NZ):
        part = fresh[z, :, :, HID:].reshape(256, HID)
        cols = slice(z * 256, (z + 1) * 256)
        out_ref[:, cols] = (values[:, cols] + gain * contract_last(hidden, part)).astype(bf16)
    mid.drain(4)
    blocks.drain(4)
    blocks.finish()


def partners(me):
    ys = [me.at_y(k) for k in range(1, NY)]
    xs = [me.at_x(k) for k in range(1, NX)]
    return ys + xs + [me.at_z(k) for k in (1, 2, -1, -2)] + [me.sibling()]


N_GATHER, N_RELAY = 26, 4


def step_kernel(
    w_ref, depth_hbm, counts_hbm, plan_hbm, x_hbm, master_hbm, first_hbm, second_hbm,
    out_ref, new_master_hbm, new_first_hbm, new_second_hbm,
    w, gains, grad, probe, gain_ref, marks_ref, master_ref, first_ref, second_ref,
    depth_ref, counts_ref, plan_ref, new_master_ref, new_first_ref, new_second_ref,
    x, g, cb, inv, pre, hid, wsum, out, pg, cb_in, hid_in, out_in, pg_in, pr, pr_in,
    fresh, ra, rb, xa, xa_out, xb, tb, share, near, far,
    x_sem, *sems,
):
    me = Place()
    get_x = pltpu.make_async_copy(
        x_hbm.at[pl.ds(pl.multiple_of(me.c * OWN, OWN), OWN)], x, x_sem.at[0]
    )
    state = [
        pltpu.make_async_copy(src, dst, x_sem.at[i + 1])
        for i, (src, dst) in enumerate(
            (
                (depth_hbm, depth_ref),
                (counts_hbm, counts_ref),
                (plan_hbm, plan_ref),
                (master_hbm, master_ref),
                (first_hbm, first_ref),
                (second_hbm, second_ref),
            )
        )
    ]
    keep = pltpu.make_async_copy(w_ref, w.at[me.c, me.y, me.z, me.x], x_sem.at[7])
    keep.start()
    for get in state[:3]:
        get.start()
    get_x.start()
    for get in state[3:]:
        get.start()
    greet(partners(me))

    def ready():
        for get in state[:3]:
            get.wait()
        gain_ref[...] = jnp.broadcast_to(lax.rsqrt(1.0 + depth_ref[...].astype(f32) / 8.0), (8, 128))
        place_in_block = lax.broadcasted_iota(jnp.int32, (TOK, 128), 0)
        for m in range(ROWS // TOK):
            rows = pl.ds(m * TOK, TOK)
            marks_ref[0, rows, :] = (place_in_block < counts_ref[0:1, m : m + 1]).astype(f32)
            planned = jnp.broadcast_to((plan_ref[0:1, 15:16] == m).astype(f32), (TOK, 128))
            marks_ref[1, rows, :] = planned

    settle = gather_all(me, w_ref, keep, ready, w, gains, gain_ref, *sems[:N_GATHER])
    get_x.wait()
    for get in state[3:]:
        get.wait()
    relay(
        me, w, gains, marks_ref, grad, probe,
        x, g, cb, inv, pre, hid, wsum, out, pg, cb_in, hid_in, out_in, pg_in, pr, pr_in,
        *sems[N_GATHER : N_GATHER + N_RELAY],
    )
    put = [
        pltpu.make_async_copy(src, dst, x_sem.at[i])
        for i, (src, dst) in enumerate(
            (
                (new_master_ref, new_master_hbm),
                (new_first_ref, new_first_hbm),
                (new_second_ref, new_second_hbm),
            )
        )
    ]
    finish(
        me, settle, put, grad, master_ref, first_ref, second_ref, gain_ref, probe,
        out_ref, new_master_ref, new_first_ref, new_second_ref,
        fresh, ra, rb, xa, xa_out, xb, tb, share, near, far,
        *sems[N_GATHER + N_RELAY :],
    )
    for copy in put:
        copy.wait()


def hand_out_kernel(*refs):
    for i in range(4):
        refs[4 + i][...] = refs[i][...]


def shards(inputs, stashed, master, first_moment, second_moment, counts, plan, layer_index):
    state = jax.ShapeDtypeStruct((SHARD, 2 * HID), f32)
    vmem = pl.BlockSpec(memory_space=pltpu.VMEM)
    anywhere = pl.BlockSpec(memory_space=pl.ANY)
    chunks = (NZ, NX, SHARD, 2 * HID)
    probe_out, new_master, new_first, new_second = pl.pallas_call(
        step_kernel,
        out_shape=(jax.ShapeDtypeStruct((TOK, WIDTH), bf16), state, state, state),
        in_specs=[anywhere] * 8,
        out_specs=(vmem, anywhere, anywhere, anywhere),
        scratch_shapes=[
            pltpu.VMEM((2, NY, *chunks), bf16),
            pltpu.VMEM((2, NY, 8, 128), f32),
            pltpu.VMEM(chunks, bf16),
            pltpu.VMEM((TOK, WIDTH), bf16),
            pltpu.VMEM((8, 128), f32),
            pltpu.VMEM((2, ROWS, 128), f32),
            *[pltpu.VMEM((SHARD, 2 * HID), f32)] * 3,
            pltpu.VMEM((1, 1), jnp.int32),
            *[pltpu.VMEM((1, ROWS // TOK), jnp.int32)] * 2,
            *[pltpu.VMEM((SHARD, 2 * HID), f32)] * 3,
            pltpu.VMEM((OWN, WIDTH), bf16),
            pltpu.VMEM((OWN, WIDTH), bf16),
            pltpu.VMEM((SECTIONS, OWN, WIDTH), bf16),
            pltpu.VMEM((SECTIONS, OWN, 128), f32),
            pltpu.VMEM((SECTIONS, OWN, HID), f32),
            pltpu.VMEM((SECTIONS, OWN, HID), bf16),
            pltpu.VMEM((SECTIONS, 8, HID), f32),
            pltpu.VMEM((2, OWN, WIDTH), bf16),
            pltpu.VMEM((2, OWN, HID), bf16),
            pltpu.VMEM((OWN, WIDTH), bf16),
            pltpu.VMEM((OWN, HID), bf16),
            pltpu.VMEM((OWN, WIDTH), bf16),
            pltpu.VMEM((OWN, HID), bf16),
            pltpu.VMEM((TOK, WIDTH), bf16),
            pltpu.VMEM((TOK, WIDTH), bf16),
            pltpu.VMEM(chunks, bf16),
            pltpu.VMEM((2, 9, NX, ROWS_Z, 2 * HID), bf16),
            pltpu.VMEM((2, 9, ROWS_X, 2 * HID), bf16),
            pltpu.VMEM((NX, ROWS_Z, 2 * HID), bf16),
            pltpu.VMEM((NX, ROWS_Z, 2 * HID), bf16),
            pltpu.VMEM((NX, NZ, ROWS_X, 2 * HID), bf16),
            pltpu.VMEM((NZ, ROWS_X, 2 * HID), bf16),
            pltpu.VMEM((SHARD, 2 * HID), f32),
            pltpu.VMEM((GROUP, 8, 128), f32),
            pltpu.VMEM((NZ, 8, 128), f32),
            DMA((8,)),
            *[DMA((NY,))] * 4,
            *[DMA((3, 9))] * 2,
            *ROUND_SEMS,
            *ROUND_SEMS,
            *BLOCK_SEMS,
            *OVER_SEMS,
            *[DMA((3,))] * 2,
            *[DMA((PIECES + 1,))] * 2,
            *[DMA((2, 9, 3))] * 2,
            *[DMA((3, NX))] * 2,
            *[DMA((GROUP,))] * 2,
            *[DMA((NZ,))] * 2,
            *ROUND_SEMS,
            *BLOCK_SEMS,
        ],
        compiler_params=pltpu.CompilerParams(
            collective_id=0, has_side_effects=True, vmem_limit_bytes=60 * 2**20
        ),
        name="optimizer_step",
    )(
        stashed[0], layer_index.reshape(1, 1), counts, plan.reshape(1, 16),
        inputs.reshape(ROWS, WIDTH), master[0], first_moment[0], second_moment[0],
    )
    results = (probe_out[None], new_master[None], new_first[None], new_second[None])
    return pl.pallas_call(
        hand_out_kernel,
        out_shape=tuple(jax.ShapeDtypeStruct(r.shape, r.dtype) for r in results),
        in_specs=[vmem] * 4,
        out_specs=(vmem,) * 4,
        compiler_params=pltpu.CompilerParams(vmem_limit_bytes=60 * 2**20),
        name="hand_out",
    )(*results)


def solution(mesh):
    in_specs = (
        P(None, "dp", None),
        P("section", "dp", None),
        P("section", "dp", None),
        P("section", "dp", None),
        P("section", "dp", None),
        P("dp", None),
        P(),
        P("section"),
    )
    out_specs = (
        P("section", "dp", None),
        P("section", "dp", None),
        P("section", "dp", None),
        P("section", "dp", None),
    )
    return jax.shard_map(shards, mesh=mesh, in_specs=in_specs, out_specs=out_specs, check_vma=False)
```
